32 devices in a mesh: seq: 16 (over z, y, x), fsdp: 2 (over core).
Axes of the slice: x: 2, y: 2, z: 4, core: 2. Of those that a mesh axis runs over, the one named last changes fastest.
Arguments:
- tokens: bfloat16 [2, 2, 2048, 1152], P('fsdp', None, 'seq'), may hold values from -6 to 6
- cotangent: bfloat16 [2, 2, 2048, 1152], P('fsdp', None, 'seq'), may hold values from -6 to 6
- lengths: int32 [2, 2, 8], P('fsdp'), may hold values from 0 to 2048, as said below
- deal_order: int32 [2, 16], P('fsdp'), may hold values from 0 to 15, each once within a row
- w_query: bfloat16 [1152, 1024], P('fsdp'), may hold values from -0.1875 to 0.1875
- w_key: bfloat16 [1152, 256], P('fsdp'), may hold values from -0.1875 to 0.1875
- w_value: bfloat16 [1152, 256], P('fsdp'), may hold values from -0.1875 to 0.1875
- w_out: bfloat16 [1024, 1152], P(None, 'fsdp'), may hold values from -0.1875 to 0.1875
- w_gate: bfloat16 [1152, 6912], P(None, 'fsdp'), may hold values from -0.1875 to 0.1875
- w_up: bfloat16 [1152, 6912], P(None, 'fsdp'), may hold values from -0.1875 to 0.1875
- w_down: bfloat16 [6912, 1152], P('fsdp'), may hold values from -0.078125 to 0.078125
- norm_gains: float32 [4, 1152], replicated, may hold values from 0.1 to 1.9
- head_gains: float32 [2, 256], replicated, may hold values from 0.1 to 1.9
Outputs:
- output: float32 [2, 2, 2048, 1152], P('fsdp', None, 'seq')
- input_grad: float32 [2, 2, 2048, 1152], P('fsdp', None, 'seq')
- query_grad: float32 [1152, 1024], P('fsdp', 'seq')
- key_grad: float32 [1152, 256], P('fsdp', 'seq')
- value_grad: float32 [1152, 256], P('fsdp', 'seq')
- out_grad: float32 [1024, 1152], P('seq', 'fsdp')
- gate_grad: float32 [1152, 6912], P('seq', 'fsdp')
- up_grad: float32 [1152, 6912], P('seq', 'fsdp')
- down_grad: float32 [6912, 1152], P('fsdp', 'seq')
- norm_gains_grad: float32 [4, 1152], replicated
- head_gains_grad: float32 [2, 256], replicated
The draws below stay inside these ranges and needn't reach their ends.
Inputs may be any that keep to these rules, and one draw needn't show every extreme that they name: In every group one lane, drawn from the seed, holds a single sequence of 2048 tokens and zeros after it; in the other lanes all 8 lengths are positive. Each lane's lengths sum to 2048. `deal_order`: each row is a permutation of the block positions.
All inputs are finite; a program needn't handle non-finite values.
Results may differ from the reference program's by a relative error of at most 0.019.
Values may be sent and summed in bfloat16 or wider, within the bound.
No kernel may reach another device: no remote copies, remote signals or barrier semaphores. Data moves between devices by JAX's collectives and lax.ppermute only.
A program may use at most 256 MiB of HBM per device.

```python
import functools
import math
import jax
import jax.numpy as jnp
from jax import lax

D = 1152
HQ = 4
HD = 256
FF = 6912
W = 512
LANE = 128
SEQS = 8
LANES = 2
GROUPS = 2
BLOCKS = 16
SPAN = 2048


def draw_lengths(key, part):
    key = jax.random.fold_in(key, 17)
    weight_key, lane_key = jax.random.split(key)
    shares = jax.random.randint(weight_key, (GROUPS, LANES, SEQS), 1, 6, dtype=jnp.int32)
    bounds = SPAN * jnp.cumsum(shares, axis=-1) // jnp.sum(shares, axis=-1, keepdims=True)
    previous = jnp.concatenate([jnp.zeros((GROUPS, LANES, 1), bounds.dtype), bounds[..., :-1]], axis=-1)
    pieces = bounds - previous
    whole_lane = jnp.where(jnp.arange(SEQS) == 0, SPAN, 0)
    chosen = jax.random.randint(lane_key, (GROUPS, 1, 1), 0, LANES, dtype=jnp.int32)
    lane_index = jnp.arange(LANES).reshape(1, LANES, 1)
    return jnp.where(lane_index == chosen, whole_lane, pieces).astype(jnp.int32)


def block_scale(stream_key, extent, cuts, least, top_value):
    loudness = 1.0
    for dim, shards_of in cuts:
        heights = jax.random.uniform(jax.random.fold_in(jax.random.fold_in(stream_key, 6), dim), (shards_of,), jnp.float32, least / len(cuts), top_value / len(cuts))
        loudness = loudness * jnp.repeat(jnp.exp(heights), extent[dim] // shards_of).reshape((-1,) + (1,) * (len(extent) - 1 - dim))
    return loudness


def bell_draw(key, dims, width, reach, cuts=(), kind=jnp.bfloat16):
    drawn = width * jax.random.normal(key, dims, jnp.float32)
    if cuts:
        drawn = drawn * block_scale(key, dims, cuts, -0.22, 0.18)
    return jnp.clip(drawn, -reach, reach).astype(kind)


def setup_inputs(seed: int = 0) -> dict:
    key_of = jax.random.split(jax.random.key(seed), 14)
    tokens = bell_draw(key_of[0], (GROUPS, LANES, SPAN, D), 1.0, 6.0, ((0, 2), (2, 16)))
    cotangent = bell_draw(key_of[1], (GROUPS, LANES, SPAN, D), 1.0, 6.0, ((0, 2), (2, 16)))
    lengths = draw_lengths(jax.random.fold_in(key_of[13], 71), 0)
    deal_order = jax.vmap(lambda own: jax.random.permutation(own, BLOCKS))(jax.random.split(key_of[3], GROUPS)).reshape((GROUPS, BLOCKS)).astype(jnp.int32)
    w_query = bell_draw(key_of[4], (D, HQ * HD), D ** -0.5, 0.1875, ((0, 2),))
    w_key = bell_draw(key_of[5], (D, HD), D ** -0.5, 0.1875, ((0, 2),))
    w_value = bell_draw(key_of[6], (D, HD), D ** -0.5, 0.1875, ((0, 2),))
    w_out = bell_draw(key_of[7], (HQ * HD, D), (HQ * HD) ** -0.5, 0.1875, ((1, 2),))
    w_gate = bell_draw(key_of[8], (D, FF), D ** -0.5, 0.1875, ((1, 2),))
    w_up = bell_draw(key_of[9], (D, FF), D ** -0.5, 0.1875, ((1, 2),))
    w_down = bell_draw(key_of[10], (FF, D), FF ** -0.5, 0.078125, ((0, 2),))
    norm_gains = jnp.clip(1.0 + 0.18 * jax.random.normal(key_of[11], (4, D), jnp.float32), 0.1, 1.9)
    head_gains = jnp.clip(1.0 + 0.18 * jax.random.normal(key_of[12], (2, HD), jnp.float32), 0.1, 1.9)
    return dict(tokens=tokens, cotangent=cotangent, lengths=lengths, deal_order=deal_order, w_query=w_query, w_key=w_key, w_value=w_value, w_out=w_out, w_gate=w_gate, w_up=w_up, w_down=w_down, norm_gains=norm_gains, head_gains=head_gains)


EPSILON = 1e-06
ROPE_BASE = 10000.0

@jax.custom_vjp
def low(v):
    return lax.optimization_barrier(v.astype(jnp.bfloat16)).astype(jnp.float32)

@jax.custom_vjp
def low_back(v):
    return v

def low_keep(v):
    return (low(v), None)

def low_pass(kept, grad):
    return (grad,)

def back_keep(v):
    return (v, None)

def back_low(kept, grad):
    return (low(grad),)
low.defvjp(low_keep, low_pass)
low_back.defvjp(back_keep, back_low)

def matmul(left_side, right_side):
    return jnp.dot(left_side, right_side, precision=lax.Precision.HIGHEST, preferred_element_type=jnp.float32)

def rms_norm(values, gain_vec):
    return values * lax.rsqrt(lax.optimization_barrier(jnp.mean(values * values, axis=-1, keepdims=True)) + EPSILON) * gain_vec

def rope_tables(seq_pos, head_dim):
    half_dim = head_dim // 2
    frequency = jnp.exp(jnp.arange(half_dim, dtype=jnp.float32) * (-2.0 * math.log(ROPE_BASE) / head_dim))
    angles = seq_pos.astype(jnp.float32)[..., None] * frequency
    return (jnp.cos(angles), jnp.sin(angles))

def rotate(values, cosine_table, sine_table):
    half_dim = values.shape[-1] // 2
    first_half = values[..., :half_dim]
    second_half = values[..., half_dim:]
    return jnp.concatenate([first_half * cosine_table - second_half * sine_table, second_half * cosine_table + first_half * sine_table], axis=-1)

def gelu_tanh(values):
    return jax.nn.gelu(values, approximate=True)

def sequence_info(lengths, stream_pos):
    seq_ends = jnp.cumsum(lengths, axis=-1)
    before = seq_ends[..., None, :] <= stream_pos[..., :, None]
    seq_ids = lax.optimization_barrier(jnp.sum(before.astype(jnp.int32), axis=-1))
    starts = lax.optimization_barrier(jnp.sum(jnp.where(before, lengths[..., None, :], 0), axis=-1))
    return (seq_ids.astype(jnp.int32), (stream_pos - starts).astype(jnp.int32))

def attend_block(key_pad, value_pad, ids_pad, stream_pad, query_block, query_ids, query_stream, block_start):
    key_rows = lax.dynamic_slice_in_dim(key_pad, block_start, W - 1 + LANE, 0)
    value_rows = lax.dynamic_slice_in_dim(value_pad, block_start, W - 1 + LANE, 0)
    ids_rows = lax.dynamic_slice_in_dim(ids_pad, block_start, W - 1 + LANE, 0)
    stream_rows = lax.dynamic_slice_in_dim(stream_pad, block_start, W - 1 + LANE, 0)
    raw_scores = jnp.einsum('qhd,kd->qhk', query_block, key_rows, precision=lax.Precision.HIGHEST)
    scores = low_back(raw_scores) * HD ** (-0.5)
    allowed = (ids_rows[None, :] == query_ids[:, None]) & (stream_rows[None, :] <= query_stream[:, None]) & (query_stream[:, None] - stream_rows[None, :] < W) & (stream_rows[None, :] >= 0)
    scores = jnp.where(allowed[:, None, :], scores, -1e+30)
    probabilities_reduced = low(jax.nn.softmax(scores, axis=-1))
    return jnp.einsum('qhk,kd->qhd', probabilities_reduced, value_rows, precision=lax.Precision.HIGHEST)

def lane_layer(params, lane_tokens, seq_ids, seq_pos):
    w_query, w_key, w_value, w_out, w_gate, w_up, w_down, norm_gains, head_gains = params
    stream_pos = jnp.arange(SPAN, dtype=jnp.int32)
    attn_in = low(rms_norm(lane_tokens, norm_gains[0]))
    query_proj = low_back(matmul(attn_in, w_query)).reshape(SPAN, HQ, HD)
    key_proj = low_back(matmul(attn_in, w_key))
    value_proj = low(low_back(matmul(attn_in, w_value)))
    cosine_table, sine_table = rope_tables(seq_pos, HD)
    query_rot = low(rotate(rms_norm(query_proj, head_gains[0]), cosine_table[:, None, :], sine_table[:, None, :]))
    key_rot = low(rotate(rms_norm(key_proj, head_gains[1]), cosine_table, sine_table))
    key_pad = jnp.concatenate([jnp.zeros((W - 1, HD), jnp.float32), key_rot], axis=0)
    value_pad = jnp.concatenate([jnp.zeros((W - 1, HD), jnp.float32), value_proj], axis=0)
    ids_pad = jnp.concatenate([jnp.zeros((W - 1,), jnp.int32), seq_ids.astype(jnp.int32)])
    stream_pad = jnp.concatenate([jnp.full((W - 1,), -1, jnp.int32), stream_pos])
    block_fn = jax.checkpoint(functools.partial(attend_block, key_pad, value_pad, ids_pad, stream_pad))

    def run_block(block_item):
        return block_fn(block_item[0], block_item[1], block_item[2], block_item[3])
    starts = (jnp.arange(BLOCKS, dtype=jnp.int32) * LANE).astype(jnp.int32)
    attention_output = lax.map(run_block, (query_rot.reshape(BLOCKS, LANE, HQ, HD), seq_ids.reshape(BLOCKS, LANE), stream_pos.reshape(BLOCKS, LANE), starts))
    mixed_low = low(low_back(attention_output.reshape(SPAN, HQ * HD)))
    branch = low_back(matmul(mixed_low, w_out))
    middle = lane_tokens + rms_norm(branch, norm_gains[1])
    ffn_in = low(rms_norm(middle, norm_gains[2]))
    gate_proj = low_back(matmul(ffn_in, w_gate))
    upward = low_back(matmul(ffn_in, w_up))
    hidden = low(gelu_tanh(gate_proj) * upward)
    ffn_out = low_back(matmul(hidden, w_down))
    return middle + rms_norm(ffn_out, norm_gains[3])

def reorder(blocks, block_index):
    return jnp.take(blocks, block_index, axis=1)

def reference(tokens, cotangent, lengths, deal_order, w_query, w_key, w_value, w_out, w_gate, w_up, w_down, norm_gains, head_gains):
    back_keys = jnp.argsort(deal_order, axis=-1).astype(jnp.int32)
    lane_total = GROUPS * LANES

    def deal_rows(values):
        blocks = values.astype(jnp.float32).reshape(GROUPS, LANES, BLOCKS, LANE, D)
        return jax.vmap(reorder)(blocks, back_keys).reshape(lane_total, SPAN, D)

    def home_rows(values):
        blocks = values.reshape(GROUPS, LANES, BLOCKS, LANE, D)
        return jax.vmap(reorder)(blocks, deal_order.astype(jnp.int32)).reshape(GROUPS, LANES, SPAN, D)
    stream_pos = jnp.broadcast_to(jnp.arange(SPAN, dtype=jnp.int32), (GROUPS, LANES, SPAN))
    seq_ids, seq_pos = sequence_info(lengths, stream_pos)
    seq_ids = seq_ids.reshape(lane_total, SPAN)
    seq_pos = seq_pos.reshape(lane_total, SPAN)
    params = (w_query.astype(jnp.float32), w_key.astype(jnp.float32), w_value.astype(jnp.float32), w_out.astype(jnp.float32), w_gate.astype(jnp.float32), w_up.astype(jnp.float32), w_down.astype(jnp.float32), norm_gains.astype(jnp.float32), head_gains.astype(jnp.float32))
    lane_fn = jax.checkpoint(lane_layer)

    def forward(dealt, weights_all):

        def run_lane(lane_item):
            return lane_fn(weights_all, lane_item[0], lane_item[1], lane_item[2])
        return lax.map(run_lane, (dealt, seq_ids, seq_pos))
    result, pullback = jax.vjp(forward, deal_rows(tokens), params)
    grad_dealt, grad_params = pullback(deal_rows(cotangent))
    return (home_rows(result), home_rows(grad_dealt), grad_params[0], grad_params[1], grad_params[2], grad_params[3], grad_params[4], grad_params[5], grad_params[6], grad_params[7], grad_params[8])
```

```python
import math

import jax
import jax.numpy as jnp
from jax import lax
from jax.sharding import PartitionSpec as P

HQ = 4
HD = 256
W = 512
EPSILON = 1e-06
ROPE_BASE = 10000.0
SPLIT_BIT = 4

BF = jnp.bfloat16
F32 = jnp.float32


def swap(value, axis, mask):
    count = lax.axis_size(axis)
    return lax.ppermute(value, axis, [(i, i ^ mask) for i in range(count)])


def masks(count):
    return [1 << k for k in range(count.bit_length() - 1)]


def gather_cores(block):
    for mask in masks(lax.axis_size("fsdp")):
        block = jnp.concatenate([block, swap(block, "fsdp", mask)], axis=0)
    return block


def sum_cores(block):
    for mask in reversed(masks(lax.axis_size("fsdp"))):
        half = block.shape[0] // 2
        got = swap(block[half:].astype(BF), "fsdp", mask)
        block = block[:half].astype(F32) + got.astype(F32)
    return block


def flip(parts, index):
    count = parts.shape[0]
    for mask in masks(count):
        turned = jnp.stack([parts[j ^ mask] for j in range(count)])
        parts = jnp.where((index & mask) != 0, turned, parts)
    return parts


def rms_scale(values):
    return lax.rsqrt(jnp.mean(values * values, axis=-1, keepdims=True) + EPSILON)


def rms_forward(values, gain_vec):
    return values * rms_scale(values) * gain_vec


def rms_backward(values, gain_vec, grad_out):
    scale_rows = rms_scale(values)
    weighted = grad_out * gain_vec
    inner_mean = jnp.mean(weighted * values, axis=-1, keepdims=True)
    grad_in = scale_rows * weighted - values * (scale_rows * scale_rows * scale_rows) * inner_mean
    return (grad_in, grad_out * values * scale_rows)


def rope_tables(seq_pos, head_dim):
    half_dim = head_dim // 2
    frequency = jnp.exp(
        jnp.arange(half_dim, dtype=F32) * (-2.0 * math.log(ROPE_BASE) / head_dim)
    )
    angles = seq_pos.astype(F32)[..., None] * frequency
    return (jnp.cos(angles), jnp.sin(angles))


def rotate(values, cosine_table, sine_table):
    half_dim = values.shape[-1] // 2
    first_half = values[..., :half_dim]
    second_half = values[..., half_dim:]
    return jnp.concatenate(
        [
            first_half * cosine_table - second_half * sine_table,
            second_half * cosine_table + first_half * sine_table,
        ],
        axis=-1,
    )


def gelu_tanh(values):
    return jax.nn.gelu(values, approximate=True)


def sequence_info(lengths, stream_pos):
    seq_ends = jnp.cumsum(lengths, axis=-1)
    before = seq_ends[..., None, :] <= stream_pos[..., :, None]
    seq_ids = jnp.sum(before.astype(jnp.int32), axis=-1)
    starts = jnp.sum(jnp.where(before, lengths[..., None, :], 0), axis=-1)
    return (seq_ids, stream_pos - starts)


def dot(a, b):
    return jnp.dot(a, b, preferred_element_type=F32)


def dot_tn(a, b):
    return lax.dot_general(a, b, (((0,), (0,)), ((), ())), preferred_element_type=F32)


def dot_nt(a, b):
    return lax.dot_general(a, b, (((1,), (1,)), ((), ())), preferred_element_type=F32)


def pick(table, source):
    return jnp.take(source, table, axis=0)


def pick_sum(hops, table, valid, source):
    terms = jnp.take(source, table, axis=0).astype(F32) * valid.astype(F32)[:, None, None]
    count = table.shape[0] // hops
    return jnp.sum(terms.reshape((count, hops) + source.shape[1:]), axis=1).astype(source.dtype)


def halve(block, order, own, keep_bits=()):
    count = block.shape[0]
    bits = masks(count)[::-1]
    shape = block.shape[1:]
    block = block.reshape((2,) * len(bits) + shape)
    left = list(bits)
    for mask in order:
        axis = left.index(mask)
        mine = ((own & mask) != 0).astype(jnp.int32)
        sent = lax.dynamic_index_in_dim(block, 1 - mine, axis, keepdims=False)
        kept = lax.dynamic_index_in_dim(block, mine, axis, keepdims=False)
        got = swap(sent.astype(BF), "seq", mask)
        block = kept.astype(F32) + got.astype(F32)
        left.remove(mask)
        if mask != order[-1] or left:
            block = block.astype(BF)
    return block.reshape((2 ** len(left),) + shape)


def shards(
    tokens,
    cotangent,
    lengths,
    deal_order,
    w_query,
    w_key,
    w_value,
    w_out,
    w_gate,
    w_up,
    w_down,
    norm_gains,
    head_gains,
):
    lanes, rows, width = tokens.shape[1:]
    total = lanes * rows
    seq_count = lax.axis_size("seq")
    cores = lax.axis_size("fsdp")
    own = lax.axis_index("seq")
    core = lax.axis_index("fsdp")
    window = W
    hops = (window - 1 + rows - 1) // rows
    chunk = total // seq_count

    deal = deal_order[0]
    places = jnp.arange(seq_count, dtype=jnp.int32)
    back = jnp.sum(jnp.where(deal[None, :] == places[:, None], places[None, :], 0), axis=1)
    place = deal[own]
    steps = jnp.arange(1, hops + 1, dtype=jnp.int32)
    wanted = deal[:, None] - steps[None, :]
    fetch_table = back[jnp.maximum(wanted, 0)].reshape(-1)
    readers = deal[:, None] + steps[None, :]
    reader_ok = (readers < seq_count).astype(jnp.int32).reshape(-1)
    reader_table = (
        back[jnp.minimum(readers, seq_count - 1)] * hops + (steps[None, :] - 1)
    ).reshape(-1)

    inputs = tokens[0].astype(F32).reshape(total, width)
    upstream = cotangent[0].astype(F32).reshape(total, width)

    w_in = jnp.concatenate([w_query, w_key, w_value], axis=1)
    peers_in = gather_cores(w_in).reshape((cores,) + w_in.shape)
    w_in_full = flip(peers_in, core).reshape(width, w_in.shape[1])
    peers_out = gather_cores(w_out).reshape((cores,) + w_out.shape)
    peers_out = flip(peers_out, core)
    w_out_full = jnp.concatenate([peers_out[j] for j in range(cores)], axis=1)
    q_width = HQ * HD

    gain_in, gain_mid, gain_ffn, gain_top = (norm_gains[i] for i in range(4))
    query_gain, key_gain = (head_gains[0], head_gains[1])

    local_stream = place * rows + jnp.arange(rows, dtype=jnp.int32)
    query_ids, query_pos = sequence_info(lengths[0], jnp.broadcast_to(local_stream, (lanes, rows)))
    cosine, sine = rope_tables(query_pos, HD)

    attn_in = rms_forward(inputs, gain_in).astype(BF)
    kv_proj = dot(attn_in, w_in_full[:, q_width:])
    key_proj = kv_proj[:, :HD].reshape(lanes, rows, HD)
    value_proj = kv_proj[:, HD:].reshape(lanes, rows, HD).astype(BF)
    key_rot = rotate(rms_forward(key_proj, key_gain), cosine, sine).astype(BF)
    kv_local = jnp.concatenate([key_rot, value_proj], axis=-1)

    spread = lax.all_to_all(
        kv_local.reshape(seq_count, chunk, 2 * HD), "seq", 0, 0, tiled=True
    )
    picked = pick(fetch_table, spread).reshape(seq_count, hops * chunk, 2 * HD)
    arrived = lax.all_to_all(picked, "seq", 0, 0, tiled=True)
    earlier = (
        arrived.reshape(seq_count, hops, chunk, 2 * HD)
        .transpose(1, 0, 2, 3)
        .reshape(hops, lanes, rows, 2 * HD)
    )

    query_proj = dot(attn_in, w_in_full[:, :q_width]).reshape(lanes, rows, HQ, HD)
    query_rot = rotate(
        rms_forward(query_proj, query_gain), cosine[:, :, None, :], sine[:, :, None, :]
    ).astype(BF)

    hidden_cols = w_gate.shape[1]
    share = hidden_cols // 2
    part = ((own & SPLIT_BIT) != 0).astype(jnp.int32)
    gate_share = lax.dynamic_slice_in_dim(w_gate, part * share, share, 1)
    up_share = lax.dynamic_slice_in_dim(w_up, part * share, share, 1)
    down_share = lax.dynamic_slice_in_dim(w_down, part * share, share, 0)

    kv_all = jnp.concatenate([earlier[d] for d in range(hops - 1, -1, -1)] + [kv_local], axis=1)
    key_total = kv_all.shape[1]
    key_stream = (place - hops) * rows + jnp.arange(key_total, dtype=jnp.int32)
    key_ids = sequence_info(lengths[0], jnp.broadcast_to(key_stream, (lanes, key_total)))[0]
    allowed = (
        (key_ids[:, None, :] == query_ids[:, :, None])
        & (key_stream[None, None, :] <= local_stream[None, :, None])
        & (local_stream[None, :, None] - key_stream[None, None, :] < window)
        & (key_stream[None, None, :] >= 0)
    )
    allowed = jnp.repeat(allowed, HQ, axis=1)
    flat_query = query_rot.reshape(lanes, rows * HQ, HD)
    all_keys = kv_all[..., :HD]
    all_values = kv_all[..., HD:]
    score_scale = HD ** (-0.5)

    raw_scores = jnp.einsum("nfi,nhi->nfh", flat_query, all_keys, preferred_element_type=F32)
    masked = jnp.where(allowed, raw_scores * score_scale, -1e30)
    top_score = jnp.max(masked, axis=-1, keepdims=True)
    exponents = jnp.exp(masked - top_score)
    soft = exponents / jnp.sum(exponents, axis=-1, keepdims=True)
    probs_low = soft.astype(BF)
    mixed_low = (
        jnp.einsum("ajm,amn->ajn", probs_low, all_values, preferred_element_type=F32)
        .reshape(total, q_width)
        .astype(BF)
    )
    branch = dot(mixed_low, w_out_full)
    middle = inputs + rms_forward(branch, gain_mid)
    ffn_in = rms_forward(middle, gain_ffn).astype(BF)

    far_in = swap(ffn_in, "seq", SPLIT_BIT)
    near_all = gather_cores(ffn_in)
    far_all = gather_cores(far_in)

    def ffn_forward(rows_in):
        gate = dot(rows_in, gate_share)
        upward = dot(rows_in, up_share)
        hid = (gelu_tanh(gate) * upward).astype(BF)
        return gate, upward, hid, dot(hid, down_share)

    near = ffn_forward(near_all)
    far = ffn_forward(far_all)

    def sum_group(near_part, far_part):
        far_sum = sum_cores(far_part)
        got = swap(far_sum.astype(BF), "seq", SPLIT_BIT)
        return sum_cores(near_part) + got.astype(F32)

    ffn_out = sum_group(near[3], far[3])
    result = middle + rms_forward(ffn_out, gain_top)

    grad_ffn_out, top_terms = rms_backward(ffn_out, gain_top, upstream)
    grad_low = grad_ffn_out.astype(BF)
    far_grad = swap(grad_low, "seq", SPLIT_BIT)
    near_grads = gather_cores(grad_low)
    far_grads = gather_cores(far_grad)

    def ffn_backward(saved, grads):
        gate, upward, hid, _ = saved
        d_hidden = dot_nt(grads, down_share)
        activated, pull = jax.vjp(gelu_tanh, gate)
        d_gate = pull(d_hidden * upward)[0].astype(BF)
        d_up = (d_hidden * activated).astype(BF)
        return d_gate, d_up, dot_nt(d_gate, gate_share) + dot_nt(d_up, up_share)

    near_back = ffn_backward(near, near_grads)
    far_back = ffn_backward(far, far_grads)

    grad_ffn_in = sum_group(near_back[2], far_back[2])

    def weight_terms(left_near, left_far, right_near, right_far):
        left = jnp.concatenate([left_near, left_far], axis=0)
        right = jnp.concatenate([right_near, right_far], axis=0)
        out = dot_tn(left, right).astype(BF)
        return out.reshape(seq_count, width // seq_count, share)

    others = [m for m in masks(seq_count) if m != SPLIT_BIT]

    def owned(terms, order):
        block = halve(terms, order, own)
        mine = lax.dynamic_index_in_dim(block, part, 0, keepdims=False)
        sent = lax.dynamic_index_in_dim(block, 1 - part, 0, keepdims=False)
        got = swap(sent.astype(BF), "seq", SPLIT_BIT).astype(F32)
        mine = mine.astype(F32)
        return jnp.where(
            part == 0,
            jnp.concatenate([mine, got], axis=1),
            jnp.concatenate([got, mine], axis=1),
        )

    swapped = [others[1], others[0]] + others[2:]
    down_terms = weight_terms(near_grads, far_grads, near[2], far[2])
    down_grad = owned(down_terms, others).T
    gate_terms = weight_terms(near_all, far_all, near_back[0], far_back[0])
    gate_grad = owned(gate_terms, swapped)
    up_terms = weight_terms(near_all, far_all, near_back[1], far_back[1])
    up_grad = owned(up_terms, others)

    grad_middle_norm, ffn_terms = rms_backward(middle, gain_ffn, grad_ffn_in)
    grad_middle = upstream + grad_middle_norm
    grad_branch, mid_terms = rms_backward(branch, gain_mid, grad_middle)
    grad_branch_low = grad_branch.astype(BF)
    grad_mixed = dot_nt(grad_branch_low, w_out_full).astype(BF).reshape(lanes, rows * HQ, HD)

    grad_probs = jnp.einsum("nfi,nhi->nfh", grad_mixed, all_values, preferred_element_type=F32)
    inner_sum = jnp.sum(soft * grad_probs, axis=-1, keepdims=True)
    grad_raw = (soft * (grad_probs - inner_sum) * score_scale).astype(BF)
    grad_query = jnp.einsum("ajm,amn->ajn", grad_raw, all_keys, preferred_element_type=F32)
    grad_keys = jnp.einsum("xzo,xza->xoa", grad_raw, flat_query, preferred_element_type=F32)
    grad_values = jnp.einsum("xzo,xza->xoa", probs_low, grad_mixed, preferred_element_type=F32)
    grad_kv = jnp.concatenate([grad_keys, grad_values], axis=-1)

    outward = (
        jnp.stack(
            [
                grad_kv[:, (hops - d) * rows : (hops - d + 1) * rows].reshape(total, 2 * HD)
                for d in range(1, hops + 1)
            ]
        )
        .astype(BF)
        .reshape(hops, seq_count, chunk, 2 * HD)
        .transpose(1, 0, 2, 3)
        .reshape(seq_count, hops * chunk, 2 * HD)
    )
    collected = lax.all_to_all(outward, "seq", 0, 0, tiled=True)
    summed = pick_sum(
        hops, reader_table, reader_ok, collected.reshape(seq_count * hops, chunk, 2 * HD)
    )
    returned = lax.all_to_all(summed, "seq", 0, 0, tiled=True)
    grad_local = grad_kv[:, hops * rows :] + returned.reshape(lanes, rows, 2 * HD).astype(F32)

    grad_value_low = grad_local[..., HD:].reshape(total, HD).astype(BF)
    key_normed_grad = rotate(grad_local[..., :HD], cosine, -sine)
    grad_key_proj, key_terms = rms_backward(key_proj, key_gain, key_normed_grad)
    grad_key_low = grad_key_proj.reshape(total, HD).astype(BF)
    query_normed_grad = rotate(
        grad_query.reshape(lanes, rows, HQ, HD), cosine[:, :, None, :], -sine[:, :, None, :]
    )
    grad_query_proj, query_terms = rms_backward(query_proj, query_gain, query_normed_grad)
    grad_query_low = grad_query_proj.reshape(total, q_width).astype(BF)

    grad_kv_low = jnp.concatenate([grad_key_low, grad_value_low], axis=1)
    grad_attn_in = dot_nt(grad_query_low, w_in_full[:, :q_width]) + dot_nt(
        grad_kv_low, w_in_full[:, q_width:]
    )
    grad_input_norm, in_terms = rms_backward(inputs, gain_in, grad_attn_in)
    grad_inputs = grad_middle + grad_input_norm

    def by_peer(values):
        columns = values.reshape(total, cores, width // cores).transpose(1, 0, 2)
        return flip(columns, core)

    def peer_terms(left, right):
        return jnp.concatenate([dot_tn(left, right[j]) for j in range(cores)], axis=0)

    in_peers = by_peer(attn_in)
    branch_peers = by_peer(grad_branch_low)
    narrow = width // cores
    out_terms = sum_cores(peer_terms(mixed_low, branch_peers).astype(BF)).astype(BF)
    query_terms_w = sum_cores(peer_terms(grad_query_low, in_peers).astype(BF)).astype(BF)
    every = masks(seq_count)
    out_grad = halve(
        out_terms.reshape(seq_count, q_width // seq_count, narrow), every, own
    ).reshape(q_width // seq_count, narrow)
    query_grad = (
        halve(query_terms_w.reshape(seq_count, q_width // seq_count, narrow), swapped + [SPLIT_BIT], own)
        .reshape(q_width // seq_count, narrow)
        .T
    )

    kv_terms = sum_cores(peer_terms(grad_kv_low, in_peers).astype(BF)).astype(BF)
    kv_rows = HD // seq_count
    kv_terms = (
        kv_terms.reshape(2, seq_count, kv_rows, narrow)
        .transpose(1, 0, 2, 3)
        .reshape(seq_count, 2 * kv_rows, narrow)
    )
    gains = jnp.concatenate(
        [
            jnp.sum(in_terms, axis=0),
            jnp.sum(mid_terms, axis=0),
            jnp.sum(ffn_terms, axis=0),
            jnp.sum(top_terms, axis=0),
            jnp.sum(query_terms, axis=(0, 1, 2)),
            jnp.sum(key_terms, axis=(0, 1)),
        ]
    )
    for mask in masks(cores):
        gains = gains + swap(gains, "fsdp", mask)
    gain_size = gains.shape[0]
    gain_rows = -(-gain_size // narrow)
    gains = jnp.pad(gains, (0, gain_rows * narrow - gain_size)).reshape(gain_rows, narrow)
    high = lax.reduce_precision(gains, 8, 7)
    low = gains - high
    tail = jnp.concatenate(
        [
            kv_terms,
            jnp.broadcast_to(high.astype(BF), (seq_count, gain_rows, narrow)),
            jnp.broadcast_to(low.astype(BF), (seq_count, gain_rows, narrow)),
        ],
        axis=1,
    )
    tail = jnp.sum(lax.all_to_all(tail, "seq", 0, 0, tiled=True).astype(F32), axis=0)
    key_grad = tail[:kv_rows].T
    value_grad = tail[kv_rows : 2 * kv_rows].T
    gains = tail[2 * kv_rows : 2 * kv_rows + gain_rows] + tail[2 * kv_rows + gain_rows :]
    gains = gains.reshape(-1)[:gain_size]
    norm_total = gains[: 4 * width].reshape(4, width)
    head_total = gains[4 * width :].reshape(2, HD)

    return (
        result.reshape(1, lanes, rows, width),
        grad_inputs.reshape(1, lanes, rows, width),
        query_grad,
        key_grad,
        value_grad,
        out_grad,
        gate_grad,
        up_grad,
        down_grad,
        norm_total,
        head_total,
    )


def solution(mesh):
    in_specs = (
        P("fsdp", None, "seq", None),
        P("fsdp", None, "seq", None),
        P("fsdp", None, None),
        P("fsdp", None),
        P("fsdp", None),
        P("fsdp", None),
        P("fsdp", None),
        P(None, "fsdp"),
        P(None, "fsdp"),
        P(None, "fsdp"),
        P("fsdp", None),
        P(),
        P(),
    )
    out_specs = (
        P("fsdp", None, "seq", None),
        P("fsdp", None, "seq", None),
        P("fsdp", "seq"),
        P("fsdp", "seq"),
        P("fsdp", "seq"),
        P("seq", "fsdp"),
        P("seq", "fsdp"),
        P("seq", "fsdp"),
        P("fsdp", "seq"),
        P(),
        P(),
    )
    return jax.shard_map(shards, mesh=mesh, in_specs=in_specs, out_specs=out_specs, check_vma=False)
```

```python
import functools
import math

import jax
import jax.numpy as jnp
from jax import lax
from jax.experimental import pallas as pl
from jax.experimental.pallas import tpu as pltpu
from jax.sharding import PartitionSpec as P

HQ = 4
HD = 256
W = 512
EPSILON = 1e-06
ROPE_BASE = 10000.0
SPLIT_BIT = 4

BF = jnp.bfloat16
F32 = jnp.float32


def swap(value, axis, mask):
    count = lax.axis_size(axis)
    return lax.ppermute(value, axis, [(i, i ^ mask) for i in range(count)])


def masks(count):
    return [1 << k for k in range(count.bit_length() - 1)]


def gather_cores(block):
    for mask in masks(lax.axis_size("fsdp")):
        block = jnp.concatenate([block, swap(block, "fsdp", mask)], axis=0)
    return block


def sum_cores(block):
    for mask in reversed(masks(lax.axis_size("fsdp"))):
        half = block.shape[0] // 2
        got = swap(block[half:].astype(BF), "fsdp", mask)
        block = block[:half].astype(F32) + got.astype(F32)
    return block


def flip(parts, index):
    count = parts.shape[0]
    for mask in masks(count):
        turned = jnp.stack([parts[j ^ mask] for j in range(count)])
        parts = jnp.where((index & mask) != 0, turned, parts)
    return parts


def rms_scale(values):
    return lax.rsqrt(jnp.mean(values * values, axis=-1, keepdims=True) + EPSILON)


def rms_forward(values, gain_vec):
    return values * rms_scale(values) * gain_vec


def rms_backward(values, gain_vec, grad_out):
    scale_rows = rms_scale(values)
    weighted = grad_out * gain_vec
    inner_mean = jnp.mean(weighted * values, axis=-1, keepdims=True)
    grad_in = scale_rows * weighted - values * (scale_rows * scale_rows * scale_rows) * inner_mean
    return (grad_in, grad_out * values * scale_rows)


def rope_tables(seq_pos, head_dim):
    half_dim = head_dim // 2
    frequency = jnp.exp(
        jnp.arange(half_dim, dtype=F32) * (-2.0 * math.log(ROPE_BASE) / head_dim)
    )
    angles = seq_pos.astype(F32)[..., None] * frequency
    return (jnp.cos(angles), jnp.sin(angles))


def rotate(values, cosine_table, sine_table):
    half_dim = values.shape[-1] // 2
    first_half = values[..., :half_dim]
    second_half = values[..., half_dim:]
    return jnp.concatenate(
        [
            first_half * cosine_table - second_half * sine_table,
            second_half * cosine_table + first_half * sine_table,
        ],
        axis=-1,
    )


def gelu_tanh(values):
    return jax.nn.gelu(values, approximate=True)


def sequence_info(lengths, stream_pos):
    seq_ends = jnp.cumsum(lengths, axis=-1)
    before = seq_ends[..., None, :] <= stream_pos[..., :, None]
    seq_ids = jnp.sum(before.astype(jnp.int32), axis=-1)
    starts = jnp.sum(jnp.where(before, lengths[..., None, :], 0), axis=-1)
    return (seq_ids, stream_pos - starts)


def dot(a, b):
    return jnp.dot(a, b, preferred_element_type=F32)


def dot_tn(a, b):
    return lax.dot_general(a, b, (((0,), (0,)), ((), ())), preferred_element_type=F32)


def dot_nt(a, b):
    return lax.dot_general(a, b, (((1,), (1,)), ((), ())), preferred_element_type=F32)


def pick(table, source):
    return jnp.take(source, table, axis=0)


def pick_sum(hops, table, valid, source):
    terms = jnp.take(source, table, axis=0).astype(F32) * valid.astype(F32)[:, None, None]
    count = table.shape[0] // hops
    return jnp.sum(terms.reshape((count, hops) + source.shape[1:]), axis=1).astype(source.dtype)


def arrangement(order):
    if not order:
        return [0]
    rest = arrangement(order[1:])
    return [j | order[0] for j in rest] + rest


def halve(first, rest, order):
    for mask in order:
        got = swap(first, "seq", mask)
        total = rest.astype(F32) + got.astype(F32)
        half = total.shape[0] // 2
        first, rest = total[:half].astype(BF), total[half:].astype(BF)
    return total


def tiles(size):
    tile = 256 if size % 256 == 0 else 128
    return tile, size // tile


def column_tiles(size):
    return [(start, min(256, size - start)) for start in range(0, size, 256)]


VMEM = pl.BlockSpec(memory_space=pltpu.VMEM)
SMEM = pl.BlockSpec(memory_space=pltpu.SMEM)
PARAMS = pltpu.CompilerParams(vmem_limit_bytes=56 * 1024 * 1024)
ROOT = math.sqrt(2.0 / math.pi)
CUBE = 0.044715


def ffn_forward_kernel(n, *refs):
    x_refs, (wg, wu, wd) = refs[:n], refs[n : n + 3]
    hid, act, slope, keep, send, x_all = refs[n + 3 :]
    rows = x_refs[0].shape[0]
    for j in range(n):
        x_all[j * rows : (j + 1) * rows, :] = x_refs[j][...]
    tile, count = tiles(wg.shape[1])

    @pl.loop(0, count)
    def _(i):
        cols = pl.ds(pl.multiple_of(i * tile, tile), tile)
        g = dot(x_all[...], wg[:, cols])
        u = dot(x_all[...], wu[:, cols])
        square = g * g
        t = jnp.tanh(g * (ROOT + ROOT * CUBE * square))
        half = 0.5 * (1.0 + t)
        a = g * half
        d = half + a * (1.0 - t) * (ROOT + 3.0 * ROOT * CUBE * square)
        hid[:, cols] = (a * u).astype(BF)
        act[:, cols] = a.astype(BF)
        slope[:, cols] = (u * d).astype(BF)

    for start, size in column_tiles(wd.shape[1]):
        out = dot(hid[...], wd[:, start : start + size])
        half = out.shape[0] // 2
        keep[:, start : start + size] = out[:half]
        send[:, start : start + size] = out[half:].astype(BF)


def ffn_forward(blocks, wg, wu, wd):
    n, (rows, width), share = len(blocks), blocks[0].shape, wg.shape[1]
    total = n * rows
    return pl.pallas_call(
        functools.partial(ffn_forward_kernel, n),
        out_shape=[jax.ShapeDtypeStruct((total, share), BF)] * 3
        + [
            jax.ShapeDtypeStruct((total // 2, width), F32),
            jax.ShapeDtypeStruct((total // 2, width), BF),
        ],
        in_specs=[VMEM] * (n + 3),
        out_specs=[VMEM] * 5,
        scratch_shapes=[pltpu.VMEM((total, width), BF)],
        compiler_params=PARAMS,
        cost_estimate=pl.CostEstimate(
            flops=6 * total * width * share,
            bytes_accessed=6 * width * share + 6 * total * share,
            transcendentals=total * share,
        ),
    )(*blocks, wg, wu, wd)


def ffn_backward_kernel(n, *refs):
    g_refs, (act, slope, wg, wu, wd) = refs[:n], refs[n : n + 5]
    d_gate, d_up, keep, send, g_all = refs[n + 5 :]
    rows = g_refs[0].shape[0]
    for j in range(n):
        g_all[j * rows : (j + 1) * rows, :] = g_refs[j][...]
    tile, count = tiles(wg.shape[1])

    @pl.loop(0, count)
    def _(i):
        cols = pl.ds(pl.multiple_of(i * tile, tile), tile)
        d = dot_nt(g_all[...], wd[cols, :])
        d_gate[:, cols] = (d * slope[:, cols].astype(F32)).astype(BF)
        d_up[:, cols] = (d * act[:, cols].astype(F32)).astype(BF)

    for start, size in column_tiles(wg.shape[0]):
        out = dot_nt(d_gate[...], wg[start : start + size, :])
        out = out + dot_nt(d_up[...], wu[start : start + size, :])
        half = out.shape[0] // 2
        keep[:, start : start + size] = out[:half]
        send[:, start : start + size] = out[half:].astype(BF)


def ffn_backward(blocks, act, slope, wg, wu, wd):
    n, (rows, width), share = len(blocks), blocks[0].shape, wg.shape[1]
    total = n * rows
    return pl.pallas_call(
        functools.partial(ffn_backward_kernel, n),
        out_shape=[jax.ShapeDtypeStruct((total, share), BF)] * 2
        + [
            jax.ShapeDtypeStruct((total // 2, width), F32),
            jax.ShapeDtypeStruct((total // 2, width), BF),
        ],
        in_specs=[VMEM] * (n + 5),
        out_specs=[VMEM] * 4,
        scratch_shapes=[pltpu.VMEM((total, width), BF)],
        compiler_params=PARAMS,
        cost_estimate=pl.CostEstimate(
            flops=6 * total * width * share,
            bytes_accessed=6 * width * share + 8 * total * share,
            transcendentals=0,
        ),
    )(*blocks, act, slope, wg, wu, wd)


def weight_kernel(n, order, *refs):
    own, left = refs[0], refs[1 : n + 1]
    near, far = refs[n + 1 : n + 3]
    first, rest, turned, out = refs[n + 3 :]
    rows = left[0].shape[0]
    for j in range(n):
        turned[:, j * rows : (j + 1) * rows] = left[j][...].T
    tile, count = tiles(near.shape[1])
    half = near.shape[0]
    block = first.shape[1]
    me = own[0]

    @pl.loop(0, count)
    def _(i):
        cols = pl.ds(pl.multiple_of(i * tile, tile), tile)
        out[...] = dot(turned[:, :half], near[:, cols]) + dot(turned[:, half:], far[:, cols])
        for k, j in enumerate(arrangement(order)):
            source = pl.multiple_of((me ^ j) * block, 8)
            target = first if k < first.shape[0] else rest
            target[k % first.shape[0], :, cols] = out[pl.ds(source, block), :].astype(BF)


def weight_terms(own, seq_count, order, left, near, far):
    width, share = left[0].shape[1], near.shape[1]
    block = width // seq_count
    n = len(left)
    if block % 8:
        full = dot_tn(jnp.concatenate(left), jnp.concatenate([near, far])).astype(BF)
        full = full.reshape(seq_count, block, share)
        full = jnp.take(full, own ^ jnp.array(arrangement(order), jnp.int32), axis=0)
        return full[: seq_count // 2], full[seq_count // 2 :]
    tile, _ = tiles(share)
    return pl.pallas_call(
        functools.partial(weight_kernel, n, order),
        out_shape=[jax.ShapeDtypeStruct((seq_count // 2, block, share), BF)] * 2,
        in_specs=[SMEM] + [VMEM] * (n + 2),
        out_specs=[VMEM] * 2,
        scratch_shapes=[
            pltpu.VMEM((width, n * left[0].shape[0]), BF),
            pltpu.VMEM((width, tile), F32),
        ],
        compiler_params=PARAMS,
        cost_estimate=pl.CostEstimate(
            flops=2 * n * left[0].shape[0] * width * share,
            bytes_accessed=2 * width * share + 2 * n * left[0].shape[0] * (width + share),
            transcendentals=0,
        ),
    )(own.reshape(1), *left, near, far)


def shards(
    tokens,
    cotangent,
    lengths,
    deal_order,
    w_query,
    w_key,
    w_value,
    w_out,
    w_gate,
    w_up,
    w_down,
    norm_gains,
    head_gains,
):
    lanes, rows, width = tokens.shape[1:]
    total = lanes * rows
    seq_count = lax.axis_size("seq")
    cores = lax.axis_size("fsdp")
    own = lax.axis_index("seq")
    core = lax.axis_index("fsdp")
    window = W
    hops = (window - 1 + rows - 1) // rows
    chunk = total // seq_count

    deal = deal_order[0]
    places = jnp.arange(seq_count, dtype=jnp.int32)
    back = jnp.sum(jnp.where(deal[None, :] == places[:, None], places[None, :], 0), axis=1)
    place = deal[own]
    steps = jnp.arange(1, hops + 1, dtype=jnp.int32)
    wanted = deal[:, None] - steps[None, :]
    fetch_table = back[jnp.maximum(wanted, 0)].reshape(-1)
    readers = deal[:, None] + steps[None, :]
    reader_ok = (readers < seq_count).astype(jnp.int32).reshape(-1)
    reader_table = (
        back[jnp.minimum(readers, seq_count - 1)] * hops + (steps[None, :] - 1)
    ).reshape(-1)

    inputs = tokens[0].astype(F32).reshape(total, width)
    upstream = cotangent[0].astype(F32).reshape(total, width)

    w_in = jnp.concatenate([w_query, w_key, w_value], axis=1)
    peers_in = gather_cores(w_in).reshape((cores,) + w_in.shape)
    w_in_full = flip(peers_in, core).reshape(width, w_in.shape[1])
    peers_out = gather_cores(w_out).reshape((cores,) + w_out.shape)
    peers_out = flip(peers_out, core)
    w_out_full = jnp.concatenate([peers_out[j] for j in range(cores)], axis=1)
    q_width = HQ * HD

    gain_in, gain_mid, gain_ffn, gain_top = (norm_gains[i] for i in range(4))
    query_gain, key_gain = (head_gains[0], head_gains[1])

    local_stream = place * rows + jnp.arange(rows, dtype=jnp.int32)
    query_ids, query_pos = sequence_info(lengths[0], jnp.broadcast_to(local_stream, (lanes, rows)))
    cosine, sine = rope_tables(query_pos, HD)

    attn_in = rms_forward(inputs, gain_in).astype(BF)
    kv_proj = dot(attn_in, w_in_full[:, q_width:])
    key_proj = kv_proj[:, :HD].reshape(lanes, rows, HD)
    value_proj = kv_proj[:, HD:].reshape(lanes, rows, HD).astype(BF)
    key_rot = rotate(rms_forward(key_proj, key_gain), cosine, sine).astype(BF)
    kv_local = jnp.concatenate([key_rot, value_proj], axis=-1)

    spread = lax.all_to_all(
        kv_local.reshape(seq_count, chunk, 2 * HD), "seq", 0, 0, tiled=True
    )
    picked = pick(fetch_table, spread).reshape(seq_count, hops * chunk, 2 * HD)
    arrived = lax.all_to_all(picked, "seq", 0, 0, tiled=True)
    earlier = (
        arrived.reshape(seq_count, hops, chunk, 2 * HD)
        .transpose(1, 0, 2, 3)
        .reshape(hops, lanes, rows, 2 * HD)
    )

    query_proj = dot(attn_in, w_in_full[:, :q_width]).reshape(lanes, rows, HQ, HD)
    query_rot = rotate(
        rms_forward(query_proj, query_gain), cosine[:, :, None, :], sine[:, :, None, :]
    ).astype(BF)

    hidden_cols = w_gate.shape[1]
    share = -(-hidden_cols // 256) * 128
    overlap = 2 * share - hidden_cols
    part = ((own & SPLIT_BIT) != 0).astype(jnp.int32)
    begin = part * (hidden_cols - share)
    gate_share = lax.dynamic_slice_in_dim(w_gate, begin, share, 1)
    up_share = lax.dynamic_slice_in_dim(w_up, begin, share, 1)
    down_share = lax.dynamic_slice_in_dim(w_down, begin, share, 0)
    counted = (part == 0) | (jnp.arange(share) >= overlap)
    down_share = jnp.where(counted[:, None], down_share, 0)

    kv_all = jnp.concatenate([earlier[d] for d in range(hops - 1, -1, -1)] + [kv_local], axis=1)
    key_total = kv_all.shape[1]
    key_stream = (place - hops) * rows + jnp.arange(key_total, dtype=jnp.int32)
    key_ids = sequence_info(lengths[0], jnp.broadcast_to(key_stream, (lanes, key_total)))[0]
    allowed = (
        (key_ids[:, None, :] == query_ids[:, :, None])
        & (key_stream[None, None, :] <= local_stream[None, :, None])
        & (local_stream[None, :, None] - key_stream[None, None, :] < window)
        & (key_stream[None, None, :] >= 0)
    )
    allowed = jnp.repeat(allowed, HQ, axis=1)
    flat_query = query_rot.reshape(lanes, rows * HQ, HD)
    all_keys = kv_all[..., :HD]
    all_values = kv_all[..., HD:]
    score_scale = HD ** (-0.5)

    raw_scores = jnp.einsum("nfi,nhi->nfh", flat_query, all_keys, preferred_element_type=F32)
    masked = jnp.where(allowed, raw_scores * score_scale, -1e30)
    top_score = jnp.max(masked, axis=-1, keepdims=True)
    exponents = jnp.exp(masked - top_score)
    soft = exponents / jnp.sum(exponents, axis=-1, keepdims=True)
    probs_low = soft.astype(BF)
    mixed_low = (
        jnp.einsum("ajm,amn->ajn", probs_low, all_values, preferred_element_type=F32)
        .reshape(total, q_width)
        .astype(BF)
    )
    branch = dot(mixed_low, w_out_full)
    middle = inputs + rms_forward(branch, gain_mid)
    ffn_in = rms_forward(middle, gain_ffn).astype(BF)

    def core_blocks(block):
        blocks = [block]
        for mask in masks(cores):
            together = jnp.concatenate(blocks, axis=0) if len(blocks) > 1 else blocks[0]
            got = swap(together, "fsdp", mask)
            blocks = blocks + [got[j * total : (j + 1) * total] for j in range(len(blocks))]
        return blocks

    def core_sum(keep, send):
        steps = masks(cores)[::-1]
        for mask in steps:
            out = keep + swap(send, "fsdp", mask).astype(F32)
            half = out.shape[0] // 2
            keep, send = out[:half], out[half:].astype(BF)
        return out

    def sum_group(near_part, far_part):
        got = swap(core_sum(*far_part).astype(BF), "seq", SPLIT_BIT)
        return core_sum(*near_part) + got.astype(F32)

    far_in = swap(ffn_in, "seq", SPLIT_BIT)
    near_all = core_blocks(ffn_in)
    far_all = core_blocks(far_in)
    near = ffn_forward(near_all, gate_share, up_share, down_share)
    far = ffn_forward(far_all, gate_share, up_share, down_share)
    ffn_out = sum_group(near[3:], far[3:])
    result = middle + rms_forward(ffn_out, gain_top)

    grad_ffn_out, top_terms = rms_backward(ffn_out, gain_top, upstream)
    grad_low = grad_ffn_out.astype(BF)
    far_grad = swap(grad_low, "seq", SPLIT_BIT)
    near_grads = core_blocks(grad_low)
    far_grads = core_blocks(far_grad)
    near_back = ffn_backward(near_grads, near[1], near[2], gate_share, up_share, down_share)
    far_back = ffn_backward(far_grads, far[1], far[2], gate_share, up_share, down_share)
    grad_ffn_in = sum_group(near_back[2:], far_back[2:])

    others = [m for m in masks(seq_count) if m != SPLIT_BIT]
    swapped = [others[1], others[0]] + others[2:]

    def owned(left, near_right, far_right, order):
        first, rest = weight_terms(
            own, seq_count, order + [SPLIT_BIT], left, near_right, far_right
        )
        block = halve(first, rest, order)
        mine = block[1]
        got = swap(block[0].astype(BF), "seq", SPLIT_BIT).astype(F32)
        lower = jnp.where(part == 0, mine, got)
        upper = jnp.where(part == 0, got, mine)
        return jnp.concatenate([lower, upper[:, overlap:]], axis=1)

    down_grad = owned(near_grads + far_grads, near[0], far[0], others).T
    gate_grad = owned(near_all + far_all, near_back[0], far_back[0], swapped)
    up_grad = owned(near_all + far_all, near_back[1], far_back[1], others)

    grad_middle_norm, ffn_terms = rms_backward(middle, gain_ffn, grad_ffn_in)
    grad_middle = upstream + grad_middle_norm
    grad_branch, mid_terms = rms_backward(branch, gain_mid, grad_middle)
    grad_branch_low = grad_branch.astype(BF)
    grad_mixed = dot_nt(grad_branch_low, w_out_full).astype(BF).reshape(lanes, rows * HQ, HD)

    grad_probs = jnp.einsum("nfi,nhi->nfh", grad_mixed, all_values, preferred_element_type=F32)
    inner_sum = jnp.sum(soft * grad_probs, axis=-1, keepdims=True)
    grad_raw = (soft * (grad_probs - inner_sum) * score_scale).astype(BF)
    grad_query = jnp.einsum("ajm,amn->ajn", grad_raw, all_keys, preferred_element_type=F32)
    grad_keys = jnp.einsum("xzo,xza->xoa", grad_raw, flat_query, preferred_element_type=F32)
    grad_values = jnp.einsum("xzo,xza->xoa", probs_low, grad_mixed, preferred_element_type=F32)
    grad_kv = jnp.concatenate([grad_keys, grad_values], axis=-1)

    outward = (
        jnp.stack(
            [
                grad_kv[:, (hops - d) * rows : (hops - d + 1) * rows].reshape(total, 2 * HD)
                for d in range(1, hops + 1)
            ]
        )
        .astype(BF)
        .reshape(hops, seq_count, chunk, 2 * HD)
        .transpose(1, 0, 2, 3)
        .reshape(seq_count, hops * chunk, 2 * HD)
    )
    collected = lax.all_to_all(outward, "seq", 0, 0, tiled=True)
    summed = pick_sum(
        hops, reader_table, reader_ok, collected.reshape(seq_count * hops, chunk, 2 * HD)
    )
    returned = lax.all_to_all(summed, "seq", 0, 0, tiled=True)
    grad_local = grad_kv[:, hops * rows :] + returned.reshape(lanes, rows, 2 * HD).astype(F32)

    grad_value_low = grad_local[..., HD:].reshape(total, HD).astype(BF)
    key_normed_grad = rotate(grad_local[..., :HD], cosine, -sine)
    grad_key_proj, key_terms = rms_backward(key_proj, key_gain, key_normed_grad)
    grad_key_low = grad_key_proj.reshape(total, HD).astype(BF)
    query_normed_grad = rotate(
        grad_query.reshape(lanes, rows, HQ, HD), cosine[:, :, None, :], -sine[:, :, None, :]
    )
    grad_query_proj, query_terms = rms_backward(query_proj, query_gain, query_normed_grad)
    grad_query_low = grad_query_proj.reshape(total, q_width).astype(BF)

    grad_kv_low = jnp.concatenate([grad_key_low, grad_value_low], axis=1)
    grad_attn_in = dot_nt(grad_query_low, w_in_full[:, :q_width]) + dot_nt(
        grad_kv_low, w_in_full[:, q_width:]
    )
    grad_input_norm, in_terms = rms_backward(inputs, gain_in, grad_attn_in)
    grad_inputs = grad_middle + grad_input_norm

    def by_peer(values):
        columns = values.reshape(total, cores, width // cores).transpose(1, 0, 2)
        return flip(columns, core)

    def peer_terms(left, right):
        return jnp.concatenate([dot_tn(left, right[j]) for j in range(cores)], axis=0)

    in_peers = by_peer(attn_in)
    branch_peers = by_peer(grad_branch_low)
    narrow = width // cores
    out_terms = sum_cores(peer_terms(mixed_low, branch_peers).astype(BF)).astype(BF)
    query_terms_w = sum_cores(peer_terms(grad_query_low, in_peers).astype(BF)).astype(BF)
    def rows_owned(terms, order):
        terms = terms.reshape(seq_count, q_width // seq_count, narrow)
        terms = jnp.take(terms, own ^ jnp.array(arrangement(order), jnp.int32), axis=0)
        half = seq_count // 2
        return halve(terms[:half], terms[half:], order)[0]

    out_grad = rows_owned(out_terms, others + [SPLIT_BIT])
    query_grad = rows_owned(query_terms_w, swapped + [SPLIT_BIT]).T

    kv_terms = sum_cores(peer_terms(grad_kv_low, in_peers).astype(BF)).astype(BF)
    kv_rows = HD // seq_count
    kv_terms = (
        kv_terms.reshape(2, seq_count, kv_rows, narrow)
        .transpose(1, 0, 2, 3)
        .reshape(seq_count, 2 * kv_rows, narrow)
    )
    gains = jnp.concatenate(
        [
            jnp.sum(in_terms, axis=0),
            jnp.sum(mid_terms, axis=0),
            jnp.sum(ffn_terms, axis=0),
            jnp.sum(top_terms, axis=0),
            jnp.sum(query_terms, axis=(0, 1, 2)),
            jnp.sum(key_terms, axis=(0, 1)),
        ]
    )
    for mask in masks(cores):
        gains = gains + swap(gains, "fsdp", mask)
    gain_size = gains.shape[0]
    gain_rows = -(-gain_size // narrow)
    gains = jnp.pad(gains, (0, gain_rows * narrow - gain_size)).reshape(gain_rows, narrow)
    high = lax.reduce_precision(gains, 8, 7)
    low = gains - high
    tail = jnp.concatenate(
        [
            kv_terms,
            jnp.broadcast_to(high.astype(BF), (seq_count, gain_rows, narrow)),
            jnp.broadcast_to(low.astype(BF), (seq_count, gain_rows, narrow)),
        ],
        axis=1,
    )
    tail = jnp.sum(lax.all_to_all(tail, "seq", 0, 0, tiled=True).astype(F32), axis=0)
    key_grad = tail[:kv_rows].T
    value_grad = tail[kv_rows : 2 * kv_rows].T
    gains = tail[2 * kv_rows : 2 * kv_rows + gain_rows] + tail[2 * kv_rows + gain_rows :]
    gains = gains.reshape(-1)[:gain_size]
    norm_total = gains[: 4 * width].reshape(4, width)
    head_total = gains[4 * width :].reshape(2, HD)

    return (
        result.reshape(1, lanes, rows, width),
        grad_inputs.reshape(1, lanes, rows, width),
        query_grad,
        key_grad,
        value_grad,
        out_grad,
        gate_grad,
        up_grad,
        down_grad,
        norm_total,
        head_total,
    )


def solution(mesh):
    in_specs = (
        P("fsdp", None, "seq", None),
        P("fsdp", None, "seq", None),
        P("fsdp", None, None),
        P("fsdp", None),
        P("fsdp", None),
        P("fsdp", None),
        P("fsdp", None),
        P(None, "fsdp"),
        P(None, "fsdp"),
        P(None, "fsdp"),
        P("fsdp", None),
        P(),
        P(),
    )
    out_specs = (
        P("fsdp", None, "seq", None),
        P("fsdp", None, "seq", None),
        P("fsdp", "seq"),
        P("fsdp", "seq"),
        P("fsdp", "seq"),
        P("seq", "fsdp"),
        P("seq", "fsdp"),
        P("seq", "fsdp"),
        P("fsdp", "seq"),
        P(),
        P(),
    )
    return jax.shard_map(shards, mesh=mesh, in_specs=in_specs, out_specs=out_specs, check_vma=False)
```

```python
import functools
import math

import jax
import jax.numpy as jnp
from jax import lax
from jax.experimental import pallas as pl
from jax.experimental.pallas import tpu as pltpu
from jax.sharding import PartitionSpec as P

HQ = 4
HD = 256
W = 512
EPSILON = 1e-06
ROPE_BASE = 10000.0
SPLIT_BIT = 4

BF = jnp.bfloat16
F32 = jnp.float32


def swap(value, axis, mask):
    count = lax.axis_size(axis)
    return lax.ppermute(value, axis, [(i, i ^ mask) for i in range(count)])


def masks(count):
    return [1 << k for k in range(count.bit_length() - 1)]


def gather_cores(block):
    for mask in masks(lax.axis_size("fsdp")):
        block = jnp.concatenate([block, swap(block, "fsdp", mask)], axis=0)
    return block


def sum_cores(block):
    for mask in reversed(masks(lax.axis_size("fsdp"))):
        half = block.shape[0] // 2
        got = swap(block[half:].astype(BF), "fsdp", mask)
        block = block[:half].astype(F32) + got.astype(F32)
    return block


def flip(parts, index):
    count = parts.shape[0]
    for mask in masks(count):
        turned = jnp.stack([parts[j ^ mask] for j in range(count)])
        parts = jnp.where((index & mask) != 0, turned, parts)
    return parts


def rms_scale(values):
    return lax.rsqrt(jnp.mean(values * values, axis=-1, keepdims=True) + EPSILON)


def rms_forward(values, gain_vec):
    return values * rms_scale(values) * gain_vec


def rms_backward(values, gain_vec, grad_out):
    scale_rows = rms_scale(values)
    weighted = grad_out * gain_vec
    inner_mean = jnp.mean(weighted * values, axis=-1, keepdims=True)
    grad_in = scale_rows * weighted - values * (scale_rows * scale_rows * scale_rows) * inner_mean
    return (grad_in, grad_out * values * scale_rows)


def rope_tables(seq_pos, head_dim):
    half_dim = head_dim // 2
    frequency = jnp.exp(
        jnp.arange(half_dim, dtype=F32) * (-2.0 * math.log(ROPE_BASE) / head_dim)
    )
    angles = seq_pos.astype(F32)[..., None] * frequency
    return (jnp.cos(angles), jnp.sin(angles))


def rotate(values, cosine_table, sine_table):
    half_dim = values.shape[-1] // 2
    first_half = values[..., :half_dim]
    second_half = values[..., half_dim:]
    return jnp.concatenate(
        [
            first_half * cosine_table - second_half * sine_table,
            second_half * cosine_table + first_half * sine_table,
        ],
        axis=-1,
    )


def gelu_tanh(values):
    return jax.nn.gelu(values, approximate=True)


def sequence_info(lengths, stream_pos):
    seq_ends = jnp.cumsum(lengths, axis=-1)
    before = seq_ends[..., None, :] <= stream_pos[..., :, None]
    seq_ids = jnp.sum(before.astype(jnp.int32), axis=-1)
    starts = jnp.sum(jnp.where(before, lengths[..., None, :], 0), axis=-1)
    return (seq_ids, stream_pos - starts)


def dot(a, b):
    return jnp.dot(a, b, preferred_element_type=F32)


def dot_tn(a, b):
    return lax.dot_general(a, b, (((0,), (0,)), ((), ())), preferred_element_type=F32)


def dot_nt(a, b):
    return lax.dot_general(a, b, (((1,), (1,)), ((), ())), preferred_element_type=F32)


def pick(table, source):
    return jnp.take(source, table, axis=0)


def pick_sum(hops, table, valid, source):
    terms = jnp.take(source, table, axis=0).astype(F32) * valid.astype(F32)[:, None, None]
    count = table.shape[0] // hops
    return jnp.sum(terms.reshape((count, hops) + source.shape[1:]), axis=1).astype(source.dtype)


def arrangement(order):
    if not order:
        return [0]
    rest = arrangement(order[1:])
    return [j | order[0] for j in rest] + rest


def after(value, *others):
    return lax.optimization_barrier((value,) + others)[0]


class Turns:
    def __init__(self, token):
        self.token = token

    def wait(self, value):
        return after(value, self.token)

    def end(self, token):
        self.token = token


class Chain:
    def __init__(self, first, rest, order):
        self.rest, self.order = rest, list(order)
        self.got = swap(first, "seq", self.order[0])

    def step(self, turns):
        got = turns.wait(self.got)
        self.total = self.rest.astype(F32) + got.astype(F32)
        half = self.total.shape[0] // 2
        self.order.pop(0)
        if self.order:
            first, self.rest = self.total[:half].astype(BF), self.total[half:].astype(BF)
            self.got = swap(first, "seq", self.order[0])
            turns.end(first)
        else:
            turns.end(self.total)


def tiles(size):
    tile = 256 if size % 256 == 0 else 128
    return tile, size // tile


def column_tiles(size):
    return [(start, min(256, size - start)) for start in range(0, size, 256)]


COST = pl.CostEstimate(flops=1024, bytes_accessed=1024, transcendentals=0)
VMEM = pl.BlockSpec(memory_space=pltpu.VMEM)
SMEM = pl.BlockSpec(memory_space=pltpu.SMEM)
PARAMS = pltpu.CompilerParams(vmem_limit_bytes=56 * 1024 * 1024)
ROOT = math.sqrt(2.0 / math.pi)
CUBE = 0.044715


def ffn_forward_kernel(n, overlap, *refs):
    part, x_refs, (wg, wu, wd) = refs[0], refs[1 : n + 1], refs[n + 1 : n + 4]
    hid_out, act_out, slope_out, keep, send = refs[n + 4 : n + 9]
    x_all, wg_all, wu_all, wd_all, gate, hid, act, slope, load, store = refs[n + 9 :]
    rows = x_refs[0].shape[0]
    share = hid.shape[1]
    tile, count = tiles(share)
    begin = pl.multiple_of(part[0] * (wg.shape[1] - share), 128)
    down_begin = pl.multiple_of(part[0] * (wd.shape[0] - share), 16)
    loads = [
        pltpu.make_async_copy(wg.at[:, pl.ds(begin, share)], wg_all, load.at[0]),
        pltpu.make_async_copy(wu.at[:, pl.ds(begin, share)], wu_all, load.at[1]),
        pltpu.make_async_copy(wd.at[pl.ds(down_begin, share), :], wd_all, load.at[2]),
    ]
    for copy in loads:
        copy.start()
    for j in range(n):
        x_all[j * rows : (j + 1) * rows, :] = x_refs[j][...]
    parts = [slice(i * tile, (i + 1) * tile) for i in range(count)]
    loads[0].wait()
    for cols in parts:
        gate[:, cols] = dot(x_all[...], wg_all[:, cols])
    loads[1].wait()
    for i, cols in enumerate(parts):
        g, u = gate[:, cols], dot(x_all[...], wu_all[:, cols])
        square = g * g
        t = jnp.tanh(g * (ROOT + ROOT * CUBE * square))
        half = 0.5 * (1.0 + t)
        a = g * half
        d = half + a * (1.0 - t) * (ROOT + 3.0 * ROOT * CUBE * square)
        if i * tile < overlap:
            index = i * tile + lax.broadcasted_iota(jnp.int32, a.shape, 1)
            counted = index >= part[0] * overlap
            a, u = jnp.where(counted, a, 0.0), jnp.where(counted, u, 0.0)
        hid[:, cols] = (a * u).astype(BF)
        act[:, cols] = a.astype(BF)
        slope[:, cols] = (u * d).astype(BF)
    stores = [
        pltpu.make_async_copy(hid, hid_out, store.at[0]),
        pltpu.make_async_copy(act, act_out, store.at[1]),
        pltpu.make_async_copy(slope, slope_out, store.at[2]),
    ]
    for copy in stores:
        copy.start()
    loads[2].wait()
    for start, size in column_tiles(wd.shape[1]):
        out = dot(hid[...], wd_all[:, start : start + size])
        half = out.shape[0] // 2
        keep[:, start : start + size] = out[:half]
        send[:, start : start + size] = out[half:].astype(BF)
    for copy in stores:
        copy.wait()


ANY = pl.BlockSpec(memory_space=pl.ANY)


def ffn_forward(part, blocks, wg, wu, wd, share, overlap):
    n, (rows, width) = len(blocks), blocks[0].shape
    total = n * rows
    return pl.pallas_call(
        functools.partial(ffn_forward_kernel, n, overlap),
        out_shape=[jax.ShapeDtypeStruct((total, share), BF)] * 3
        + [
            jax.ShapeDtypeStruct((total // 2, width), F32),
            jax.ShapeDtypeStruct((total // 2, width), BF),
        ],
        in_specs=[SMEM] + [VMEM] * n + [ANY] * 3,
        out_specs=[ANY] * 3 + [VMEM] * 2,
        scratch_shapes=[pltpu.VMEM((total, width), BF)]
        + [pltpu.VMEM((width, share), BF)] * 2
        + [pltpu.VMEM((share, width), BF)]
        + [pltpu.VMEM((total, share), F32)]
        + [pltpu.VMEM((total, share), BF)] * 3
        + [pltpu.SemaphoreType.DMA((3,))] * 2,
        compiler_params=PARAMS,
        cost_estimate=COST,
    )(part, *blocks, wg, wu, wd)


def ffn_backward_kernel(n, *refs):
    part, g_refs, (act, slope, wg, wu, wd) = refs[0], refs[1 : n + 1], refs[n + 1 : n + 6]
    gate_out, up_out, keep, send = refs[n + 6 : n + 10]
    g_all, act_all, slope_all, wg_all, wu_all, wd_all, d_gate, d_up, load, store = refs[n + 10 :]
    rows = g_refs[0].shape[0]
    share = d_gate.shape[1]
    tile, count = tiles(share)
    down_begin = pl.multiple_of(part[0] * (wd.shape[0] - share), 16)
    begin = pl.multiple_of(part[0] * (wg.shape[1] - share), 128)
    loads = [
        pltpu.make_async_copy(wd.at[pl.ds(down_begin, share), :], wd_all, load.at[0]),
        pltpu.make_async_copy(act, act_all, load.at[1]),
        pltpu.make_async_copy(slope, slope_all, load.at[2]),
        pltpu.make_async_copy(wg.at[:, pl.ds(begin, share)], wg_all, load.at[3]),
        pltpu.make_async_copy(wu.at[:, pl.ds(begin, share)], wu_all, load.at[4]),
    ]
    for copy in loads:
        copy.start()
    for j in range(n):
        g_all[j * rows : (j + 1) * rows, :] = g_refs[j][...]
    for copy in loads[:3]:
        copy.wait()
    for i in range(count):
        cols = slice(i * tile, (i + 1) * tile)
        d = dot_nt(g_all[...], wd_all[cols, :])
        d_gate[:, cols] = (d * slope_all[:, cols].astype(F32)).astype(BF)
        d_up[:, cols] = (d * act_all[:, cols].astype(F32)).astype(BF)
    stores = [
        pltpu.make_async_copy(d_gate, gate_out, store.at[0]),
        pltpu.make_async_copy(d_up, up_out, store.at[1]),
    ]
    for copy in stores:
        copy.start()
    for copy in loads[3:]:
        copy.wait()
    for start, size in column_tiles(wg.shape[0]):
        out = dot_nt(d_gate[...], wg_all[start : start + size, :])
        out = out + dot_nt(d_up[...], wu_all[start : start + size, :])
        half = out.shape[0] // 2
        keep[:, start : start + size] = out[:half]
        send[:, start : start + size] = out[half:].astype(BF)
    for copy in stores:
        copy.wait()


def ffn_backward(part, blocks, act, slope, wg, wu, wd):
    n, (rows, width), share = len(blocks), blocks[0].shape, act.shape[1]
    total = n * rows
    return pl.pallas_call(
        functools.partial(ffn_backward_kernel, n),
        out_shape=[jax.ShapeDtypeStruct((total, share), BF)] * 2
        + [
            jax.ShapeDtypeStruct((total // 2, width), F32),
            jax.ShapeDtypeStruct((total // 2, width), BF),
        ],
        in_specs=[SMEM] + [VMEM] * n + [ANY] * 5,
        out_specs=[ANY] * 2 + [VMEM] * 2,
        scratch_shapes=[pltpu.VMEM((total, width), BF)]
        + [pltpu.VMEM((total, share), BF)] * 2
        + [pltpu.VMEM((width, share), BF)] * 2
        + [pltpu.VMEM((share, width), BF)]
        + [pltpu.VMEM((total, share), BF)] * 2
        + [pltpu.SemaphoreType.DMA((5,)), pltpu.SemaphoreType.DMA((2,))],
        compiler_params=PARAMS,
        cost_estimate=COST,
    )(part, *blocks, act, slope, wg, wu, wd)


def weight_kernel(n, pieces, *refs):
    own, left = refs[0], refs[1 : n + 1]
    outs, (turned, out, right, load) = refs[n + 3 : -4], refs[-4:]
    rows = left[0].shape[0]
    tile, count = tiles(right.shape[1])
    half = right.shape[0] // 2

    def copies(i):
        cols = pl.ds(pl.multiple_of(i * tile, tile), tile)
        return [
            pltpu.make_async_copy(
                refs[n + 1 + k].at[:, cols], right.at[k * half : (k + 1) * half, cols], load.at[k, i]
            )
            for k in range(2)
        ]

    for i in range(count):
        for copy in copies(i):
            copy.start()
    for j in range(n):
        turned[:, j * rows : (j + 1) * rows] = left[j][...].T
    me = own[0]
    begin = 0
    for p, (order, size) in enumerate(pieces):
        halves = outs[2 * p : 2 * p + 2]
        block = halves[0].shape[1]

        @pl.loop(0, size // tile)
        def _(i):
            cols = pl.ds(pl.multiple_of(begin + i * tile, tile), tile)
            into = pl.ds(pl.multiple_of(i * tile, tile), tile)
            for copy in copies(begin // tile + i):
                copy.wait()
            out[...] = dot(turned[...], right[:, cols])
            for k, j in enumerate(arrangement(order)):
                source = pl.multiple_of((me ^ j) * block, 8)
                top, k = divmod(k, halves[0].shape[0])
                halves[top][k, :, into] = out[pl.ds(source, block), :].astype(BF)

        begin = begin + size


def weight_terms(own, seq_count, pieces, left, near, far):
    width, share = left[0].shape[1], near.shape[1]
    block = width // seq_count
    half = seq_count // 2
    n = len(left)
    if block % 8:
        full = dot_tn(jnp.concatenate(left), jnp.concatenate([near, far])).astype(BF)
        full = full.reshape(seq_count, block, share)
        outs, begin = [], 0
        for order, size in pieces:
            piece = full[:, :, begin : begin + size]
            piece = jnp.take(piece, own ^ jnp.array(arrangement(order), jnp.int32), axis=0)
            outs += [piece[:half], piece[half:]]
            begin += size
        return outs
    tile, _ = tiles(share)
    return pl.pallas_call(
        functools.partial(weight_kernel, n, pieces),
        out_shape=[
            jax.ShapeDtypeStruct((half, block, size), BF) for _, size in pieces for _ in range(2)
        ],
        in_specs=[SMEM] + [VMEM] * n + [ANY] * 2,
        out_specs=[VMEM] * (2 * len(pieces)),
        scratch_shapes=[
            pltpu.VMEM((width, n * left[0].shape[0]), BF),
            pltpu.VMEM((width, tile), F32),
            pltpu.VMEM((n * left[0].shape[0], share), BF),
            pltpu.SemaphoreType.DMA((2, share // tile)),
        ],
        compiler_params=PARAMS,
        cost_estimate=COST,
    )(own.reshape(1), *left, near, far)


def window_size(width, cores):
    narrow = width // cores
    return max(-(-((c * narrow) % 128 + narrow) // 128) for c in range(cores)) * 128


def window_of(core, narrow, size):
    return pl.ds(pl.multiple_of(core * narrow // 128 * 128, 128), size)


def outer_kernel(cores, core, mixed, branch, query, attn_in, keep, send):
    size = keep.shape[1]
    split = mixed.shape[1]
    narrow = branch.shape[1] // cores
    for part, (left, right) in enumerate(((mixed, branch), (query, attn_in))):
        turned = left[...].T
        for j in range(cores):
            out = dot(turned, right[:, window_of(core[0] ^ j, narrow, size)])
            target, row = (keep, j) if j < cores // 2 else (send, j - cores // 2)
            row = (2 * row + part) * split
            target[row : row + split, :] = out.astype(target.dtype)


def outer_sum_kernel(order, own, keep, got, first, rest):
    me = own[0]
    half, two, _ = first.shape
    block = two // 2
    width = keep.shape[0] // 2
    for k, j in enumerate(arrangement(order)):
        target = first if k < half else rest
        for part in range(2):
            source = pl.ds(pl.multiple_of(part * width + (me ^ j) * block, 16), block)
            total = keep[source, :] + got[source, :].astype(F32)
            target[k % half, part * block : (part + 1) * block, :] = total.astype(BF)


def outer_begin(core, cores, mixed, branch, query, attn_in):
    width = mixed.shape[1]
    size = window_size(branch.shape[1], cores)
    return pl.pallas_call(
        functools.partial(outer_kernel, cores),
        out_shape=[
            jax.ShapeDtypeStruct((cores * width, size), F32),
            jax.ShapeDtypeStruct((cores * width, size), BF),
        ],
        in_specs=[SMEM] + [VMEM] * 4,
        out_specs=[VMEM] * 2,
        compiler_params=PARAMS,
        cost_estimate=COST,
    )(core, mixed, branch, query, attn_in)


def outer_end(own, seq_count, order, keep, got):
    total, size = keep.shape
    block = total // 2 // seq_count
    half = seq_count // 2
    return pl.pallas_call(
        functools.partial(outer_sum_kernel, order),
        out_shape=[jax.ShapeDtypeStruct((half, 2 * block, size), BF)] * 2,
        in_specs=[SMEM, VMEM, VMEM],
        out_specs=[VMEM] * 2,
        compiler_params=PARAMS,
        cost_estimate=COST,
    )(own, keep, got)


def whole_rows(core, peers, full):
    for j, peer in enumerate(peers):
        rows = peer.shape[0]
        full[pl.ds(pl.multiple_of((core[0] ^ j) * rows, 16), rows), :] = peer[...]


def key_value_kernel(n, core, tokens, *refs):
    peers, (gains, head_gains, cosine, sine) = refs[:n], refs[n : n + 4]
    attn_in, key_proj, kv_local, full = refs[n + 4 :]
    whole_rows(core, peers, full)
    normed = rms_forward(tokens[...].astype(F32), gains[0:1, :]).astype(BF)
    attn_in[...] = normed
    both = dot(normed, full[...])
    keys = both[:, :HD]
    key_proj[...] = keys
    turned = rotate(rms_forward(keys, head_gains[1:2, :]), cosine[...], sine[...])
    kv_local[:, :HD] = turned.astype(BF)
    kv_local[:, HD:] = both[:, HD:].astype(BF)


def key_value(core, tokens, peers, gains, head_gains, cosine, sine):
    total, width = tokens.shape
    return pl.pallas_call(
        functools.partial(key_value_kernel, len(peers)),
        out_shape=[
            jax.ShapeDtypeStruct((total, width), BF),
            jax.ShapeDtypeStruct((total, HD), F32),
            jax.ShapeDtypeStruct((total, 2 * HD), BF),
        ],
        in_specs=[SMEM] + [VMEM] * (len(peers) + 5),
        out_specs=[VMEM] * 3,
        scratch_shapes=[pltpu.VMEM((width, 2 * HD), BF)],
        compiler_params=PARAMS,
        cost_estimate=COST,
    )(core, tokens, *peers, gains, head_gains, cosine, sine)


def query_kernel(n, core, attn_in, *refs):
    peers, (head_gains, cosine, sine, proj, query, full) = refs[:n], refs[n:]
    whole_rows(core, peers, full)
    for h in range(HQ):
        cols = slice(h * HD, (h + 1) * HD)
        out = dot(attn_in[...], full[:, cols])
        proj[:, cols] = out
        turned = rotate(rms_forward(out, head_gains[0:1, :]), cosine[...], sine[...])
        query[:, cols] = turned.astype(BF)


def queries_of(core, attn_in, peers, head_gains, cosine, sine):
    total, width = attn_in.shape
    return pl.pallas_call(
        functools.partial(query_kernel, len(peers)),
        out_shape=[
            jax.ShapeDtypeStruct((total, HQ * HD), F32),
            jax.ShapeDtypeStruct((total, HQ * HD), BF),
        ],
        in_specs=[SMEM] + [VMEM] * (len(peers) + 4),
        out_specs=[VMEM] * 2,
        scratch_shapes=[pltpu.VMEM((width, HQ * HD), BF)],
        compiler_params=PARAMS,
        cost_estimate=COST,
    )(core, attn_in, *peers, head_gains, cosine, sine)


def last_kernel(n, core, *refs):
    q_peers, kv_peers = refs[:n], refs[n : 2 * n]
    (
        tokens, attn_in, grad_middle, grad_query, grad_kv, returned, key_proj, cosine, sine,
        gains, head_gains, grad_inputs, keep, send, in_terms, key_terms, q_full, kv_full,
    ) = refs[2 * n :]
    whole_rows(core, q_peers, q_full)
    whole_rows(core, kv_peers, kv_full)
    grads = grad_kv[...] + returned[...].astype(F32)
    normed = rotate(grads[:, :HD], cosine[...], -sine[...])
    d_key, terms = rms_backward(key_proj[...], head_gains[1:2, :], normed)
    key_terms[...] = jnp.broadcast_to(jnp.sum(terms, axis=0, keepdims=True), key_terms.shape)
    low = jnp.concatenate([d_key.astype(BF), grads[:, HD:].astype(BF)], axis=1)
    size = keep.shape[1]
    narrow = attn_in.shape[1] // n
    turned = low.T
    for j in range(n):
        out = dot(turned, attn_in[:, window_of(core[0] ^ j, narrow, size)])
        target, row = (keep, j) if j < n // 2 else (send, j - n // 2)
        row = row * 2 * HD
        target[row : row + 2 * HD, :] = out.astype(target.dtype)
    d_in = dot_nt(grad_query[...], q_full[...]) + dot_nt(low, kv_full[...])
    d_tokens, terms = rms_backward(tokens[...].astype(F32), gains[0:1, :], d_in)
    in_terms[...] = jnp.broadcast_to(jnp.sum(terms, axis=0, keepdims=True), in_terms.shape)
    grad_inputs[...] = grad_middle[...] + d_tokens


def last(core, q_peers, kv_peers, *rest):
    n = len(q_peers)
    total, width = rest[0].shape
    size = window_size(width, n)
    return pl.pallas_call(
        functools.partial(last_kernel, n),
        out_shape=[
            jax.ShapeDtypeStruct((total, width), F32),
            jax.ShapeDtypeStruct((n * HD, size), F32),
            jax.ShapeDtypeStruct((n * HD, size), BF),
            jax.ShapeDtypeStruct((8, width), F32),
            jax.ShapeDtypeStruct((8, HD), F32),
        ],
        in_specs=[SMEM] + [VMEM] * (2 * n + len(rest)),
        out_specs=[VMEM] * 5,
        scratch_shapes=[pltpu.VMEM((width, HQ * HD), BF), pltpu.VMEM((width, 2 * HD), BF)],
        compiler_params=PARAMS,
        cost_estimate=COST,
    )(core, *q_peers, *kv_peers, *rest)


SCALE = HD ** (-0.5)


def keys_of(lane, rows, hops, earlier, kv_local, keys):
    for d in range(1, hops + 1):
        keys[(hops - d) * rows : (hops - d + 1) * rows, :] = earlier[
            d - 1, lane * rows : (lane + 1) * rows, :
        ]
    keys[hops * rows :, :] = kv_local[lane * rows : (lane + 1) * rows, :]


def allowed_of(place, lengths, lane, rows, hops, window):
    first = place[0] * rows
    q_pos = first + lax.broadcasted_iota(jnp.int32, (rows, 1), 0)
    k_pos = first - hops * rows + lax.broadcasted_iota(jnp.int32, (1, (hops + 1) * rows), 1)
    q_id, k_id = jnp.zeros_like(q_pos), jnp.zeros_like(k_pos)
    end = jnp.int32(0)
    for j in range(lengths.shape[1]):
        end = end + lengths[lane, j]
        q_id = q_id + (end <= q_pos).astype(jnp.int32)
        k_id = k_id + (end <= k_pos).astype(jnp.int32)
    return (q_id == k_id) & (k_pos <= q_pos) & (q_pos - k_pos < window) & (k_pos >= 0)


def soft_of(query, keys, allowed):
    scores = jnp.where(allowed, dot_nt(query, keys) * SCALE, -1e30)
    grown = jnp.exp(scores - jnp.max(scores, axis=-1, keepdims=True))
    return grown * (1.0 / jnp.sum(grown, axis=-1, keepdims=True))


def attention_kernel(
    hops, place, lengths, query, kv_local, earlier, tokens, w_out, gains,
    mixed, branch, middle, ffn_in, keys,
):
    lanes = lengths.shape[0]
    rows = query.shape[0] // lanes
    for lane in range(lanes):
        span = slice(lane * rows, (lane + 1) * rows)
        keys_of(lane, rows, hops, earlier, kv_local, keys)
        allowed = allowed_of(place, lengths, lane, rows, hops, W)
        for h in range(HQ):
            cols = slice(h * HD, (h + 1) * HD)
            soft = soft_of(query[span, cols], keys[:, :HD], allowed)
            mixed[span, cols] = dot(soft.astype(BF), keys[:, HD:]).astype(BF)
        out = dot(mixed[span, :], w_out[...])
        branch[span, :] = out
        mid = tokens[span, :].astype(F32) + rms_forward(out, gains[1:2, :])
        middle[span, :] = mid
        ffn_in[span, :] = rms_forward(mid, gains[2:3, :]).astype(BF)


def attention(hops, place, lengths, query, kv_local, earlier, tokens, w_out, gains):
    total, width = tokens.shape
    lanes = lengths.shape[0]
    return pl.pallas_call(
        functools.partial(attention_kernel, hops),
        out_shape=[
            jax.ShapeDtypeStruct(query.shape, BF),
            jax.ShapeDtypeStruct((total, width), F32),
            jax.ShapeDtypeStruct((total, width), F32),
            jax.ShapeDtypeStruct((total, width), BF),
        ],
        in_specs=[SMEM, SMEM] + [VMEM] * 6,
        out_specs=[VMEM] * 4,
        scratch_shapes=[pltpu.VMEM(((hops + 1) * (total // lanes), 2 * HD), BF)],
        compiler_params=PARAMS,
        cost_estimate=COST,
    )(place, lengths, query, kv_local, earlier, tokens, w_out, gains)


def attention_back_kernel(
    hops, place, lengths, query, kv_local, earlier, upstream, w_out, gains, head_gains,
    branch, middle, keep, got, query_proj, cosine, sine,
    grad_middle, grad_branch, grad_query, grad_kv, grad_earlier, norm_terms, head_terms,
    keys, d_mixed, raws, softs, queries, mixes,
):
    lanes = lengths.shape[0]
    rows = query.shape[0] // lanes
    norm_terms[...] = jnp.zeros_like(norm_terms)
    head_terms[...] = jnp.zeros_like(head_terms)
    for lane in range(lanes):
        span = slice(lane * rows, (lane + 1) * rows)
        d_ffn_in = keep[span, :] + got[span, :].astype(F32)
        d_mid, ffn_terms = rms_backward(middle[span, :], gains[2:3, :], d_ffn_in)
        d_mid = d_mid + upstream[span, :].astype(F32)
        grad_middle[span, :] = d_mid
        d_branch, mid_terms = rms_backward(branch[span, :], gains[1:2, :], d_mid)
        norm_terms[0:1, :] += jnp.sum(mid_terms, axis=0, keepdims=True)
        norm_terms[1:2, :] += jnp.sum(ffn_terms, axis=0, keepdims=True)
        low = d_branch.astype(BF)
        grad_branch[span, :] = low
        d_mixed[...] = dot_nt(low, w_out[...]).astype(BF)
        keys_of(lane, rows, hops, earlier, kv_local, keys)
        allowed = allowed_of(place, lengths, lane, rows, hops, W)
        cos, sin = cosine[span, :], sine[span, :]
        for h in range(HQ):
            cols = slice(h * HD, (h + 1) * HD)
            stack = slice(h * rows, (h + 1) * rows)
            soft = soft_of(query[span, cols], keys[:, :HD], allowed)
            d_soft = dot_nt(d_mixed[:, cols], keys[:, HD:])
            inner = jnp.sum(soft * d_soft, axis=-1, keepdims=True)
            raw = (soft * (d_soft - inner) * SCALE).astype(BF)
            raws[stack, :] = raw
            softs[stack, :] = soft.astype(BF)
            queries[stack, :] = query[span, cols]
            mixes[stack, :] = d_mixed[:, cols]
            normed = rotate(dot(raw, keys[:, :HD]), cos, -sin)
            d_query, terms = rms_backward(query_proj[span, cols], head_gains[0:1, :], normed)
            grad_query[span, cols] = d_query.astype(BF)
            head_terms[0:1, :] += jnp.sum(terms, axis=0, keepdims=True)
        for part, (left, right) in enumerate(((raws, queries), (softs, mixes))):
            cols = slice(part * HD, (part + 1) * HD)
            out = dot_tn(left[...], right[...])
            for d in range(1, hops + 1):
                grad_earlier[d - 1, span, cols] = out[
                    (hops - d) * rows : (hops - d + 1) * rows
                ].astype(BF)
            grad_kv[span, cols] = out[hops * rows :]


def attention_back(
    hops, place, lengths, query, kv_local, earlier, upstream, w_out, gains, head_gains,
    branch, middle, keep, got, query_proj, cosine, sine,
):
    total, width = upstream.shape
    lanes = lengths.shape[0]
    rows = total // lanes
    span = (hops + 1) * rows
    return pl.pallas_call(
        functools.partial(attention_back_kernel, hops),
        out_shape=[
            jax.ShapeDtypeStruct((total, width), F32),
            jax.ShapeDtypeStruct((total, width), BF),
            jax.ShapeDtypeStruct(query.shape, BF),
            jax.ShapeDtypeStruct(kv_local.shape, F32),
            jax.ShapeDtypeStruct(earlier.shape, BF),
            jax.ShapeDtypeStruct((8, width), F32),
            jax.ShapeDtypeStruct((8, HD), F32),
        ],
        in_specs=[SMEM, SMEM] + [VMEM] * 14,
        out_specs=[VMEM] * 7,
        scratch_shapes=[
            pltpu.VMEM((span, 2 * HD), BF),
            pltpu.VMEM((rows, HQ * HD), BF),
            pltpu.VMEM((HQ * rows, span), BF),
            pltpu.VMEM((HQ * rows, span), BF),
            pltpu.VMEM((HQ * rows, HD), BF),
            pltpu.VMEM((HQ * rows, HD), BF),
        ],
        compiler_params=PARAMS,
        cost_estimate=COST,
    )(
        place, lengths, query, kv_local, earlier, upstream, w_out, gains, head_gains,
        branch, middle, keep, got, query_proj, cosine, sine,
    )


def shards(
    tokens,
    cotangent,
    lengths,
    deal_order,
    w_query,
    w_key,
    w_value,
    w_out,
    w_gate,
    w_up,
    w_down,
    norm_gains,
    head_gains,
):
    lanes, rows, width = tokens.shape[1:]
    total = lanes * rows
    seq_count = lax.axis_size("seq")
    cores = lax.axis_size("fsdp")
    own = lax.axis_index("seq")
    core = lax.axis_index("fsdp")
    window = W
    hops = (window - 1 + rows - 1) // rows
    chunk = total // seq_count

    deal = deal_order[0]
    places = jnp.arange(seq_count, dtype=jnp.int32)
    back = jnp.sum(jnp.where(deal[None, :] == places[:, None], places[None, :], 0), axis=1)
    place = deal[own]
    steps = jnp.arange(1, hops + 1, dtype=jnp.int32)
    wanted = deal[:, None] - steps[None, :]
    fetch_table = back[jnp.maximum(wanted, 0)].reshape(-1)
    readers = deal[:, None] + steps[None, :]
    reader_ok = (readers < seq_count).astype(jnp.int32).reshape(-1)
    reader_table = (
        back[jnp.minimum(readers, seq_count - 1)] * hops + (steps[None, :] - 1)
    ).reshape(-1)

    token_rows = tokens.reshape(total, width)
    upstream_rows = cotangent.reshape(total, width)
    q_width = HQ * HD
    narrow = width // cores
    core_ref, own_ref = core.reshape(1), own.reshape(1)

    def core_blocks(block):
        blocks = [block]
        for mask in masks(cores):
            together = jnp.concatenate(blocks, axis=0) if len(blocks) > 1 else blocks[0]
            got = swap(together, "fsdp", mask)
            size = block.shape[0]
            blocks = blocks + [got[j * size : (j + 1) * size] for j in range(len(blocks))]
        return blocks

    def core_sum(keep, send):
        steps = masks(cores)[::-1]
        for mask in steps:
            out = keep + swap(send, "fsdp", mask).astype(F32)
            half = out.shape[0] // 2
            keep, send = out[:half], out[half:].astype(BF)
        return out

    kv_peers = core_blocks(jnp.concatenate([w_key, w_value], axis=1))
    local_stream = place * rows + jnp.arange(rows, dtype=jnp.int32)
    positions = sequence_info(lengths[0], jnp.broadcast_to(local_stream, (lanes, rows)))[1]
    cosine, sine = rope_tables(positions.reshape(total), HD)
    attn_in, key_proj, kv_local = key_value(
        core_ref, token_rows, kv_peers, norm_gains, head_gains, cosine, sine
    )

    spread = lax.all_to_all(
        kv_local.reshape(seq_count, chunk, 2 * HD), "seq", 0, 0, tiled=True
    )
    picked = pick(fetch_table, spread).reshape(seq_count, hops * chunk, 2 * HD)
    arrived = lax.all_to_all(picked, "seq", 0, 0, tiled=True)
    earlier = (
        arrived.reshape(seq_count, hops, chunk, 2 * HD)
        .transpose(1, 0, 2, 3)
        .reshape(hops, total, 2 * HD)
    )

    w_query, w_out = lax.optimization_barrier((w_query, w_out, kv_local))[:2]
    query_peers = core_blocks(w_query)
    size = -(-narrow // 128) * 128
    peers_out = gather_cores(jnp.pad(w_out, ((0, 0), (0, size - narrow))))
    peers_out = flip(peers_out.reshape(cores, q_width, size), core)
    w_out_full = jnp.concatenate([peers_out[j, :, :narrow] for j in range(cores)], axis=1)
    query_proj, query_rot = queries_of(
        core_ref, attn_in, query_peers, head_gains, cosine, sine
    )

    hidden_cols = w_gate.shape[1]
    share = -(-hidden_cols // 256) * 128
    overlap = 2 * share - hidden_cols
    part = ((own & SPLIT_BIT) != 0).astype(jnp.int32)
    part_ref = part.reshape(1)
    if (hidden_cols - share) % 128:
        begin = part * (hidden_cols - share)
        w_gate = lax.dynamic_slice_in_dim(w_gate, begin, share, 1)
        w_up = lax.dynamic_slice_in_dim(w_up, begin, share, 1)
        w_down = lax.dynamic_slice_in_dim(w_down, begin, share, 0)

    earlier = after(earlier, query_rot, w_out_full)
    place_ref, lengths_ref = place.reshape(1), lengths[0]
    mixed_low, branch, middle, ffn_in = attention(
        hops, place_ref, lengths_ref, query_rot, kv_local, earlier, token_rows, w_out_full, norm_gains
    )

    def sum_group(near_part, far_part):
        got = swap(core_sum(*far_part).astype(BF), "seq", SPLIT_BIT)
        return core_sum(*near_part), got

    far_in = swap(ffn_in, "seq", SPLIT_BIT)
    near_all = core_blocks(ffn_in)
    near = ffn_forward(part_ref, near_all, w_gate, w_up, w_down, share, overlap)
    far_all = core_blocks(after(far_in, near[0]))
    far = ffn_forward(part_ref, far_all, w_gate, w_up, w_down, share, overlap)
    keep, got = sum_group(near[3:], far[3:])
    ffn_out = keep + got.astype(F32)
    result = middle + rms_forward(ffn_out, norm_gains[3])

    grad_ffn_out, top_terms = rms_backward(ffn_out, norm_gains[3], upstream_rows.astype(F32))
    top_terms = jnp.sum(top_terms, axis=0)
    grad_low = grad_ffn_out.astype(BF)
    far_grad = swap(grad_low, "seq", SPLIT_BIT)
    near_grads = core_blocks(grad_low)
    near_back = ffn_backward(part_ref, near_grads, near[1], near[2], w_gate, w_up, w_down)
    far_grads = core_blocks(after(far_grad, near_back[0]))
    others = [m for m in masks(seq_count) if m != SPLIT_BIT]
    swapped = [others[1], others[0]] + others[2:]

    def terms_of(left, right, pieces):
        pieces = [(order + [SPLIT_BIT], size) for order, size in pieces]
        return weight_terms(own, seq_count, pieces, left, *right)

    down_terms = terms_of(
        near_grads + far_grads,
        (near[0], far[0]),
        [(others, share)],
    )
    far_grads[0] = after(far_grads[0], *down_terms)
    far_back = ffn_backward(part_ref, far_grads, far[1], far[2], w_gate, w_up, w_down)
    keep, got = sum_group(near_back[2:], far_back[2:])

    gate_terms = terms_of(near_all + far_all, (near_back[0], far_back[0]), [(swapped, share)])
    up_terms = terms_of(
        near_all + far_all, (near_back[1], after(far_back[1], *gate_terms)), [(others, share)]
    )
    down_c = Chain(*down_terms, others)
    gate_c = Chain(*gate_terms, swapped)
    up_c = Chain(*up_terms, others)
    turns = Turns(up_terms[0])

    (
        grad_middle, grad_branch_low, grad_query_low, grad_kv, grad_earlier, norm_terms, head_terms
    ) = attention_back(
        hops, place_ref, lengths_ref, query_rot, kv_local, earlier, upstream_rows, w_out_full,
        norm_gains, head_gains, branch, middle, keep, turns.wait(got), query_proj, cosine, sine,
    )

    outward = (
        grad_earlier.reshape(hops, seq_count, chunk, 2 * HD)
        .transpose(1, 0, 2, 3)
        .reshape(seq_count, hops * chunk, 2 * HD)
    )
    collected = lax.all_to_all(outward, "seq", 0, 0, tiled=True)

    turns.end(outward)
    down_c.step(turns)
    outer_keep, outer_send = outer_begin(
        core_ref, cores, mixed_low, grad_branch_low, turns.wait(grad_query_low), attn_in
    )
    turns.end(outer_send)
    every = swapped + [SPLIT_BIT]
    if cores == 2:
        outer_got = swap(outer_send, "fsdp", 1)
    else:
        outer_keep = core_sum(outer_keep, outer_send)
        outer_got = jnp.zeros(outer_keep.shape, BF)
    gate_c.step(turns)
    attention_terms = outer_end(own_ref, seq_count, every, outer_keep, turns.wait(outer_got))
    turns.end(attention_terms[0])
    outer_c = Chain(*attention_terms, every)
    up_c.step(turns)
    down_c.step(turns)
    summed = pick_sum(
        hops,
        reader_table,
        reader_ok,
        turns.wait(collected).reshape(seq_count * hops, chunk, 2 * HD),
    )
    turns.end(summed)
    returned = lax.all_to_all(summed, "seq", 0, 0, tiled=True)
    gate_c.step(turns)
    down_c.step(turns)
    up_c.step(turns)
    outer_c.step(turns)
    returned = turns.wait(returned)

    grad_inputs, kv_keep, kv_send, in_terms, key_terms = last(
        core_ref, query_peers, kv_peers, token_rows, attn_in, grad_middle, grad_query_low, grad_kv,
        returned.reshape(total, 2 * HD), key_proj, cosine, sine, norm_gains, head_gains,
    )
    kv_terms = core_sum(kv_keep, kv_send).astype(BF)
    size = kv_terms.shape[1]
    kv_rows = HD // seq_count
    kv_terms = (
        kv_terms.reshape(2, seq_count, kv_rows, size)
        .transpose(1, 0, 2, 3)
        .reshape(seq_count, 2 * kv_rows, size)
    )
    gains = jnp.concatenate(
        [in_terms[0], norm_terms[0], norm_terms[1], top_terms, head_terms[0], key_terms[0]]
    )
    for mask in masks(cores):
        gains = gains + swap(gains, "fsdp", mask)
    gain_size = gains.shape[0]
    gain_rows = -(-gain_size // size)
    gains = jnp.pad(gains, (0, gain_rows * size - gain_size)).reshape(gain_rows, size)
    tail = jnp.concatenate(
        [kv_terms, jnp.broadcast_to(gains.astype(BF), (seq_count, gain_rows, size))], axis=1
    )
    ended = lax.all_to_all(tail, "seq", 0, 0, tiled=True)
    turns.end(tail)

    def exchanged(*chains):
        mine = jnp.concatenate([chain.total[1] for chain in chains], axis=1)
        sent = jnp.concatenate([chain.total[0].astype(BF) for chain in chains], axis=1)
        return mine, swap(sent, "seq", SPLIT_BIT)

    gate_c.step(turns)
    outer_c.step(turns)
    up_c.step(turns)
    ffn_mine, ffn_got = exchanged(down_c, gate_c, up_c)
    outer_c.step(turns)

    def own_columns(values):
        return lax.dynamic_slice_in_dim(values, core * narrow % 128, narrow, 1)

    ended = jnp.sum(turns.wait(ended).astype(F32), axis=0)
    key_grad = own_columns(ended[:kv_rows]).T
    value_grad = own_columns(ended[kv_rows : 2 * kv_rows]).T
    gains = ended[2 * kv_rows :].reshape(-1)[:gain_size]

    ffn_got = turns.wait(ffn_got).astype(F32)
    lower = jnp.where(part == 0, ffn_mine, ffn_got)
    upper = jnp.where(part == 0, ffn_got, ffn_mine)
    down_grad, gate_grad, up_grad = (
        jnp.concatenate(
            [
                lower[:, k * share : (k + 1) * share],
                upper[:, k * share + overlap : (k + 1) * share],
            ],
            axis=1,
        )
        for k in range(3)
    )
    down_grad = down_grad.T
    outer_c.step(turns)
    attention_grad = own_columns(outer_c.total[0])
    query_rows = q_width // seq_count
    out_grad = attention_grad[:query_rows]
    query_grad = attention_grad[query_rows:].T

    norm_total = gains[: 4 * width].reshape(4, width)
    head_total = gains[4 * width :].reshape(2, HD)

    return (
        result.reshape(1, lanes, rows, width),
        grad_inputs.reshape(1, lanes, rows, width),
        query_grad,
        key_grad,
        value_grad,
        out_grad,
        gate_grad,
        up_grad,
        down_grad,
        norm_total,
        head_total,
    )


def solution(mesh):
    in_specs = (
        P("fsdp", None, "seq", None),
        P("fsdp", None, "seq", None),
        P("fsdp", None, None),
        P("fsdp", None),
        P("fsdp", None),
        P("fsdp", None),
        P("fsdp", None),
        P(None, "fsdp"),
        P(None, "fsdp"),
        P(None, "fsdp"),
        P("fsdp", None),
        P(),
        P(),
    )
    out_specs = (
        P("fsdp", None, "seq", None),
        P("fsdp", None, "seq", None),
        P("fsdp", "seq"),
        P("fsdp", "seq"),
        P("fsdp", "seq"),
        P("seq", "fsdp"),
        P("seq", "fsdp"),
        P("seq", "fsdp"),
        P("fsdp", "seq"),
        P(),
        P(),
    )
    return jax.shard_map(shards, mesh=mesh, in_specs=in_specs, out_specs=out_specs, check_vma=False)
```

```python
import functools
import math

import jax
import jax.numpy as jnp
from jax import lax
from jax.experimental import pallas as pl
from jax.experimental.pallas import tpu as pltpu
from jax.sharding import PartitionSpec as P

HQ = 4
HD = 256
W = 512
EPSILON = 1e-06
ROPE_BASE = 10000.0
SPLIT_BIT = 4

BF = jnp.bfloat16
F32 = jnp.float32


def swap(value, axis, mask):
    count = lax.axis_size(axis)
    return lax.ppermute(value, axis, [(i, i ^ mask) for i in range(count)])


def masks(count):
    return [1 << k for k in range(count.bit_length() - 1)]


def gather_cores(block):
    for mask in masks(lax.axis_size("fsdp")):
        block = jnp.concatenate([block, swap(block, "fsdp", mask)], axis=0)
    return block


def sum_cores(block):
    for mask in reversed(masks(lax.axis_size("fsdp"))):
        half = block.shape[0] // 2
        got = swap(block[half:].astype(BF), "fsdp", mask)
        block = block[:half].astype(F32) + got.astype(F32)
    return block


def flip(parts, index):
    count = parts.shape[0]
    for mask in masks(count):
        turned = jnp.stack([parts[j ^ mask] for j in range(count)])
        parts = jnp.where((index & mask) != 0, turned, parts)
    return parts


def rms_scale(values):
    return lax.rsqrt(jnp.mean(values * values, axis=-1, keepdims=True) + EPSILON)


def rms_forward(values, gain_vec):
    return values * rms_scale(values) * gain_vec


def rms_backward(values, gain_vec, grad_out):
    scale_rows = rms_scale(values)
    weighted = grad_out * gain_vec
    inner_mean = jnp.mean(weighted * values, axis=-1, keepdims=True)
    grad_in = scale_rows * weighted - values * (scale_rows * scale_rows * scale_rows) * inner_mean
    return (grad_in, grad_out * values * scale_rows)


def rope_tables(seq_pos, head_dim):
    half_dim = head_dim // 2
    frequency = jnp.exp(
        jnp.arange(half_dim, dtype=F32) * (-2.0 * math.log(ROPE_BASE) / head_dim)
    )
    angles = seq_pos.astype(F32)[..., None] * frequency
    return (jnp.cos(angles), jnp.sin(angles))


def rotate(values, cosine_table, sine_table):
    half_dim = values.shape[-1] // 2
    first_half = values[..., :half_dim]
    second_half = values[..., half_dim:]
    return jnp.concatenate(
        [
            first_half * cosine_table - second_half * sine_table,
            second_half * cosine_table + first_half * sine_table,
        ],
        axis=-1,
    )


def gelu_tanh(values):
    return jax.nn.gelu(values, approximate=True)


def sequence_info(lengths, stream_pos):
    seq_ends = jnp.cumsum(lengths, axis=-1)
    before = seq_ends[..., None, :] <= stream_pos[..., :, None]
    seq_ids = jnp.sum(before.astype(jnp.int32), axis=-1)
    starts = jnp.sum(jnp.where(before, lengths[..., None, :], 0), axis=-1)
    return (seq_ids, stream_pos - starts)


def dot(a, b):
    return jnp.dot(a, b, preferred_element_type=F32)


def dot_tn(a, b):
    return lax.dot_general(a, b, (((0,), (0,)), ((), ())), preferred_element_type=F32)


def dot_nt(a, b):
    return lax.dot_general(a, b, (((1,), (1,)), ((), ())), preferred_element_type=F32)


def pick(table, source):
    return jnp.take(source, table, axis=0, mode="clip")


def pick_sum(hops, table, valid, source):
    terms = jnp.take(source, table, axis=0, mode="clip").astype(F32) * valid.astype(F32)[:, None, None]
    count = table.shape[0] // hops
    return jnp.sum(terms.reshape((count, hops) + source.shape[1:]), axis=1).astype(source.dtype)


QUAD = 4


def quads(count):
    return [[base + q for q in range(QUAD)] for base in range(0, count, QUAD)]


def quad_arrangement(order):
    return [(q, j) for q in range(QUAD) for j in arrangement(order)]


def places_of(order, quad):
    if quad:
        return [lambda me, q=q, j=j: ((me & ~(QUAD - 1)) ^ j) + q for q, j in quad_arrangement(order)]
    return [lambda me, j=j: me ^ j for j in arrangement(order)]


def arrangement(order):
    if not order:
        return [0]
    rest = arrangement(order[1:])
    return [j | order[0] for j in rest] + rest


def after(value, *others):
    return lax.optimization_barrier((value,) + others)[0]


class Turns:
    def __init__(self, token):
        self.token = token

    def wait(self, value):
        return after(value, self.token)

    def end(self, token):
        self.token = token


def step_kernel(rest, got, *outs):
    count = rest.shape[0]
    for k in range(count):
        total = rest[k].astype(F32) + got[k].astype(F32)
        top, row = divmod(k, outs[0].shape[0])
        outs[top][row] = total.astype(outs[top].dtype)


def step_of(rest, got, final):
    count = rest.shape[0]
    parts, kind = (1, F32) if final else (2, BF)
    shape = jax.ShapeDtypeStruct((count // parts,) + rest.shape[1:], kind)
    return pl.pallas_call(
        step_kernel,
        out_shape=[shape] * parts,
        in_specs=[VMEM] * 2,
        out_specs=[VMEM] * parts,
        compiler_params=PARAMS,
        cost_estimate=COST,
    )(rest, got)


def quad_kernel(got, *outs):
    count = got.shape[0] // QUAD
    for k in range(count):
        total = sum(got[q * count + k].astype(F32) for q in range(QUAD))
        top, row = divmod(k, outs[0].shape[0])
        outs[top][row] = total.astype(BF)


def quad_sum(got):
    shape = jax.ShapeDtypeStruct((got.shape[0] // QUAD // 2,) + got.shape[1:], BF)
    return pl.pallas_call(
        quad_kernel,
        out_shape=[shape] * 2,
        in_specs=[VMEM],
        out_specs=[VMEM] * 2,
        compiler_params=PARAMS,
        cost_estimate=COST,
    )(got)


class Chain:
    def __init__(self, first, rest, order):
        self.rest, self.order = rest, list(order)
        self.got = swap(first, "seq", self.order[0])

    def step(self, turns):
        got = turns.wait(self.got)
        self.order.pop(0)
        if self.order:
            first, self.rest = step_of(self.rest, got, False)
            self.got = swap(first, "seq", self.order[0])
            turns.end(first)
        else:
            (self.total,) = step_of(self.rest, got, True)
            turns.end(self.total)


def tiles(size):
    tile = 256 if size % 256 == 0 else 128
    return tile, size // tile


def column_tiles(size):
    return [(start, min(256, size - start)) for start in range(0, size, 256)]


COST = pl.CostEstimate(flops=1024, bytes_accessed=1024, transcendentals=0)
VMEM = pl.BlockSpec(memory_space=pltpu.VMEM)
SMEM = pl.BlockSpec(memory_space=pltpu.SMEM)
PARAMS = pltpu.CompilerParams(vmem_limit_bytes=56 * 1024 * 1024)
ROOT = math.sqrt(2.0 / math.pi)
CUBE = 0.044715


def ffn_forward_kernel(n, overlap, *refs):
    part, x_refs, (wg, wu, wd) = refs[0], refs[1 : n + 1], refs[n + 1 : n + 4]
    hid_out, act_out, slope_out, keep, send = refs[n + 4 : n + 9]
    x_all, wg_all, wu_all, wd_all, gate, hid, act, slope, load, store = refs[n + 9 :]
    rows = x_refs[0].shape[0]
    share = hid.shape[1]
    tile, count = tiles(share)
    begin = pl.multiple_of(part[0] * (wg.shape[1] - share), 128)
    down_begin = pl.multiple_of(part[0] * (wd.shape[0] - share), 16)
    loads = [
        pltpu.make_async_copy(wg.at[:, pl.ds(begin, share)], wg_all, load.at[0]),
        pltpu.make_async_copy(wu.at[:, pl.ds(begin, share)], wu_all, load.at[1]),
        pltpu.make_async_copy(wd.at[pl.ds(down_begin, share), :], wd_all, load.at[2]),
    ]
    for copy in loads:
        copy.start()
    for j in range(n):
        x_all[j * rows : (j + 1) * rows, :] = x_refs[j][...]
    parts = [slice(i * tile, (i + 1) * tile) for i in range(count)]
    loads[0].wait()
    for cols in parts:
        gate[:, cols] = dot(x_all[...], wg_all[:, cols])
    loads[1].wait()
    for i, cols in enumerate(parts):
        g, u = gate[:, cols], dot(x_all[...], wu_all[:, cols])
        square = g * g
        t = jnp.tanh(g * (ROOT + ROOT * CUBE * square))
        half = 0.5 * (1.0 + t)
        a = g * half
        d = half + a * (1.0 - t) * (ROOT + 3.0 * ROOT * CUBE * square)
        if i * tile < overlap:
            index = i * tile + lax.broadcasted_iota(jnp.int32, a.shape, 1)
            counted = index >= part[0] * overlap
            a, u = jnp.where(counted, a, 0.0), jnp.where(counted, u, 0.0)
        hid[:, cols] = (a * u).astype(BF)
        act[:, cols] = a.astype(BF)
        slope[:, cols] = (u * d).astype(BF)
    stores = [
        pltpu.make_async_copy(hid, hid_out, store.at[0]),
        pltpu.make_async_copy(act, act_out, store.at[1]),
        pltpu.make_async_copy(slope, slope_out, store.at[2]),
    ]
    for copy in stores:
        copy.start()
    loads[2].wait()
    for start, size in column_tiles(wd.shape[1]):
        out = dot(hid[...], wd_all[:, start : start + size])
        half = out.shape[0] // 2
        keep[:, start : start + size] = out[:half]
        send[:, start : start + size] = out[half:].astype(BF)
    for copy in stores:
        copy.wait()


ANY = pl.BlockSpec(memory_space=pl.ANY)


def ffn_forward(part, blocks, wg, wu, wd, share, overlap):
    n, (rows, width) = len(blocks), blocks[0].shape
    total = n * rows
    return pl.pallas_call(
        functools.partial(ffn_forward_kernel, n, overlap),
        out_shape=[jax.ShapeDtypeStruct((total, share), BF)] * 3
        + [
            jax.ShapeDtypeStruct((total // 2, width), F32),
            jax.ShapeDtypeStruct((total // 2, width), BF),
        ],
        in_specs=[SMEM] + [VMEM] * n + [ANY] * 3,
        out_specs=[ANY] * 3 + [VMEM] * 2,
        scratch_shapes=[pltpu.VMEM((total, width), BF)]
        + [pltpu.VMEM((width, share), BF)] * 2
        + [pltpu.VMEM((share, width), BF)]
        + [pltpu.VMEM((total, share), F32)]
        + [pltpu.VMEM((total, share), BF)] * 3
        + [pltpu.SemaphoreType.DMA((3,))] * 2,
        compiler_params=PARAMS,
        cost_estimate=COST,
    )(part, *blocks, wg, wu, wd)


def ffn_backward_kernel(n, *refs):
    part, g_refs, (act, slope, wg, wu, wd) = refs[0], refs[1 : n + 1], refs[n + 1 : n + 6]
    gate_out, up_out, keep, send = refs[n + 6 : n + 10]
    g_all, act_all, slope_all, wg_all, wu_all, wd_all, d_gate, d_up, load, store = refs[n + 10 :]
    rows = g_refs[0].shape[0]
    share = d_gate.shape[1]
    tile, count = tiles(share)
    down_begin = pl.multiple_of(part[0] * (wd.shape[0] - share), 16)
    begin = pl.multiple_of(part[0] * (wg.shape[1] - share), 128)
    loads = [
        pltpu.make_async_copy(wd.at[pl.ds(down_begin, share), :], wd_all, load.at[0]),
        pltpu.make_async_copy(act, act_all, load.at[1]),
        pltpu.make_async_copy(slope, slope_all, load.at[2]),
        pltpu.make_async_copy(wg.at[:, pl.ds(begin, share)], wg_all, load.at[3]),
        pltpu.make_async_copy(wu.at[:, pl.ds(begin, share)], wu_all, load.at[4]),
    ]
    for copy in loads:
        copy.start()
    for j in range(n):
        g_all[j * rows : (j + 1) * rows, :] = g_refs[j][...]
    for copy in loads[:3]:
        copy.wait()
    for i in range(count):
        cols = slice(i * tile, (i + 1) * tile)
        d = dot_nt(g_all[...], wd_all[cols, :])
        d_gate[:, cols] = (d * slope_all[:, cols].astype(F32)).astype(BF)
        d_up[:, cols] = (d * act_all[:, cols].astype(F32)).astype(BF)
    stores = [
        pltpu.make_async_copy(d_gate, gate_out, store.at[0]),
        pltpu.make_async_copy(d_up, up_out, store.at[1]),
    ]
    for copy in stores:
        copy.start()
    for copy in loads[3:]:
        copy.wait()
    for start, size in column_tiles(wg.shape[0]):
        out = dot_nt(d_gate[...], wg_all[start : start + size, :])
        out = out + dot_nt(d_up[...], wu_all[start : start + size, :])
        half = out.shape[0] // 2
        keep[:, start : start + size] = out[:half]
        send[:, start : start + size] = out[half:].astype(BF)
    for copy in stores:
        copy.wait()


def ffn_backward(part, blocks, act, slope, wg, wu, wd):
    n, (rows, width), share = len(blocks), blocks[0].shape, act.shape[1]
    total = n * rows
    return pl.pallas_call(
        functools.partial(ffn_backward_kernel, n),
        out_shape=[jax.ShapeDtypeStruct((total, share), BF)] * 2
        + [
            jax.ShapeDtypeStruct((total // 2, width), F32),
            jax.ShapeDtypeStruct((total // 2, width), BF),
        ],
        in_specs=[SMEM] + [VMEM] * n + [ANY] * 5,
        out_specs=[ANY] * 2 + [VMEM] * 2,
        scratch_shapes=[pltpu.VMEM((total, width), BF)]
        + [pltpu.VMEM((total, share), BF)] * 2
        + [pltpu.VMEM((width, share), BF)] * 2
        + [pltpu.VMEM((share, width), BF)]
        + [pltpu.VMEM((total, share), BF)] * 2
        + [pltpu.SemaphoreType.DMA((5,)), pltpu.SemaphoreType.DMA((2,))],
        compiler_params=PARAMS,
        cost_estimate=COST,
    )(part, *blocks, act, slope, wg, wu, wd)


def weight_kernel(n, pieces, *refs):
    own, left = refs[0], refs[1 : n + 1]
    outs, (turned, out, right, load) = refs[n + 3 : -4], refs[-4:]
    rows = left[0].shape[0]
    tile, count = tiles(right.shape[1])
    half = right.shape[0] // 2

    def copies(i):
        cols = pl.ds(pl.multiple_of(i * tile, tile), tile)
        return [
            pltpu.make_async_copy(
                refs[n + 1 + k].at[:, cols], right.at[k * half : (k + 1) * half, cols], load.at[k, i]
            )
            for k in range(2)
        ]

    for i in range(count):
        for copy in copies(i):
            copy.start()
    for j in range(n):
        turned[:, j * rows : (j + 1) * rows] = left[j][...].T
    me = own[0]
    begin = 0
    for order, size, quad in pieces:
        halves, outs = (outs[:1], outs[1:]) if quad else (outs[:2], outs[2:])
        block = halves[0].shape[1]

        @pl.loop(0, size // tile)
        def _(i):
            cols = pl.ds(pl.multiple_of(begin + i * tile, tile), tile)
            into = pl.ds(pl.multiple_of(i * tile, tile), tile)
            for copy in copies(begin // tile + i):
                copy.wait()
            out[...] = dot(turned[...], right[:, cols])
            for k, owner in enumerate(places_of(order, quad)):
                source = pl.multiple_of(owner(me) * block, 8)
                top, k = divmod(k, halves[0].shape[0])
                halves[top][k, :, into] = out[pl.ds(source, block), :].astype(BF)

        begin = begin + size


def weight_terms(own, seq_count, pieces, left, near, far):
    width, share = left[0].shape[1], near.shape[1]
    block = width // seq_count
    half = seq_count // 2
    n = len(left)
    if block % 8:
        full = dot_tn(jnp.concatenate(left), jnp.concatenate([near, far])).astype(BF)
        full = full.reshape(seq_count, block, share)
        outs, begin = [], 0
        for order, size, quad in pieces:
            piece = full[:, :, begin : begin + size]
            owners = jnp.stack([owner(own) for owner in places_of(order, quad)])
            piece = jnp.take(piece, owners, axis=0, mode="clip")
            outs += [piece] if quad else [piece[:half], piece[half:]]
            begin += size
        return outs
    tile, _ = tiles(share)
    return pl.pallas_call(
        functools.partial(weight_kernel, n, pieces),
        out_shape=[
            jax.ShapeDtypeStruct((seq_count if quad else half, block, size), BF)
            for _, size, quad in pieces
            for _ in range(1 if quad else 2)
        ],
        in_specs=[SMEM] + [VMEM] * n + [ANY] * 2,
        out_specs=[VMEM] * sum(1 if quad else 2 for _, _, quad in pieces),
        scratch_shapes=[
            pltpu.VMEM((width, n * left[0].shape[0]), BF),
            pltpu.VMEM((width, tile), F32),
            pltpu.VMEM((n * left[0].shape[0], share), BF),
            pltpu.SemaphoreType.DMA((2, share // tile)),
        ],
        compiler_params=PARAMS,
        cost_estimate=COST,
    )(own.reshape(1), *left, near, far)


def window_size(width, cores):
    narrow = width // cores
    return max(-(-((c * narrow) % 128 + narrow) // 128) for c in range(cores)) * 128


def window_of(core, narrow, size):
    return pl.ds(pl.multiple_of(core * narrow // 128 * 128, 128), size)


def outer_kernel(cores, core, mixed, branch, query, attn_in, keep, send):
    size = keep.shape[1]
    split = mixed.shape[1]
    narrow = branch.shape[1] // cores
    for part, (left, right) in enumerate(((mixed, branch), (query, attn_in))):
        turned = left[...].T
        for j in range(cores):
            out = dot(turned, right[:, window_of(core[0] ^ j, narrow, size)])
            target, row = (keep, j) if j < cores // 2 else (send, j - cores // 2)
            row = (2 * row + part) * split
            target[row : row + split, :] = out.astype(target.dtype)


def outer_sum_kernel(order, own, keep, got, first, rest):
    me = own[0]
    half, padded, two = first.shape
    size = two // 2
    width = keep.shape[0] // 2
    block = width // (2 * half)
    for k, j in enumerate(arrangement(order)):
        target = first if k < half else rest
        for part in range(2):
            source = pl.ds(pl.multiple_of(part * width + (me ^ j) * block, 16), block)
            total = keep[source, :] + got[source, :].astype(F32)
            total = jnp.concatenate([total, jnp.zeros((padded - block, size), F32)], axis=0)
            target[k % half, :, part * size : (part + 1) * size] = total.astype(BF)


def outer_begin(core, cores, mixed, branch, query, attn_in):
    width = mixed.shape[1]
    size = window_size(branch.shape[1], cores)
    return pl.pallas_call(
        functools.partial(outer_kernel, cores),
        out_shape=[
            jax.ShapeDtypeStruct((cores * width, size), F32),
            jax.ShapeDtypeStruct((cores * width, size), BF),
        ],
        in_specs=[SMEM] + [VMEM] * 4,
        out_specs=[VMEM] * 2,
        compiler_params=PARAMS,
        cost_estimate=COST,
    )(core, mixed, branch, query, attn_in)


def outer_end(own, seq_count, order, keep, got, padded):
    total, size = keep.shape
    half = seq_count // 2
    return pl.pallas_call(
        functools.partial(outer_sum_kernel, order),
        out_shape=[jax.ShapeDtypeStruct((half, padded, 2 * size), BF)] * 2,
        in_specs=[SMEM, VMEM, VMEM],
        out_specs=[VMEM] * 2,
        compiler_params=PARAMS,
        cost_estimate=COST,
    )(own, keep, got)


def outer_pair_kernel(
    order, own, core, mixed, mixed_peer, branch, query, late, attn_in, attn_peer,
    first, rest, left, right, total,
):
    me = own[0]
    half, padded, two = first.shape
    size = two // 2
    rows, width = mixed.shape
    block = width // (2 * half)
    window = window_of(core[0], branch.shape[1] // 2, size)
    for part, (mine, peer, other, other_peer) in enumerate(
        (
            (mixed, mixed_peer, branch, late[:, width:]),
            (query, late.at[:, :width], attn_in, attn_peer[...]),
        )
    ):
        left[:rows, :] = mine[...]
        left[rows:, :] = peer[...]
        right[:rows, :] = other[:, window]
        right[rows:, :] = other_peer
        total[part] = dot_tn(left[...], right[...])
        for k, j in enumerate(arrangement(order)):
            target = first if k < half else rest
            value = total[part, pl.ds(pl.multiple_of((me ^ j) * block, 16), block), :]
            value = jnp.concatenate([value, jnp.zeros((padded - block, size), F32)], axis=0)
            target[k % half, :, part * size : (part + 1) * size] = value.astype(BF)


def outer_pair(own, core, seq_count, order, padded, mixed, *rest):
    rows, width = mixed.shape
    size = rest[-1].shape[1]
    half = seq_count // 2
    return pl.pallas_call(
        functools.partial(outer_pair_kernel, order),
        out_shape=[jax.ShapeDtypeStruct((half, padded, 2 * size), BF)] * 2,
        in_specs=[SMEM, SMEM] + [VMEM] * (1 + len(rest)),
        out_specs=[VMEM] * 2,
        scratch_shapes=[
            pltpu.VMEM((2 * rows, width), BF),
            pltpu.VMEM((2 * rows, size), BF),
            pltpu.VMEM((2, width, size), F32),
        ],
        compiler_params=PARAMS,
        cost_estimate=COST,
    )(own, core, mixed, *rest)


def whole_rows(core, peers, full):
    for j, peer in enumerate(peers):
        rows = peer.shape[0]
        full[pl.ds(pl.multiple_of((core[0] ^ j) * rows, 16), rows), :] = peer[...]


def key_value_kernel(n, core, tokens, *refs):
    peers, (gains, head_gains, cosine, sine) = refs[:n], refs[n : n + 4]
    attn_in, key_proj, kv_local, full = refs[n + 4 :]
    whole_rows(core, peers, full)
    normed = rms_forward(tokens[...].astype(F32), gains[0:1, :]).astype(BF)
    attn_in[...] = normed
    both = dot(normed, full[...])
    keys = both[:, :HD]
    key_proj[...] = keys
    turned = rotate(rms_forward(keys, head_gains[1:2, :]), cosine[...], sine[...])
    kv_local[:, :HD] = turned.astype(BF)
    kv_local[:, HD:] = both[:, HD:].astype(BF)


def key_value(core, tokens, peers, gains, head_gains, cosine, sine):
    total, width = tokens.shape
    return pl.pallas_call(
        functools.partial(key_value_kernel, len(peers)),
        out_shape=[
            jax.ShapeDtypeStruct((total, width), BF),
            jax.ShapeDtypeStruct((total, HD), F32),
            jax.ShapeDtypeStruct((total, 2 * HD), BF),
        ],
        in_specs=[SMEM] + [VMEM] * (len(peers) + 5),
        out_specs=[VMEM] * 3,
        scratch_shapes=[pltpu.VMEM((width, 2 * HD), BF)],
        compiler_params=PARAMS,
        cost_estimate=COST,
    )(core, tokens, *peers, gains, head_gains, cosine, sine)


def query_kernel(n, core, attn_in, *refs):
    peers, (head_gains, cosine, sine, proj, query, full) = refs[:n], refs[n:]
    whole_rows(core, peers, full)
    for h in range(HQ):
        cols = slice(h * HD, (h + 1) * HD)
        out = dot(attn_in[...], full[:, cols])
        proj[:, cols] = out
        turned = rotate(rms_forward(out, head_gains[0:1, :]), cosine[...], sine[...])
        query[:, cols] = turned.astype(BF)


def queries_of(core, attn_in, peers, head_gains, cosine, sine):
    total, width = attn_in.shape
    return pl.pallas_call(
        functools.partial(query_kernel, len(peers)),
        out_shape=[
            jax.ShapeDtypeStruct((total, HQ * HD), F32),
            jax.ShapeDtypeStruct((total, HQ * HD), BF),
        ],
        in_specs=[SMEM] + [VMEM] * (len(peers) + 4),
        out_specs=[VMEM] * 2,
        scratch_shapes=[pltpu.VMEM((width, HQ * HD), BF)],
        compiler_params=PARAMS,
        cost_estimate=COST,
    )(core, attn_in, *peers, head_gains, cosine, sine)


GAIN_ROWS = 16


def gain_starts(width, size):
    return [min(start, width - size) for start in range(0, width, size)]


def last_kernel(n, core, *refs):
    q_peers, kv_peers = refs[:n], refs[n : 2 * n]
    (
        tokens, attn_in, grad_middle, grad_query, grad_kv, returned, key_proj, cosine, sine,
        gains, head_gains, norm_terms, head_terms, top_terms,
        grad_inputs, keep, send, gain_terms, q_full, kv_full,
    ) = refs[2 * n :]
    whole_rows(core, q_peers, q_full)
    whole_rows(core, kv_peers, kv_full)
    grads = grad_kv[...] + returned[...].astype(F32)
    normed = rotate(grads[:, :HD], cosine[...], -sine[...])
    d_key, key_terms = rms_backward(key_proj[...], head_gains[1:2, :], normed)
    low = jnp.concatenate([d_key.astype(BF), grads[:, HD:].astype(BF)], axis=1)
    size = keep.shape[1]
    narrow = attn_in.shape[1] // n
    turned = low.T
    for j in range(n):
        out = dot(turned, attn_in[:, window_of(core[0] ^ j, narrow, size)])
        target, row = (keep, j) if j < n // 2 else (send, j - n // 2)
        row = row * 2 * HD
        target[row : row + 2 * HD, :] = out.astype(target.dtype)
    d_in = dot_nt(grad_query[...], q_full[...]) + dot_nt(low, kv_full[...])
    d_tokens, in_terms = rms_backward(tokens[...].astype(F32), gains[0:1, :], d_in)
    grad_inputs[...] = grad_middle[...] + d_tokens
    gain_terms[...] = jnp.zeros_like(gain_terms)
    gain_terms[0:1, :] = jnp.sum(in_terms, axis=0, keepdims=True)
    gain_terms[1:3, :] = norm_terms[0:2, :]
    gain_terms[3:4, :] = top_terms[...]
    gain_terms[4:5, :HD] = head_terms[0:1, :]
    gain_terms[5:6, :HD] = jnp.sum(key_terms, axis=0, keepdims=True)


def last(core, q_peers, kv_peers, *rest):
    n = len(q_peers)
    total, width = rest[0].shape
    size = window_size(width, n)
    return pl.pallas_call(
        functools.partial(last_kernel, n),
        out_shape=[
            jax.ShapeDtypeStruct((total, width), F32),
            jax.ShapeDtypeStruct((n * HD, size), F32),
            jax.ShapeDtypeStruct((n * HD, size), BF),
            jax.ShapeDtypeStruct((GAIN_ROWS, width), F32),
        ],
        in_specs=[SMEM] + [VMEM] * (2 * n + len(rest)),
        out_specs=[VMEM] * 4,
        scratch_shapes=[pltpu.VMEM((width, HQ * HD), BF), pltpu.VMEM((width, 2 * HD), BF)],
        compiler_params=PARAMS,
        cost_estimate=COST,
    )(core, *q_peers, *kv_peers, *rest)


def tail_kernel(order, count, own, keep, got, gains, gains_got, out):
    me = own[0]
    size = keep.shape[1]
    block = keep.shape[0] // 2 // count
    places = places_of(order, True)
    part = len(places) // QUAD
    starts = gain_starts(gains.shape[1], size)
    rows = part * 2 * block + len(starts) * GAIN_ROWS
    summed = (gains[...] + gains_got[...]).astype(BF)
    for k, owner in enumerate(places):
        q, k = divmod(k, part)
        for half in range(2):
            source = pl.ds(pl.multiple_of((half * count + owner(me)) * block, 16), block)
            row = q * rows + (2 * k + half) * block
            out[row : row + block, :] = (keep[source, :] + got[source, :].astype(F32)).astype(BF)
    for q in range(QUAD):
        row = (q + 1) * rows - len(starts) * GAIN_ROWS
        for k, start in enumerate(starts):
            at = row + k * GAIN_ROWS
            out[at : at + GAIN_ROWS, :] = summed[:, start : start + size]


def tail_begin(own, order, count, keep, got, gains, gains_got):
    rows, size = keep.shape
    extra = len(gain_starts(gains.shape[1], size)) * GAIN_ROWS
    return pl.pallas_call(
        functools.partial(tail_kernel, order, count),
        out_shape=jax.ShapeDtypeStruct((rows + QUAD * extra, size), BF),
        in_specs=[SMEM] + [VMEM] * 4,
        out_specs=VMEM,
        compiler_params=PARAMS,
        cost_estimate=COST,
    )(own, keep, got, gains, gains_got)


def tail_step_kernel(ways, extra, final, *refs):
    parts, outs = refs[:ways], refs[ways:]
    total = sum(part[...].astype(F32) for part in parts)
    if final:
        outs[0][...] = total
        return
    low = total.astype(BF)
    body = low.shape[0] - extra
    half = body // 2
    send, keep = outs
    send[:half, :] = low[:half]
    keep[:half, :] = low[half:body]
    send[half:, :] = low[body:]
    keep[half:, :] = low[body:]


def tail_step(parts, extra, final):
    rows, size = parts[0].shape
    if final:
        shapes = [jax.ShapeDtypeStruct((rows, size), F32)]
    else:
        half = (rows - extra) // 2 + extra
        shapes = [jax.ShapeDtypeStruct((half, size), BF)] * 2
    return pl.pallas_call(
        functools.partial(tail_step_kernel, len(parts), extra, final),
        out_shape=shapes,
        in_specs=[VMEM] * len(parts),
        out_specs=[VMEM] * len(shapes),
        compiler_params=PARAMS,
        cost_estimate=COST,
    )(*parts)


def tail_end_kernel(core, kept, got, key_grad, value_grad, norm_total, head_total):
    total = kept[...].astype(F32) + got[...].astype(F32)
    rows, size = total.shape
    width = norm_total.shape[1]
    block, narrow = key_grad.shape
    starts = gain_starts(width, size)
    for k, target in enumerate((key_grad, value_grad)):
        rows_of = total[k * block : (k + 1) * block]
        start = narrow % 128
        target[...] = jnp.where(
            core[0] == 0, rows_of[:, :narrow], rows_of[:, start : start + narrow]
        )
    first = rows - len(starts) * GAIN_ROWS
    for k, begin in enumerate(starts):
        row = first + k * GAIN_ROWS
        norm_total[:, begin : begin + size] = total[row : row + 4]
    head_total[...] = total[first + 4 : first + 6, :HD]


def tail_end(core, width, block, parts):
    narrow, size = width // 2, parts[0].shape[1]
    return pl.pallas_call(
        tail_end_kernel,
        out_shape=[
            jax.ShapeDtypeStruct((block, narrow), F32),
            jax.ShapeDtypeStruct((block, narrow), F32),
            jax.ShapeDtypeStruct((4, width), F32),
            jax.ShapeDtypeStruct((2, HD), F32),
        ],
        in_specs=[SMEM, VMEM, VMEM],
        out_specs=[VMEM] * 4,
        compiler_params=PARAMS,
        cost_estimate=COST,
    )(core, *parts)


SCALE = HD ** (-0.5)


def pieces_of(lane, rows, hops, chunk, d):
    size = min(chunk, rows)
    for start in range(0, rows, size):
        row = lane * rows + start
        yield start, size, (row // chunk * hops + d - 1) * chunk + row % chunk


def keys_of(lane, rows, hops, chunk, earlier, kv_local, keys):
    for d in range(1, hops + 1):
        for start, size, source in pieces_of(lane, rows, hops, chunk, d):
            target = (hops - d) * rows + start
            keys[target : target + size, :] = earlier[source : source + size, :]
    keys[hops * rows :, :] = kv_local[lane * rows : (lane + 1) * rows, :]


def allowed_of(place, lengths, lane, rows, hops, window):
    first = place[0] * rows
    q_pos = first + lax.broadcasted_iota(jnp.int32, (rows, 1), 0)
    k_pos = first - hops * rows + lax.broadcasted_iota(jnp.int32, (1, (hops + 1) * rows), 1)
    q_id, k_id = jnp.zeros_like(q_pos), jnp.zeros_like(k_pos)
    end = jnp.int32(0)
    for j in range(lengths.shape[1]):
        end = end + lengths[lane, j]
        q_id = q_id + (end <= q_pos).astype(jnp.int32)
        k_id = k_id + (end <= k_pos).astype(jnp.int32)
    return (q_id == k_id) & (k_pos <= q_pos) & (q_pos - k_pos < window) & (k_pos >= 0)


def soft_of(query, keys, allowed):
    scores = jnp.where(allowed, dot_nt(query, keys) * SCALE, -1e30)
    grown = jnp.exp(scores - jnp.max(scores, axis=-1, keepdims=True))
    return grown * (1.0 / jnp.sum(grown, axis=-1, keepdims=True))


def attention_kernel(
    hops, chunk, place, lengths, query, kv_local, earlier, tokens, w_out, gains,
    mixed, branch, middle, ffn_in, keys,
):
    lanes = lengths.shape[0]
    rows = query.shape[0] // lanes
    for lane in range(lanes):
        span = slice(lane * rows, (lane + 1) * rows)
        keys_of(lane, rows, hops, chunk, earlier, kv_local, keys)
        allowed = allowed_of(place, lengths, lane, rows, hops, W)
        for h in range(HQ):
            cols = slice(h * HD, (h + 1) * HD)
            soft = soft_of(query[span, cols], keys[:, :HD], allowed)
            mixed[span, cols] = dot(soft.astype(BF), keys[:, HD:]).astype(BF)
        out = dot(mixed[span, :], w_out[...])
        branch[span, :] = out
        mid = tokens[span, :].astype(F32) + rms_forward(out, gains[1:2, :])
        middle[span, :] = mid
        ffn_in[span, :] = rms_forward(mid, gains[2:3, :]).astype(BF)


def attention(hops, chunk, place, lengths, query, kv_local, earlier, tokens, w_out, gains):
    total, width = tokens.shape
    lanes = lengths.shape[0]
    return pl.pallas_call(
        functools.partial(attention_kernel, hops, chunk),
        out_shape=[
            jax.ShapeDtypeStruct(query.shape, BF),
            jax.ShapeDtypeStruct((total, width), F32),
            jax.ShapeDtypeStruct((total, width), F32),
            jax.ShapeDtypeStruct((total, width), BF),
        ],
        in_specs=[SMEM, SMEM] + [VMEM] * 6,
        out_specs=[VMEM] * 4,
        scratch_shapes=[pltpu.VMEM(((hops + 1) * (total // lanes), 2 * HD), BF)],
        compiler_params=PARAMS,
        cost_estimate=COST,
    )(place, lengths, query, kv_local, earlier, tokens, w_out, gains)


def attention_back_kernel(
    hops, chunk, cores, core, place, lengths, query, kv_local, earlier, upstream, w_out, gains,
    head_gains, branch, middle, keep, got, query_proj, cosine, sine, late, grad_middle, grad_branch, grad_query, grad_kv, grad_earlier, norm_terms, head_terms,
    keys, d_mixed, raws, softs, queries, mixes,
):
    lanes = lengths.shape[0]
    rows = query.shape[0] // lanes
    width = upstream.shape[1]
    norm_terms[...] = jnp.zeros_like(norm_terms)
    head_terms[...] = jnp.zeros_like(head_terms)
    for lane in range(lanes):
        span = slice(lane * rows, (lane + 1) * rows)
        d_ffn_in = keep[span, :] + got[span, :].astype(F32)
        d_mid, ffn_terms = rms_backward(middle[span, :], gains[2:3, :], d_ffn_in)
        d_mid = d_mid + upstream[span, :].astype(F32)
        grad_middle[span, :] = d_mid
        d_branch, mid_terms = rms_backward(branch[span, :], gains[1:2, :], d_mid)
        norm_terms[0:1, :] += jnp.sum(mid_terms, axis=0, keepdims=True)
        norm_terms[1:2, :] += jnp.sum(ffn_terms, axis=0, keepdims=True)
        low = d_branch.astype(BF)
        grad_branch[span, :] = low
        if cores == 2:
            size = late.shape[1] - HQ * HD
            window = window_of(core[0] ^ 1, width // 2, size)
            late[span, HQ * HD :] = grad_branch[span, window]
        d_mixed[...] = dot_nt(low, w_out[...]).astype(BF)
        keys_of(lane, rows, hops, chunk, earlier, kv_local, keys)
        allowed = allowed_of(place, lengths, lane, rows, hops, W)
        cos, sin = cosine[span, :], sine[span, :]
        for h in range(HQ):
            cols = slice(h * HD, (h + 1) * HD)
            stack = slice(h * rows, (h + 1) * rows)
            soft = soft_of(query[span, cols], keys[:, :HD], allowed)
            d_soft = dot_nt(d_mixed[:, cols], keys[:, HD:])
            inner = jnp.sum(soft * d_soft, axis=-1, keepdims=True)
            raw = (soft * (d_soft - inner) * SCALE).astype(BF)
            raws[stack, :] = raw
            softs[stack, :] = soft.astype(BF)
            queries[stack, :] = query[span, cols]
            mixes[stack, :] = d_mixed[:, cols]
            normed = rotate(dot(raw, keys[:, :HD]), cos, -sin)
            d_query, terms = rms_backward(query_proj[span, cols], head_gains[0:1, :], normed)
            grad_query[span, cols] = d_query.astype(BF)
            if cores == 2:
                late[span, cols] = d_query.astype(BF)
            head_terms[0:1, :] += jnp.sum(terms, axis=0, keepdims=True)
        for part, (left, right) in enumerate(((raws, queries), (softs, mixes))):
            cols = slice(part * HD, (part + 1) * HD)
            out = dot_tn(left[...], right[...])
            for d in range(1, hops + 1):
                for start, size, target in pieces_of(lane, rows, hops, chunk, d):
                    source = (hops - d) * rows + start
                    grad_earlier[target : target + size, cols] = out[
                        source : source + size
                    ].astype(BF)
            grad_kv[span, cols] = out[hops * rows :]


def attention_back(
    hops, chunk, cores, core, place, lengths, query, kv_local, earlier, upstream, w_out, gains, head_gains,
    branch, middle, keep, got, query_proj, cosine, sine,
):
    total, width = upstream.shape
    lanes = lengths.shape[0]
    rows = total // lanes
    span = (hops + 1) * rows
    return pl.pallas_call(
        functools.partial(attention_back_kernel, hops, chunk, cores),
        out_shape=[
            jax.ShapeDtypeStruct((total, HQ * HD + window_size(width, cores)), BF),
            jax.ShapeDtypeStruct((total, width), F32),
            jax.ShapeDtypeStruct((total, width), BF),
            jax.ShapeDtypeStruct(query.shape, BF),
            jax.ShapeDtypeStruct(kv_local.shape, F32),
            jax.ShapeDtypeStruct(earlier.shape, BF),
            jax.ShapeDtypeStruct((8, width), F32),
            jax.ShapeDtypeStruct((8, HD), F32),
        ],
        in_specs=[SMEM] * 3 + [VMEM] * 14,
        out_specs=[VMEM] * 8,
        scratch_shapes=[
            pltpu.VMEM((span, 2 * HD), BF),
            pltpu.VMEM((rows, HQ * HD), BF),
            pltpu.VMEM((HQ * rows, span), BF),
            pltpu.VMEM((HQ * rows, span), BF),
            pltpu.VMEM((HQ * rows, HD), BF),
            pltpu.VMEM((HQ * rows, HD), BF),
        ],
        compiler_params=PARAMS,
        cost_estimate=COST,
    )(
        core, place, lengths, query, kv_local, earlier, upstream, w_out, gains, head_gains,
        branch, middle, keep, got, query_proj, cosine, sine,
    )


def shards(
    tokens,
    cotangent,
    lengths,
    deal_order,
    w_query,
    w_key,
    w_value,
    w_out,
    w_gate,
    w_up,
    w_down,
    norm_gains,
    head_gains,
):
    lanes, rows, width = tokens.shape[1:]
    total = lanes * rows
    seq_count = lax.axis_size("seq")
    cores = lax.axis_size("fsdp")
    own = lax.axis_index("seq")
    core = lax.axis_index("fsdp")
    window = W
    hops = (window - 1 + rows - 1) // rows
    chunk = total // seq_count

    deal = deal_order[0]
    places = jnp.arange(seq_count, dtype=jnp.int32)
    back = jnp.sum(jnp.where(deal[None, :] == places[:, None], places[None, :], 0), axis=1)
    place = deal[own]
    steps = jnp.arange(1, hops + 1, dtype=jnp.int32)
    wanted = deal[:, None] - steps[None, :]
    fetch_table = back[jnp.maximum(wanted, 0)].reshape(-1)
    readers = deal[:, None] + steps[None, :]
    reader_ok = (readers < seq_count).astype(jnp.int32).reshape(-1)
    reader_table = (
        back[jnp.minimum(readers, seq_count - 1)] * hops + (steps[None, :] - 1)
    ).reshape(-1)

    token_rows = tokens.reshape(total, width)
    upstream_rows = cotangent.reshape(total, width)
    q_width = HQ * HD
    narrow = width // cores
    core_ref, own_ref = core.reshape(1), own.reshape(1)

    def core_blocks(block):
        blocks = [block]
        for mask in masks(cores):
            together = jnp.concatenate(blocks, axis=0) if len(blocks) > 1 else blocks[0]
            got = swap(together, "fsdp", mask)
            size = block.shape[0]
            blocks = blocks + [got[j * size : (j + 1) * size] for j in range(len(blocks))]
        return blocks

    def core_sum(keep, send):
        steps = masks(cores)[::-1]
        for mask in steps:
            out = keep + swap(send, "fsdp", mask).astype(F32)
            half = out.shape[0] // 2
            keep, send = out[:half], out[half:].astype(BF)
        return out

    kv_peers = core_blocks(jnp.concatenate([w_key, w_value], axis=1))
    local_stream = place * rows + jnp.arange(rows, dtype=jnp.int32)
    positions = sequence_info(lengths[0], jnp.broadcast_to(local_stream, (lanes, rows)))[1]
    cosine, sine = rope_tables(positions.reshape(total), HD)
    attn_in, key_proj, kv_local = key_value(
        core_ref, token_rows, kv_peers, norm_gains, head_gains, cosine, sine
    )

    spread = lax.all_to_all(
        kv_local.reshape(seq_count, chunk, 2 * HD), "seq", 0, 0, tiled=True
    )
    picked = pick(fetch_table, spread).reshape(seq_count, hops * chunk, 2 * HD)
    arrived = lax.all_to_all(picked, "seq", 0, 0, tiled=True)
    run = chunk
    if chunk % 16:
        run = total
        arrived = arrived.reshape(seq_count, hops, chunk, 2 * HD).transpose(1, 0, 2, 3)
    earlier = arrived.reshape(hops * total, 2 * HD)

    w_query, w_out = lax.optimization_barrier((w_query, w_out, kv_local))[:2]
    query_peers = core_blocks(w_query)
    size = -(-narrow // 128) * 128
    peers_out = gather_cores(jnp.pad(w_out, ((0, 0), (0, size - narrow))))
    peers_out = flip(peers_out.reshape(cores, q_width, size), core)
    w_out_full = jnp.concatenate([peers_out[j, :, :narrow] for j in range(cores)], axis=1)
    query_proj, query_rot = queries_of(
        core_ref, attn_in, query_peers, head_gains, cosine, sine
    )

    size = window_size(width, cores)

    def peer_window(values):
        start = (core ^ 1) * narrow // 128 * 128
        return lax.dynamic_slice_in_dim(values, start, size, 1)

    hidden_cols = w_gate.shape[1]
    share = -(-hidden_cols // 256) * 128
    overlap = 2 * share - hidden_cols
    part = ((own & SPLIT_BIT) != 0).astype(jnp.int32)
    part_ref = part.reshape(1)
    if (hidden_cols - share) % 128:
        begin = part * (hidden_cols - share)
        w_gate = lax.dynamic_slice_in_dim(w_gate, begin, share, 1)
        w_up = lax.dynamic_slice_in_dim(w_up, begin, share, 1)
        w_down = lax.dynamic_slice_in_dim(w_down, begin, share, 0)

    earlier = after(earlier, query_rot, w_out_full)
    place_ref, lengths_ref = place.reshape(1), lengths[0]
    mixed_low, branch, middle, ffn_in = attention(
        hops, run, place_ref, lengths_ref, query_rot, kv_local, earlier, token_rows, w_out_full, norm_gains
    )

    if cores == 2:
        mixed_peer = swap(mixed_low, "fsdp", 1)
        attn_peer = swap(peer_window(attn_in), "fsdp", 1)
        early = (mixed_peer, attn_peer)
    else:
        early = ()

    def sum_group(near_part, far_part):
        got = swap(core_sum(*far_part).astype(BF), "seq", SPLIT_BIT)
        return core_sum(*near_part), got

    far_in = swap(ffn_in, "seq", SPLIT_BIT)
    near_all = core_blocks(ffn_in)
    near = ffn_forward(part_ref, near_all, w_gate, w_up, w_down, share, overlap)
    far_all = core_blocks(after(far_in, near[0], *early))
    far = ffn_forward(part_ref, far_all, w_gate, w_up, w_down, share, overlap)
    keep, got = sum_group(near[3:], far[3:])
    ffn_out = keep + got.astype(F32)
    result = middle + rms_forward(ffn_out, norm_gains[3])

    grad_ffn_out, top_terms = rms_backward(ffn_out, norm_gains[3], upstream_rows.astype(F32))
    top_terms = jnp.sum(top_terms, axis=0, keepdims=True)
    grad_low = grad_ffn_out.astype(BF)
    far_grad = swap(grad_low, "seq", SPLIT_BIT)
    near_grads = core_blocks(grad_low)
    near_back = ffn_backward(part_ref, near_grads, near[1], near[2], w_gate, w_up, w_down)
    far_grads = core_blocks(after(far_grad, near_back[0]))
    others = [m for m in masks(seq_count) if m != SPLIT_BIT]
    swapped, beyond = [others[1], others[0]] + others[2:], others[2:]

    def terms_of(left, right, *pieces):
        pieces = [(order + [SPLIT_BIT], size, quad) for order, size, quad in pieces]
        return weight_terms(own, seq_count, pieces, left, *right)

    tile, count = tiles(share)
    minor = max(1, count * 2 // 7) * tile
    outward_first = beyond[:1] + others[:2] + beyond[1:]

    down_terms = terms_of(
        near_grads + far_grads,
        (near[0], far[0]),
        (beyond, share - minor, True),
        (outward_first, minor, False),
    )
    down_b = Chain(*down_terms[1:], outward_first)
    down_quad = lax.all_to_all(
        down_terms[0], "seq", 0, 0, tiled=True, axis_index_groups=quads(seq_count)
    )
    far_grads[0] = after(far_grads[0], *down_terms)
    far_back = ffn_backward(part_ref, far_grads, far[1], far[2], w_gate, w_up, w_down)
    far_sum = core_sum(*far_back[2:]).astype(BF)
    got = swap(far_sum, "seq", SPLIT_BIT)
    keep = core_sum(*near_back[2:])

    gate_terms = terms_of(
        near_all + far_all, (near_back[0], after(far_back[0], far_sum)), (swapped, share, False)
    )
    up_terms = terms_of(
        near_all + far_all, (near_back[1], after(far_back[1], *gate_terms)), (others, share, False)
    )
    gate_c = Chain(*gate_terms, swapped)
    up_c = Chain(*up_terms, others)
    turns = Turns(up_terms[0])

    down_b.step(turns)
    down_first, down_rest = quad_sum(turns.wait(down_quad))
    turns.end(down_first)
    down_a = Chain(down_first, down_rest, beyond)

    (
        late, grad_middle, grad_branch_low, grad_query_low, grad_kv, grad_earlier, norm_terms,
        head_terms,
    ) = attention_back(
        hops, run, cores, core_ref, place_ref, lengths_ref, query_rot, kv_local, earlier, upstream_rows, w_out_full,
        norm_gains, head_gains, branch, middle, keep, turns.wait(got), query_proj, cosine, sine,
    )

    outward = grad_earlier
    if chunk % 16:
        outward = outward.reshape(hops, seq_count, chunk, 2 * HD).transpose(1, 0, 2, 3)
    outward = outward.reshape(seq_count, hops * chunk, 2 * HD)
    collected = lax.all_to_all(outward, "seq", 0, 0, tiled=True)

    turns.end(outward)
    every = swapped + [SPLIT_BIT]
    padded = width // seq_count
    if cores == 2:
        late = swap(late, "fsdp", 1)
        attention_terms = outer_pair(
            own_ref, core_ref, seq_count, every, padded, mixed_low, mixed_peer, grad_branch_low,
            grad_query_low, turns.wait(late), attn_in, attn_peer,
        )
    else:
        outer_keep, outer_send = outer_begin(
            core_ref, cores, mixed_low, grad_branch_low, turns.wait(grad_query_low), attn_in
        )
        outer_keep = core_sum(outer_keep, outer_send)
        outer_got = jnp.zeros(outer_keep.shape, BF)
        attention_terms = outer_end(own_ref, seq_count, every, outer_keep, outer_got, padded)
    turns.end(attention_terms[0])
    outer_c = Chain(*attention_terms, swapped)
    gate_c.step(turns)
    up_c.step(turns)
    down_b.step(turns)
    summed = pick_sum(
        hops,
        reader_table,
        reader_ok,
        turns.wait(collected).reshape(seq_count * hops, chunk, 2 * HD),
    )
    turns.end(summed)
    returned = lax.all_to_all(summed, "seq", 0, 0, tiled=True)
    while down_a.order:
        down_a.step(turns)
    gate_c.step(turns)
    up_c.step(turns)
    outer_c.step(turns)
    while down_b.order:
        down_b.step(turns)
    returned = turns.wait(returned)

    grad_inputs, kv_keep, kv_send, gain_terms = last(
        core_ref, query_peers, kv_peers, token_rows, attn_in, grad_middle, grad_query_low, grad_kv,
        returned.reshape(total, 2 * HD), key_proj, cosine, sine, norm_gains, head_gains, norm_terms,
        head_terms, top_terms,
    )
    kv_rows = HD // seq_count
    tail_order = beyond + [SPLIT_BIT]
    size = kv_keep.shape[1]
    starts = gain_starts(width, size)
    extra = len(starts) * GAIN_ROWS
    if cores == 2:
        kv_got, gains_got = swap(kv_send, "fsdp", 1), swap(gain_terms, "fsdp", 1)
    else:
        kv_keep = core_sum(kv_keep, kv_send)
        kv_got = jnp.zeros(kv_keep.shape, BF)
        for mask in masks(cores)[1:]:
            gain_terms = gain_terms + swap(gain_terms, "fsdp", mask)
        gains_got = swap(gain_terms, "fsdp", 1)
    if kv_rows % 16:
        gains = (gain_terms + gains_got).astype(BF)
        owners = jnp.stack([owner(own) for owner in places_of(tail_order, True)])
        tail = (kv_keep + kv_got.astype(F32)).astype(BF).reshape(2, seq_count, kv_rows, size)
        tail = jnp.take(tail, owners, axis=1, mode="clip").transpose(1, 0, 2, 3)
        tail = tail.reshape(QUAD, -1, size)
        gains = jnp.concatenate([gains[:, start : start + size] for start in starts], axis=0)
        gains = jnp.broadcast_to(gains, (QUAD,) + gains.shape)
        tail = jnp.concatenate([tail, gains], axis=1).reshape(-1, size)
    else:
        tail = tail_begin(own_ref, tail_order, seq_count, kv_keep, kv_got, gain_terms, gains_got)
    ended = lax.all_to_all(
        tail, "seq", 0, 0, tiled=True, axis_index_groups=quads(seq_count)
    )
    turns.end(tail)

    def exchanged(*chains):
        mine = jnp.concatenate([chain.total[1] for chain in chains], axis=1)
        sent = jnp.concatenate([chain.total[0].astype(BF) for chain in chains], axis=1)
        return mine, swap(sent, "seq", SPLIT_BIT)

    down_pair = exchanged(down_a, down_b)
    while gate_c.order:
        gate_c.step(turns)
    outer_c.step(turns)
    ended = turns.wait(ended).reshape(QUAD, -1, size)
    parts = [ended[q] for q in range(QUAD)]
    for mask in tail_order:
        sent, kept = tail_step(parts, extra, False)
        turns.end(sent)
        got = swap(sent, "seq", mask)
        if mask == tail_order[0]:
            while up_c.order:
                up_c.step(turns)
            gate_pair = exchanged(gate_c, up_c)
        if mask == tail_order[-1]:
            while outer_c.order:
                outer_c.step(turns)
            outer_mine, outer_got = exchanged(outer_c)
            pair_got = turns.wait(gate_pair[1])
            turns.end(pair_got)
        parts = [kept, turns.wait(got)]

    def own_columns(values):
        return lax.dynamic_slice_in_dim(values, core * narrow % 128, narrow, 1)

    if kv_rows % 16 or cores != 2:
        (ended,) = tail_step(parts, extra, True)
        key_grad = own_columns(ended[:kv_rows]).T
        value_grad = own_columns(ended[kv_rows : 2 * kv_rows]).T
        windows = ended[-extra:].reshape(len(starts), GAIN_ROWS, size)
        gains = jnp.concatenate(
            [windows[k][:, k * size - start :] for k, start in enumerate(starts)], axis=1
        )
        norm_total, head_total = gains[:4], gains[4:6, :HD]
    else:
        key_grad, value_grad, norm_total, head_total = tail_end(core_ref, width, kv_rows, parts)
        key_grad, value_grad = key_grad.T, value_grad.T

    mine, got = down_pair
    mine = jnp.concatenate([mine, gate_pair[0]], axis=1)
    got = jnp.concatenate([turns.wait(got), pair_got], axis=1).astype(F32)
    lower, upper = jnp.where(part == 0, mine, got), jnp.where(part == 0, got, mine)
    down_grad, gate_grad, up_grad = (
        jnp.concatenate(
            [
                lower[:, k * share : (k + 1) * share],
                upper[:, k * share + overlap : (k + 1) * share],
            ],
            axis=1,
        )
        for k in range(3)
    )
    down_grad = down_grad.T
    attention_grad = outer_mine + turns.wait(outer_got).astype(F32)
    query_rows = q_width // seq_count
    size = attention_grad.shape[1] // 2
    out_grad = own_columns(attention_grad[:query_rows, :size])
    query_grad = own_columns(attention_grad[:query_rows, size:]).T


    return (
        result.reshape(1, lanes, rows, width),
        grad_inputs.reshape(1, lanes, rows, width),
        query_grad,
        key_grad,
        value_grad,
        out_grad,
        gate_grad,
        up_grad,
        down_grad,
        norm_total,
        head_total,
    )


def solution(mesh):
    in_specs = (
        P("fsdp", None, "seq", None),
        P("fsdp", None, "seq", None),
        P("fsdp", None, None),
        P("fsdp", None),
        P("fsdp", None),
        P("fsdp", None),
        P("fsdp", None),
        P(None, "fsdp"),
        P(None, "fsdp"),
        P(None, "fsdp"),
        P("fsdp", None),
        P(),
        P(),
    )
    out_specs = (
        P("fsdp", None, "seq", None),
        P("fsdp", None, "seq", None),
        P("fsdp", "seq"),
        P("fsdp", "seq"),
        P("fsdp", "seq"),
        P("seq", "fsdp"),
        P("seq", "fsdp"),
        P("seq", "fsdp"),
        P("fsdp", "seq"),
        P(),
        P(),
    )
    return jax.shard_map(shards, mesh=mesh, in_specs=in_specs, out_specs=out_specs, check_vma=False)
```

```python
import functools
import math

import jax
import jax.numpy as jnp
from jax import lax
from jax.experimental import pallas as pl
from jax.experimental.pallas import tpu as pltpu
from jax.sharding import PartitionSpec as P

HQ = 4
HD = 256
W = 512
EPSILON = 1e-06
ROPE_BASE = 10000.0
SPLIT_BIT = 4

BF = jnp.bfloat16
F32 = jnp.float32


def swap(value, axis, mask):
    count = lax.axis_size(axis)
    return lax.ppermute(value, axis, [(i, i ^ mask) for i in range(count)])


def masks(count):
    return [1 << k for k in range(count.bit_length() - 1)]


def gather_cores(block):
    for mask in masks(lax.axis_size("fsdp")):
        block = jnp.concatenate([block, swap(block, "fsdp", mask)], axis=0)
    return block


def sum_cores(block):
    for mask in reversed(masks(lax.axis_size("fsdp"))):
        half = block.shape[0] // 2
        got = swap(block[half:].astype(BF), "fsdp", mask)
        block = block[:half].astype(F32) + got.astype(F32)
    return block


def flip(parts, index):
    count = parts.shape[0]
    for mask in masks(count):
        turned = jnp.stack([parts[j ^ mask] for j in range(count)])
        parts = jnp.where((index & mask) != 0, turned, parts)
    return parts


def rms_scale(values):
    return lax.rsqrt(jnp.mean(values * values, axis=-1, keepdims=True) + EPSILON)


def rms_forward(values, gain_vec):
    return values * rms_scale(values) * gain_vec


def rms_backward(values, gain_vec, grad_out):
    scale_rows = rms_scale(values)
    weighted = grad_out * gain_vec
    inner_mean = jnp.mean(weighted * values, axis=-1, keepdims=True)
    grad_in = scale_rows * weighted - values * (scale_rows * scale_rows * scale_rows) * inner_mean
    return (grad_in, grad_out * values * scale_rows)


def rope_tables(seq_pos, head_dim):
    half_dim = head_dim // 2
    frequency = jnp.exp(
        jnp.arange(half_dim, dtype=F32) * (-2.0 * math.log(ROPE_BASE) / head_dim)
    )
    angles = seq_pos.astype(F32)[..., None] * frequency
    return (jnp.cos(angles), jnp.sin(angles))


def rotate(values, cosine_table, sine_table):
    half_dim = values.shape[-1] // 2
    first_half = values[..., :half_dim]
    second_half = values[..., half_dim:]
    return jnp.concatenate(
        [
            first_half * cosine_table - second_half * sine_table,
            second_half * cosine_table + first_half * sine_table,
        ],
        axis=-1,
    )


def gelu_tanh(values):
    return jax.nn.gelu(values, approximate=True)


def sequence_info(lengths, stream_pos):
    seq_ends = jnp.cumsum(lengths, axis=-1)
    before = seq_ends[..., None, :] <= stream_pos[..., :, None]
    seq_ids = jnp.sum(before.astype(jnp.int32), axis=-1)
    starts = jnp.sum(jnp.where(before, lengths[..., None, :], 0), axis=-1)
    return (seq_ids, stream_pos - starts)


def dot(a, b):
    return jnp.dot(a, b, preferred_element_type=F32)


def dot_tn(a, b):
    return lax.dot_general(a, b, (((0,), (0,)), ((), ())), preferred_element_type=F32)


def dot_nt(a, b):
    return lax.dot_general(a, b, (((1,), (1,)), ((), ())), preferred_element_type=F32)


def pick(table, source):
    return jnp.take(source, table, axis=0, mode="clip")


def pick_sum(hops, table, valid, source):
    terms = jnp.take(source, table, axis=0, mode="clip").astype(F32) * valid.astype(F32)[:, None, None]
    count = table.shape[0] // hops
    return jnp.sum(terms.reshape((count, hops) + source.shape[1:]), axis=1).astype(source.dtype)


QUAD = 4


def quads(count):
    return [[base + q for q in range(QUAD)] for base in range(0, count, QUAD)]


def quad_arrangement(order):
    return [(q, j) for q in range(QUAD) for j in arrangement(order)]


def places_of(order, quad):
    if quad:
        return [lambda me, q=q, j=j: ((me & ~(QUAD - 1)) ^ j) + q for q, j in quad_arrangement(order)]
    return [lambda me, j=j: me ^ j for j in arrangement(order)]


def arrangement(order):
    if not order:
        return [0]
    rest = arrangement(order[1:])
    return [j | order[0] for j in rest] + rest


def after(value, *others):
    return lax.optimization_barrier((value,) + others)[0]


class Turns:
    def __init__(self, token):
        self.token = token

    def wait(self, value):
        return after(value, self.token)

    def end(self, token):
        self.token = token


def step_kernel(rest, got, *outs):
    count = rest.shape[0]
    for k in range(count):
        total = rest[k].astype(F32) + got[k].astype(F32)
        top, row = divmod(k, outs[0].shape[0])
        outs[top][row] = total.astype(outs[top].dtype)


def step_of(rest, got, final):
    count = rest.shape[0]
    parts, kind = (1, F32) if final else (2, BF)
    shape = jax.ShapeDtypeStruct((count // parts,) + rest.shape[1:], kind)
    return pl.pallas_call(
        step_kernel,
        out_shape=[shape] * parts,
        in_specs=[VMEM] * 2,
        out_specs=[VMEM] * parts,
        compiler_params=PARAMS,
        cost_estimate=COST,
    )(rest, got)


def quad_kernel(got, *outs):
    count = got.shape[0] // QUAD
    for k in range(count):
        total = sum(got[q * count + k].astype(F32) for q in range(QUAD))
        top, row = divmod(k, outs[0].shape[0])
        outs[top][row] = total.astype(BF)


def quad_sum(got):
    shape = jax.ShapeDtypeStruct((got.shape[0] // QUAD // 2,) + got.shape[1:], BF)
    return pl.pallas_call(
        quad_kernel,
        out_shape=[shape] * 2,
        in_specs=[VMEM],
        out_specs=[VMEM] * 2,
        compiler_params=PARAMS,
        cost_estimate=COST,
    )(got)


class Chain:
    def __init__(self, first, rest, order):
        self.rest, self.order = rest, list(order)
        self.got = swap(first, "seq", self.order[0])

    def step(self, turns):
        got = turns.wait(self.got)
        self.order.pop(0)
        if self.order:
            first, self.rest = step_of(self.rest, got, False)
            self.got = swap(first, "seq", self.order[0])
            turns.end(first)
        else:
            (self.total,) = step_of(self.rest, got, True)
            turns.end(self.total)


def tiles(size):
    tile = 256 if size % 256 == 0 else 128
    return tile, size // tile


def column_tiles(size):
    return [(start, min(256, size - start)) for start in range(0, size, 256)]


COST = pl.CostEstimate(flops=1024, bytes_accessed=1024, transcendentals=0)
VMEM = pl.BlockSpec(memory_space=pltpu.VMEM)
SMEM = pl.BlockSpec(memory_space=pltpu.SMEM)
PARAMS = pltpu.CompilerParams(vmem_limit_bytes=56 * 1024 * 1024)
ROOT = math.sqrt(2.0 / math.pi)
CUBE = 0.044715


def ffn_forward_kernel(n, overlap, *refs):
    part, x_refs, (wg, wu, wd) = refs[0], refs[1 : n + 1], refs[n + 1 : n + 4]
    hid_out, act_out, slope_out, keep, send = refs[n + 4 : n + 9]
    x_all, wg_all, wu_all, wd_all, gate, hid, act, slope, load, store = refs[n + 9 :]
    rows = x_refs[0].shape[0]
    share = hid.shape[1]
    tile, count = tiles(share)
    begin = pl.multiple_of(part[0] * (wg.shape[1] - share), 128)
    down_begin = pl.multiple_of(part[0] * (wd.shape[0] - share), 16)
    loads = [
        pltpu.make_async_copy(wg.at[:, pl.ds(begin, share)], wg_all, load.at[0]),
        pltpu.make_async_copy(wu.at[:, pl.ds(begin, share)], wu_all, load.at[1]),
        pltpu.make_async_copy(wd.at[pl.ds(down_begin, share), :], wd_all, load.at[2]),
    ]
    for copy in loads:
        copy.start()
    for j in range(n):
        x_all[j * rows : (j + 1) * rows, :] = x_refs[j][...]
    parts = [slice(i * tile, (i + 1) * tile) for i in range(count)]
    loads[0].wait()
    for cols in parts:
        gate[:, cols] = dot(x_all[...], wg_all[:, cols])
    loads[1].wait()
    for i, cols in enumerate(parts):
        g, u = gate[:, cols], dot(x_all[...], wu_all[:, cols])
        square = g * g
        t = jnp.tanh(g * (ROOT + ROOT * CUBE * square))
        half = 0.5 * (1.0 + t)
        a = g * half
        d = half + a * (1.0 - t) * (ROOT + 3.0 * ROOT * CUBE * square)
        if i * tile < overlap:
            index = i * tile + lax.broadcasted_iota(jnp.int32, a.shape, 1)
            counted = index >= part[0] * overlap
            a, u = jnp.where(counted, a, 0.0), jnp.where(counted, u, 0.0)
        hid[:, cols] = (a * u).astype(BF)
        act[:, cols] = a.astype(BF)
        slope[:, cols] = (u * d).astype(BF)
    stores = [
        pltpu.make_async_copy(hid, hid_out, store.at[0]),
        pltpu.make_async_copy(act, act_out, store.at[1]),
        pltpu.make_async_copy(slope, slope_out, store.at[2]),
    ]
    for copy in stores:
        copy.start()
    loads[2].wait()
    for start, size in column_tiles(wd.shape[1]):
        out = dot(hid[...], wd_all[:, start : start + size])
        half = out.shape[0] // 2
        keep[:, start : start + size] = out[:half]
        send[:, start : start + size] = out[half:].astype(BF)
    for copy in stores:
        copy.wait()


ANY = pl.BlockSpec(memory_space=pl.ANY)


def ffn_forward(part, blocks, wg, wu, wd, share, overlap):
    n, (rows, width) = len(blocks), blocks[0].shape
    total = n * rows
    return pl.pallas_call(
        functools.partial(ffn_forward_kernel, n, overlap),
        out_shape=[jax.ShapeDtypeStruct((total, share), BF)] * 3
        + [
            jax.ShapeDtypeStruct((total // 2, width), F32),
            jax.ShapeDtypeStruct((total // 2, width), BF),
        ],
        in_specs=[SMEM] + [VMEM] * n + [ANY] * 3,
        out_specs=[ANY] * 3 + [VMEM] * 2,
        scratch_shapes=[pltpu.VMEM((total, width), BF)]
        + [pltpu.VMEM((width, share), BF)] * 2
        + [pltpu.VMEM((share, width), BF)]
        + [pltpu.VMEM((total, share), F32)]
        + [pltpu.VMEM((total, share), BF)] * 3
        + [pltpu.SemaphoreType.DMA((3,))] * 2,
        compiler_params=PARAMS,
        cost_estimate=COST,
    )(part, *blocks, wg, wu, wd)


def ffn_backward_kernel(n, *refs):
    part, g_refs, (act, slope, wg, wu, wd) = refs[0], refs[1 : n + 1], refs[n + 1 : n + 6]
    gate_out, up_out, keep, send = refs[n + 6 : n + 10]
    g_all, act_all, slope_all, wg_all, wu_all, wd_all, d_gate, d_up, load, store = refs[n + 10 :]
    rows = g_refs[0].shape[0]
    share = d_gate.shape[1]
    tile, count = tiles(share)
    down_begin = pl.multiple_of(part[0] * (wd.shape[0] - share), 16)
    begin = pl.multiple_of(part[0] * (wg.shape[1] - share), 128)
    loads = [
        pltpu.make_async_copy(wd.at[pl.ds(down_begin, share), :], wd_all, load.at[0]),
        pltpu.make_async_copy(act, act_all, load.at[1]),
        pltpu.make_async_copy(slope, slope_all, load.at[2]),
        pltpu.make_async_copy(wg.at[:, pl.ds(begin, share)], wg_all, load.at[3]),
        pltpu.make_async_copy(wu.at[:, pl.ds(begin, share)], wu_all, load.at[4]),
    ]
    for copy in loads:
        copy.start()
    for j in range(n):
        g_all[j * rows : (j + 1) * rows, :] = g_refs[j][...]
    for copy in loads[:3]:
        copy.wait()
    for i in range(count):
        cols = slice(i * tile, (i + 1) * tile)
        d = dot_nt(g_all[...], wd_all[cols, :])
        d_gate[:, cols] = (d * slope_all[:, cols].astype(F32)).astype(BF)
        d_up[:, cols] = (d * act_all[:, cols].astype(F32)).astype(BF)
    stores = [
        pltpu.make_async_copy(d_gate, gate_out, store.at[0]),
        pltpu.make_async_copy(d_up, up_out, store.at[1]),
    ]
    for copy in stores:
        copy.start()
    for copy in loads[3:]:
        copy.wait()
    for start, size in column_tiles(wg.shape[0]):
        out = dot_nt(d_gate[...], wg_all[start : start + size, :])
        out = out + dot_nt(d_up[...], wu_all[start : start + size, :])
        half = out.shape[0] // 2
        keep[:, start : start + size] = out[:half]
        send[:, start : start + size] = out[half:].astype(BF)
    for copy in stores:
        copy.wait()


def ffn_backward(part, blocks, act, slope, wg, wu, wd):
    n, (rows, width), share = len(blocks), blocks[0].shape, act.shape[1]
    total = n * rows
    return pl.pallas_call(
        functools.partial(ffn_backward_kernel, n),
        out_shape=[jax.ShapeDtypeStruct((total, share), BF)] * 2
        + [
            jax.ShapeDtypeStruct((total // 2, width), F32),
            jax.ShapeDtypeStruct((total // 2, width), BF),
        ],
        in_specs=[SMEM] + [VMEM] * n + [ANY] * 5,
        out_specs=[ANY] * 2 + [VMEM] * 2,
        scratch_shapes=[pltpu.VMEM((total, width), BF)]
        + [pltpu.VMEM((total, share), BF)] * 2
        + [pltpu.VMEM((width, share), BF)] * 2
        + [pltpu.VMEM((share, width), BF)]
        + [pltpu.VMEM((total, share), BF)] * 2
        + [pltpu.SemaphoreType.DMA((5,)), pltpu.SemaphoreType.DMA((2,))],
        compiler_params=PARAMS,
        cost_estimate=COST,
    )(part, *blocks, act, slope, wg, wu, wd)


def weight_kernel(n, pieces, *refs):
    own, left = refs[0], refs[1 : n + 1]
    outs, (turned, out, right, load) = refs[n + 3 : -4], refs[-4:]
    rows = left[0].shape[0]
    tile, count = tiles(right.shape[1])
    half = right.shape[0] // 2

    def copies(i):
        cols = pl.ds(pl.multiple_of(i * tile, tile), tile)
        return [
            pltpu.make_async_copy(
                refs[n + 1 + k].at[:, cols], right.at[k * half : (k + 1) * half, cols], load.at[k, i]
            )
            for k in range(2)
        ]

    for i in range(count):
        for copy in copies(i):
            copy.start()
    for j in range(n):
        turned[:, j * rows : (j + 1) * rows] = left[j][...].T
    me = own[0]
    begin = 0
    for order, size, quad in pieces:
        halves, outs = (outs[:1], outs[1:]) if quad else (outs[:2], outs[2:])
        block = halves[0].shape[1]

        @pl.loop(0, size // tile)
        def _(i):
            cols = pl.ds(pl.multiple_of(begin + i * tile, tile), tile)
            into = pl.ds(pl.multiple_of(i * tile, tile), tile)
            for copy in copies(begin // tile + i):
                copy.wait()
            out[...] = dot(turned[...], right[:, cols])
            for k, owner in enumerate(places_of(order, quad)):
                source = pl.multiple_of(owner(me) * block, 8)
                top, k = divmod(k, halves[0].shape[0])
                halves[top][k, :, into] = out[pl.ds(source, block), :].astype(BF)

        begin = begin + size


def weight_terms(own, seq_count, pieces, left, near, far):
    width, share = left[0].shape[1], near.shape[1]
    block = width // seq_count
    half = seq_count // 2
    n = len(left)
    if block % 8:
        full = dot_tn(jnp.concatenate(left), jnp.concatenate([near, far])).astype(BF)
        full = full.reshape(seq_count, block, share)
        outs, begin = [], 0
        for order, size, quad in pieces:
            piece = full[:, :, begin : begin + size]
            owners = jnp.stack([owner(own) for owner in places_of(order, quad)])
            piece = jnp.take(piece, owners, axis=0, mode="clip")
            outs += [piece] if quad else [piece[:half], piece[half:]]
            begin += size
        return outs
    tile, _ = tiles(share)
    return pl.pallas_call(
        functools.partial(weight_kernel, n, pieces),
        out_shape=[
            jax.ShapeDtypeStruct((seq_count if quad else half, block, size), BF)
            for _, size, quad in pieces
            for _ in range(1 if quad else 2)
        ],
        in_specs=[SMEM] + [VMEM] * n + [ANY] * 2,
        out_specs=[VMEM] * sum(1 if quad else 2 for _, _, quad in pieces),
        scratch_shapes=[
            pltpu.VMEM((width, n * left[0].shape[0]), BF),
            pltpu.VMEM((width, tile), F32),
            pltpu.VMEM((n * left[0].shape[0], share), BF),
            pltpu.SemaphoreType.DMA((2, share // tile)),
        ],
        compiler_params=PARAMS,
        cost_estimate=COST,
    )(own.reshape(1), *left, near, far)


def window_size(width, cores):
    narrow = width // cores
    return max(-(-((c * narrow) % 128 + narrow) // 128) for c in range(cores)) * 128


def window_of(core, narrow, size):
    return pl.ds(pl.multiple_of(core * narrow // 128 * 128, 128), size)


def outer_kernel(cores, core, mixed, branch, query, attn_in, keep, send):
    size = keep.shape[1]
    split = mixed.shape[1]
    narrow = branch.shape[1] // cores
    for part, (left, right) in enumerate(((mixed, branch), (query, attn_in))):
        turned = left[...].T
        for j in range(cores):
            out = dot(turned, right[:, window_of(core[0] ^ j, narrow, size)])
            target, row = (keep, j) if j < cores // 2 else (send, j - cores // 2)
            row = (2 * row + part) * split
            target[row : row + split, :] = out.astype(target.dtype)


def outer_sum_kernel(order, own, keep, got, first, rest):
    me = own[0]
    half, padded, two = first.shape
    size = two // 2
    width = keep.shape[0] // 2
    block = width // (2 * half)
    for k, j in enumerate(arrangement(order)):
        target = first if k < half else rest
        for part in range(2):
            source = pl.ds(pl.multiple_of(part * width + (me ^ j) * block, 16), block)
            total = keep[source, :] + got[source, :].astype(F32)
            total = jnp.concatenate([total, jnp.zeros((padded - block, size), F32)], axis=0)
            target[k % half, :, part * size : (part + 1) * size] = total.astype(BF)


def outer_begin(core, cores, mixed, branch, query, attn_in):
    width = mixed.shape[1]
    size = window_size(branch.shape[1], cores)
    return pl.pallas_call(
        functools.partial(outer_kernel, cores),
        out_shape=[
            jax.ShapeDtypeStruct((cores * width, size), F32),
            jax.ShapeDtypeStruct((cores * width, size), BF),
        ],
        in_specs=[SMEM] + [VMEM] * 4,
        out_specs=[VMEM] * 2,
        compiler_params=PARAMS,
        cost_estimate=COST,
    )(core, mixed, branch, query, attn_in)


def outer_end(own, seq_count, order, keep, got, padded):
    total, size = keep.shape
    half = seq_count // 2
    return pl.pallas_call(
        functools.partial(outer_sum_kernel, order),
        out_shape=[jax.ShapeDtypeStruct((half, padded, 2 * size), BF)] * 2,
        in_specs=[SMEM, VMEM, VMEM],
        out_specs=[VMEM] * 2,
        compiler_params=PARAMS,
        cost_estimate=COST,
    )(own, keep, got)


def outer_pair_kernel(
    order, own, core, mixed, mixed_peer, branch, query, late, attn_in, attn_peer,
    first, rest, left, right, total,
):
    me = own[0]
    half, padded, two = first.shape
    size = two // 2
    rows, width = mixed.shape
    block = width // (2 * half)
    window = window_of(core[0], branch.shape[1] // 2, size)
    for part, (mine, peer, other, other_peer) in enumerate(
        (
            (mixed, mixed_peer, branch, late[:, width:]),
            (query, late.at[:, :width], attn_in, attn_peer[...]),
        )
    ):
        left[:rows, :] = mine[...]
        left[rows:, :] = peer[...]
        right[:rows, :] = other[:, window]
        right[rows:, :] = other_peer
        total[part] = dot_tn(left[...], right[...])
        for k, j in enumerate(arrangement(order)):
            target = first if k < half else rest
            value = total[part, pl.ds(pl.multiple_of((me ^ j) * block, 16), block), :]
            value = jnp.concatenate([value, jnp.zeros((padded - block, size), F32)], axis=0)
            target[k % half, :, part * size : (part + 1) * size] = value.astype(BF)


def outer_pair(own, core, seq_count, order, padded, mixed, *rest):
    rows, width = mixed.shape
    size = rest[-1].shape[1]
    half = seq_count // 2
    return pl.pallas_call(
        functools.partial(outer_pair_kernel, order),
        out_shape=[jax.ShapeDtypeStruct((half, padded, 2 * size), BF)] * 2,
        in_specs=[SMEM, SMEM] + [VMEM] * (1 + len(rest)),
        out_specs=[VMEM] * 2,
        scratch_shapes=[
            pltpu.VMEM((2 * rows, width), BF),
            pltpu.VMEM((2 * rows, size), BF),
            pltpu.VMEM((2, width, size), F32),
        ],
        compiler_params=PARAMS,
        cost_estimate=COST,
    )(own, core, mixed, *rest)


def whole_rows(core, peers, full):
    for j, peer in enumerate(peers):
        rows = peer.shape[0]
        full[pl.ds(pl.multiple_of((core[0] ^ j) * rows, 16), rows), :] = peer[...]


def angle_kernel(rows, own, deal, lengths, frequency, angles):
    place = deal[own[0]] * rows + lax.broadcasted_iota(jnp.int32, (rows, 1), 0)
    for lane in range(lengths.shape[0]):
        start, end = jnp.zeros_like(place), jnp.int32(0)
        for j in range(lengths.shape[1]):
            end = end + lengths[lane, j]
            start = start + jnp.where(end <= place, lengths[lane, j], 0)
        angles[lane * rows : (lane + 1) * rows, :] = (place - start).astype(F32) * frequency[...]


def angles_of(own, deal, lengths, rows):
    half = HD // 2
    frequency = jnp.exp(jnp.arange(half, dtype=F32) * (-2.0 * math.log(ROPE_BASE) / HD))
    return pl.pallas_call(
        functools.partial(angle_kernel, rows),
        out_shape=jax.ShapeDtypeStruct((lengths.shape[0] * rows, half), F32),
        in_specs=[SMEM] * 3 + [VMEM],
        out_specs=VMEM,
        compiler_params=PARAMS,
        cost_estimate=COST,
    )(own, deal, lengths, frequency.reshape(1, half))


def key_value_kernel(n, core, tokens, *refs):
    peers, (gains, head_gains, cosine, sine) = refs[:n], refs[n : n + 4]
    attn_in, key_proj, kv_local, full = refs[n + 4 :]
    whole_rows(core, peers, full)
    normed = rms_forward(tokens[...].astype(F32), gains[0:1, :]).astype(BF)
    attn_in[...] = normed
    both = dot(normed, full[...])
    keys = both[:, :HD]
    key_proj[...] = keys
    turned = rotate(rms_forward(keys, head_gains[1:2, :]), cosine[...], sine[...])
    kv_local[:, :HD] = turned.astype(BF)
    kv_local[:, HD:] = both[:, HD:].astype(BF)


def key_value(core, tokens, peers, gains, head_gains, cosine, sine):
    total, width = tokens.shape
    return pl.pallas_call(
        functools.partial(key_value_kernel, len(peers)),
        out_shape=[
            jax.ShapeDtypeStruct((total, width), BF),
            jax.ShapeDtypeStruct((total, HD), F32),
            jax.ShapeDtypeStruct((total, 2 * HD), BF),
        ],
        in_specs=[SMEM] + [VMEM] * (len(peers) + 5),
        out_specs=[VMEM] * 3,
        scratch_shapes=[pltpu.VMEM((width, 2 * HD), BF)],
        compiler_params=PARAMS,
        cost_estimate=COST,
    )(core, tokens, *peers, gains, head_gains, cosine, sine)


def query_kernel(n, core, attn_in, *refs):
    peers, (head_gains, cosine, sine, proj, query, full) = refs[:n], refs[n:]
    whole_rows(core, peers, full)
    for h in range(HQ):
        cols = slice(h * HD, (h + 1) * HD)
        out = dot(attn_in[...], full[:, cols])
        proj[:, cols] = out
        turned = rotate(rms_forward(out, head_gains[0:1, :]), cosine[...], sine[...])
        query[:, cols] = turned.astype(BF)


def queries_of(core, attn_in, peers, head_gains, cosine, sine):
    total, width = attn_in.shape
    return pl.pallas_call(
        functools.partial(query_kernel, len(peers)),
        out_shape=[
            jax.ShapeDtypeStruct((total, HQ * HD), F32),
            jax.ShapeDtypeStruct((total, HQ * HD), BF),
        ],
        in_specs=[SMEM] + [VMEM] * (len(peers) + 4),
        out_specs=[VMEM] * 2,
        scratch_shapes=[pltpu.VMEM((width, HQ * HD), BF)],
        compiler_params=PARAMS,
        cost_estimate=COST,
    )(core, attn_in, *peers, head_gains, cosine, sine)


GAIN_ROWS = 16


def gain_starts(width, size):
    return [min(start, width - size) for start in range(0, width, size)]


def last_kernel(n, core, *refs):
    q_peers, kv_peers = refs[:n], refs[n : 2 * n]
    (
        tokens, attn_in, grad_middle, grad_query, grad_kv, returned, key_proj, cosine, sine,
        gains, head_gains, norm_terms, head_terms, top_terms,
        grad_inputs, keep, send, gain_terms, q_full, kv_full,
    ) = refs[2 * n :]
    whole_rows(core, q_peers, q_full)
    whole_rows(core, kv_peers, kv_full)
    grads = grad_kv[...] + returned[...].astype(F32)
    normed = rotate(grads[:, :HD], cosine[...], -sine[...])
    d_key, key_terms = rms_backward(key_proj[...], head_gains[1:2, :], normed)
    low = jnp.concatenate([d_key.astype(BF), grads[:, HD:].astype(BF)], axis=1)
    size = keep.shape[1]
    narrow = attn_in.shape[1] // n
    turned = low.T
    for j in range(n):
        out = dot(turned, attn_in[:, window_of(core[0] ^ j, narrow, size)])
        target, row = (keep, j) if j < n // 2 else (send, j - n // 2)
        row = row * 2 * HD
        target[row : row + 2 * HD, :] = out.astype(target.dtype)
    d_in = dot_nt(grad_query[...], q_full[...]) + dot_nt(low, kv_full[...])
    d_tokens, in_terms = rms_backward(tokens[...].astype(F32), gains[0:1, :], d_in)
    grad_inputs[...] = grad_middle[...] + d_tokens
    gain_terms[...] = jnp.zeros_like(gain_terms)
    gain_terms[0:1, :] = jnp.sum(in_terms, axis=0, keepdims=True)
    gain_terms[1:3, :] = norm_terms[0:2, :]
    gain_terms[3:4, :] = top_terms[...]
    gain_terms[4:5, :HD] = head_terms[0:1, :]
    gain_terms[5:6, :HD] = jnp.sum(key_terms, axis=0, keepdims=True)


def last(core, q_peers, kv_peers, *rest):
    n = len(q_peers)
    total, width = rest[0].shape
    size = window_size(width, n)
    return pl.pallas_call(
        functools.partial(last_kernel, n),
        out_shape=[
            jax.ShapeDtypeStruct((total, width), F32),
            jax.ShapeDtypeStruct((n * HD, size), F32),
            jax.ShapeDtypeStruct((n * HD, size), BF),
            jax.ShapeDtypeStruct((GAIN_ROWS, width), F32),
        ],
        in_specs=[SMEM] + [VMEM] * (2 * n + len(rest)),
        out_specs=[VMEM] * 4,
        scratch_shapes=[pltpu.VMEM((width, HQ * HD), BF), pltpu.VMEM((width, 2 * HD), BF)],
        compiler_params=PARAMS,
        cost_estimate=COST,
    )(core, *q_peers, *kv_peers, *rest)


def tail_kernel(order, count, own, keep, got, gains, gains_got, out):
    me = own[0]
    size = keep.shape[1]
    block = keep.shape[0] // 2 // count
    places = places_of(order, True)
    part = len(places) // QUAD
    starts = gain_starts(gains.shape[1], size)
    rows = part * 2 * block + len(starts) * GAIN_ROWS
    summed = (gains[...] + gains_got[...]).astype(BF)
    for k, owner in enumerate(places):
        q, k = divmod(k, part)
        for half in range(2):
            source = pl.ds(pl.multiple_of((half * count + owner(me)) * block, 16), block)
            row = q * rows + (2 * k + half) * block
            out[row : row + block, :] = (keep[source, :] + got[source, :].astype(F32)).astype(BF)
    for q in range(QUAD):
        row = (q + 1) * rows - len(starts) * GAIN_ROWS
        for k, start in enumerate(starts):
            at = row + k * GAIN_ROWS
            out[at : at + GAIN_ROWS, :] = summed[:, start : start + size]


def tail_begin(own, order, count, keep, got, gains, gains_got):
    rows, size = keep.shape
    extra = len(gain_starts(gains.shape[1], size)) * GAIN_ROWS
    return pl.pallas_call(
        functools.partial(tail_kernel, order, count),
        out_shape=jax.ShapeDtypeStruct((rows + QUAD * extra, size), BF),
        in_specs=[SMEM] + [VMEM] * 4,
        out_specs=VMEM,
        compiler_params=PARAMS,
        cost_estimate=COST,
    )(own, keep, got, gains, gains_got)


def tail_step_kernel(ways, extra, final, *refs):
    parts, outs = refs[:ways], refs[ways:]
    total = sum(part[...].astype(F32) for part in parts)
    if final:
        outs[0][...] = total
        return
    low = total.astype(BF)
    body = low.shape[0] - extra
    half = body // 2
    send, keep = outs
    send[:half, :] = low[:half]
    keep[:half, :] = low[half:body]
    send[half:, :] = low[body:]
    keep[half:, :] = low[body:]


def tail_step(parts, extra, final):
    rows, size = parts[0].shape
    if final:
        shapes = [jax.ShapeDtypeStruct((rows, size), F32)]
    else:
        half = (rows - extra) // 2 + extra
        shapes = [jax.ShapeDtypeStruct((half, size), BF)] * 2
    return pl.pallas_call(
        functools.partial(tail_step_kernel, len(parts), extra, final),
        out_shape=shapes,
        in_specs=[VMEM] * len(parts),
        out_specs=[VMEM] * len(shapes),
        compiler_params=PARAMS,
        cost_estimate=COST,
    )(*parts)


def tail_end_kernel(core, kept, got, key_grad, value_grad, norm_total, head_total):
    total = kept[...].astype(F32) + got[...].astype(F32)
    rows, size = total.shape
    width = norm_total.shape[1]
    block, narrow = key_grad.shape
    starts = gain_starts(width, size)
    for k, target in enumerate((key_grad, value_grad)):
        rows_of = total[k * block : (k + 1) * block]
        start = narrow % 128
        target[...] = jnp.where(
            core[0] == 0, rows_of[:, :narrow], rows_of[:, start : start + narrow]
        )
    first = rows - len(starts) * GAIN_ROWS
    for k, begin in enumerate(starts):
        row = first + k * GAIN_ROWS
        norm_total[:, begin : begin + size] = total[row : row + 4]
    head_total[...] = total[first + 4 : first + 6, :HD]


def tail_end(core, width, block, parts):
    narrow, size = width // 2, parts[0].shape[1]
    return pl.pallas_call(
        tail_end_kernel,
        out_shape=[
            jax.ShapeDtypeStruct((block, narrow), F32),
            jax.ShapeDtypeStruct((block, narrow), F32),
            jax.ShapeDtypeStruct((4, width), F32),
            jax.ShapeDtypeStruct((2, HD), F32),
        ],
        in_specs=[SMEM, VMEM, VMEM],
        out_specs=[VMEM] * 4,
        compiler_params=PARAMS,
        cost_estimate=COST,
    )(core, *parts)


SCALE = HD ** (-0.5)


def pieces_of(lane, rows, hops, chunk, d):
    size = min(chunk, rows)
    for start in range(0, rows, size):
        row = lane * rows + start
        yield start, size, (row // chunk * hops + d - 1) * chunk + row % chunk


def keys_of(lane, rows, hops, chunk, earlier, kv_local, keys):
    for d in range(1, hops + 1):
        for start, size, source in pieces_of(lane, rows, hops, chunk, d):
            target = (hops - d) * rows + start
            keys[target : target + size, :] = earlier[source : source + size, :]
    keys[hops * rows :, :] = kv_local[lane * rows : (lane + 1) * rows, :]


def allowed_of(place, lengths, lane, rows, hops, window):
    first = place[0] * rows
    q_pos = first + lax.broadcasted_iota(jnp.int32, (rows, 1), 0)
    k_pos = first - hops * rows + lax.broadcasted_iota(jnp.int32, (1, (hops + 1) * rows), 1)
    q_id, k_id = jnp.zeros_like(q_pos), jnp.zeros_like(k_pos)
    end = jnp.int32(0)
    for j in range(lengths.shape[1]):
        end = end + lengths[lane, j]
        q_id = q_id + (end <= q_pos).astype(jnp.int32)
        k_id = k_id + (end <= k_pos).astype(jnp.int32)
    return (q_id == k_id) & (k_pos <= q_pos) & (q_pos - k_pos < window) & (k_pos >= 0)


def soft_of(query, keys, allowed):
    scores = jnp.where(allowed, dot_nt(query, keys) * SCALE, -1e30)
    grown = jnp.exp(scores - jnp.max(scores, axis=-1, keepdims=True))
    return grown * (1.0 / jnp.sum(grown, axis=-1, keepdims=True))


def attention_kernel(
    hops, chunk, place, lengths, query, kv_local, earlier, tokens, w_out, gains,
    mixed, branch, middle, ffn_in, keys,
):
    lanes = lengths.shape[0]
    rows = query.shape[0] // lanes
    for lane in range(lanes):
        span = slice(lane * rows, (lane + 1) * rows)
        keys_of(lane, rows, hops, chunk, earlier, kv_local, keys)
        allowed = allowed_of(place, lengths, lane, rows, hops, W)
        for h in range(HQ):
            cols = slice(h * HD, (h + 1) * HD)
            soft = soft_of(query[span, cols], keys[:, :HD], allowed)
            mixed[span, cols] = dot(soft.astype(BF), keys[:, HD:]).astype(BF)
        out = dot(mixed[span, :], w_out[...])
        branch[span, :] = out
        mid = tokens[span, :].astype(F32) + rms_forward(out, gains[1:2, :])
        middle[span, :] = mid
        ffn_in[span, :] = rms_forward(mid, gains[2:3, :]).astype(BF)


def attention(hops, chunk, place, lengths, query, kv_local, earlier, tokens, w_out, gains):
    total, width = tokens.shape
    lanes = lengths.shape[0]
    return pl.pallas_call(
        functools.partial(attention_kernel, hops, chunk),
        out_shape=[
            jax.ShapeDtypeStruct(query.shape, BF),
            jax.ShapeDtypeStruct((total, width), F32),
            jax.ShapeDtypeStruct((total, width), F32),
            jax.ShapeDtypeStruct((total, width), BF),
        ],
        in_specs=[SMEM, SMEM] + [VMEM] * 6,
        out_specs=[VMEM] * 4,
        scratch_shapes=[pltpu.VMEM(((hops + 1) * (total // lanes), 2 * HD), BF)],
        compiler_params=PARAMS,
        cost_estimate=COST,
    )(place, lengths, query, kv_local, earlier, tokens, w_out, gains)


def attention_back_kernel(
    hops, chunk, cores, core, place, lengths, query, kv_local, earlier, upstream, w_out, gains,
    head_gains, branch, middle, keep, got, query_proj, cosine, sine, late, grad_middle, grad_branch, grad_query, grad_kv, grad_earlier, norm_terms, head_terms,
    keys, d_mixed, raws, softs, queries, mixes,
):
    lanes = lengths.shape[0]
    rows = query.shape[0] // lanes
    width = upstream.shape[1]
    norm_terms[...] = jnp.zeros_like(norm_terms)
    head_terms[...] = jnp.zeros_like(head_terms)
    for lane in range(lanes):
        span = slice(lane * rows, (lane + 1) * rows)
        d_ffn_in = keep[span, :] + got[span, :].astype(F32)
        d_mid, ffn_terms = rms_backward(middle[span, :], gains[2:3, :], d_ffn_in)
        d_mid = d_mid + upstream[span, :].astype(F32)
        grad_middle[span, :] = d_mid
        d_branch, mid_terms = rms_backward(branch[span, :], gains[1:2, :], d_mid)
        norm_terms[0:1, :] += jnp.sum(mid_terms, axis=0, keepdims=True)
        norm_terms[1:2, :] += jnp.sum(ffn_terms, axis=0, keepdims=True)
        low = d_branch.astype(BF)
        grad_branch[span, :] = low
        if cores == 2:
            size = late.shape[1] - HQ * HD
            window = window_of(core[0] ^ 1, width // 2, size)
            late[span, HQ * HD :] = grad_branch[span, window]
        d_mixed[...] = dot_nt(low, w_out[...]).astype(BF)
        keys_of(lane, rows, hops, chunk, earlier, kv_local, keys)
        allowed = allowed_of(place, lengths, lane, rows, hops, W)
        cos, sin = cosine[span, :], sine[span, :]
        for h in range(HQ):
            cols = slice(h * HD, (h + 1) * HD)
            stack = slice(h * rows, (h + 1) * rows)
            soft = soft_of(query[span, cols], keys[:, :HD], allowed)
            d_soft = dot_nt(d_mixed[:, cols], keys[:, HD:])
            inner = jnp.sum(soft * d_soft, axis=-1, keepdims=True)
            raw = (soft * (d_soft - inner) * SCALE).astype(BF)
            raws[stack, :] = raw
            softs[stack, :] = soft.astype(BF)
            queries[stack, :] = query[span, cols]
            mixes[stack, :] = d_mixed[:, cols]
            normed = rotate(dot(raw, keys[:, :HD]), cos, -sin)
            d_query, terms = rms_backward(query_proj[span, cols], head_gains[0:1, :], normed)
            grad_query[span, cols] = d_query.astype(BF)
            if cores == 2:
                late[span, cols] = d_query.astype(BF)
            head_terms[0:1, :] += jnp.sum(terms, axis=0, keepdims=True)
        for part, (left, right) in enumerate(((raws, queries), (softs, mixes))):
            cols = slice(part * HD, (part + 1) * HD)
            out = dot_tn(left[...], right[...])
            for d in range(1, hops + 1):
                for start, size, target in pieces_of(lane, rows, hops, chunk, d):
                    source = (hops - d) * rows + start
                    grad_earlier[target : target + size, cols] = out[
                        source : source + size
                    ].astype(BF)
            grad_kv[span, cols] = out[hops * rows :]


def attention_back(
    hops, chunk, cores, core, place, lengths, query, kv_local, earlier, upstream, w_out, gains, head_gains,
    branch, middle, keep, got, query_proj, cosine, sine,
):
    total, width = upstream.shape
    lanes = lengths.shape[0]
    rows = total // lanes
    span = (hops + 1) * rows
    return pl.pallas_call(
        functools.partial(attention_back_kernel, hops, chunk, cores),
        out_shape=[
            jax.ShapeDtypeStruct((total, HQ * HD + window_size(width, cores)), BF),
            jax.ShapeDtypeStruct((total, width), F32),
            jax.ShapeDtypeStruct((total, width), BF),
            jax.ShapeDtypeStruct(query.shape, BF),
            jax.ShapeDtypeStruct(kv_local.shape, F32),
            jax.ShapeDtypeStruct(earlier.shape, BF),
            jax.ShapeDtypeStruct((8, width), F32),
            jax.ShapeDtypeStruct((8, HD), F32),
        ],
        in_specs=[SMEM] * 3 + [VMEM] * 14,
        out_specs=[VMEM] * 8,
        scratch_shapes=[
            pltpu.VMEM((span, 2 * HD), BF),
            pltpu.VMEM((rows, HQ * HD), BF),
            pltpu.VMEM((HQ * rows, span), BF),
            pltpu.VMEM((HQ * rows, span), BF),
            pltpu.VMEM((HQ * rows, HD), BF),
            pltpu.VMEM((HQ * rows, HD), BF),
        ],
        compiler_params=PARAMS,
        cost_estimate=COST,
    )(
        core, place, lengths, query, kv_local, earlier, upstream, w_out, gains, head_gains,
        branch, middle, keep, got, query_proj, cosine, sine,
    )


def shards(
    tokens,
    cotangent,
    lengths,
    deal_order,
    w_query,
    w_key,
    w_value,
    w_out,
    w_gate,
    w_up,
    w_down,
    norm_gains,
    head_gains,
):
    lanes, rows, width = tokens.shape[1:]
    total = lanes * rows
    seq_count = lax.axis_size("seq")
    cores = lax.axis_size("fsdp")
    own = lax.axis_index("seq")
    core = lax.axis_index("fsdp")
    window = W
    hops = (window - 1 + rows - 1) // rows
    chunk = total // seq_count

    deal = deal_order[0]
    places = jnp.arange(seq_count, dtype=jnp.int32)
    back = jnp.sum(jnp.where(deal[None, :] == places[:, None], places[None, :], 0), axis=1)
    place = deal[own]
    steps = jnp.arange(1, hops + 1, dtype=jnp.int32)
    wanted = deal[:, None] - steps[None, :]
    fetch_table = back[jnp.maximum(wanted, 0)].reshape(-1)
    readers = deal[:, None] + steps[None, :]
    reader_ok = (readers < seq_count).astype(jnp.int32).reshape(-1)
    reader_table = (
        back[jnp.minimum(readers, seq_count - 1)] * hops + (steps[None, :] - 1)
    ).reshape(-1)

    token_rows = tokens.reshape(total, width)
    upstream_rows = cotangent.reshape(total, width)
    q_width = HQ * HD
    narrow = width // cores
    core_ref, own_ref = core.reshape(1), own.reshape(1)

    def core_blocks(block):
        blocks = [block]
        for mask in masks(cores):
            together = jnp.concatenate(blocks, axis=0) if len(blocks) > 1 else blocks[0]
            got = swap(together, "fsdp", mask)
            size = block.shape[0]
            blocks = blocks + [got[j * size : (j + 1) * size] for j in range(len(blocks))]
        return blocks

    def core_sum(keep, send):
        steps = masks(cores)[::-1]
        for mask in steps:
            out = keep + swap(send, "fsdp", mask).astype(F32)
            half = out.shape[0] // 2
            keep, send = out[:half], out[half:].astype(BF)
        return out

    kv_peers = core_blocks(jnp.concatenate([w_key, w_value], axis=1))
    angles = angles_of(own_ref, deal, lengths[0], rows)
    cosine, sine = jnp.cos(angles), jnp.sin(angles)
    attn_in, key_proj, kv_local = key_value(
        core_ref, token_rows, kv_peers, norm_gains, head_gains, cosine, sine
    )

    spread = lax.all_to_all(
        kv_local.reshape(seq_count, chunk, 2 * HD), "seq", 0, 0, tiled=True
    )
    picked = pick(fetch_table, spread).reshape(seq_count, hops * chunk, 2 * HD)
    arrived = lax.all_to_all(picked, "seq", 0, 0, tiled=True)
    run = chunk
    if chunk % 16:
        run = total
        arrived = arrived.reshape(seq_count, hops, chunk, 2 * HD).transpose(1, 0, 2, 3)
    earlier = arrived.reshape(hops * total, 2 * HD)

    w_query, w_out = lax.optimization_barrier((w_query, w_out, kv_local))[:2]
    query_peers = core_blocks(w_query)
    size = -(-narrow // 128) * 128
    peers_out = gather_cores(jnp.pad(w_out, ((0, 0), (0, size - narrow))))
    peers_out = flip(peers_out.reshape(cores, q_width, size), core)
    w_out_full = jnp.concatenate([peers_out[j, :, :narrow] for j in range(cores)], axis=1)
    query_proj, query_rot = queries_of(
        core_ref, attn_in, query_peers, head_gains, cosine, sine
    )

    size = window_size(width, cores)

    def peer_window(values):
        start = (core ^ 1) * narrow // 128 * 128
        return lax.dynamic_slice_in_dim(values, start, size, 1)

    hidden_cols = w_gate.shape[1]
    share = -(-hidden_cols // 256) * 128
    overlap = 2 * share - hidden_cols
    part = ((own & SPLIT_BIT) != 0).astype(jnp.int32)
    part_ref = part.reshape(1)
    if (hidden_cols - share) % 128:
        begin = part * (hidden_cols - share)
        w_gate = lax.dynamic_slice_in_dim(w_gate, begin, share, 1)
        w_up = lax.dynamic_slice_in_dim(w_up, begin, share, 1)
        w_down = lax.dynamic_slice_in_dim(w_down, begin, share, 0)

    earlier = after(earlier, query_rot, w_out_full)
    place_ref, lengths_ref = place.reshape(1), lengths[0]
    mixed_low, branch, middle, ffn_in = attention(
        hops, run, place_ref, lengths_ref, query_rot, kv_local, earlier, token_rows, w_out_full, norm_gains
    )

    if cores == 2:
        mixed_peer = swap(mixed_low, "fsdp", 1)
        attn_peer = swap(peer_window(attn_in), "fsdp", 1)
        early = (mixed_peer, attn_peer)
    else:
        early = ()

    def sum_group(near_part, far_part):
        got = swap(core_sum(*far_part).astype(BF), "seq", SPLIT_BIT)
        return core_sum(*near_part), got

    far_in = swap(ffn_in, "seq", SPLIT_BIT)
    near_all = core_blocks(ffn_in)
    near = ffn_forward(part_ref, near_all, w_gate, w_up, w_down, share, overlap)
    far_all = core_blocks(after(far_in, near[0], *early))
    far = ffn_forward(part_ref, far_all, w_gate, w_up, w_down, share, overlap)
    keep, got = sum_group(near[3:], far[3:])
    ffn_out = keep + got.astype(F32)
    result = middle + rms_forward(ffn_out, norm_gains[3])

    grad_ffn_out, top_terms = rms_backward(ffn_out, norm_gains[3], upstream_rows.astype(F32))
    top_terms = jnp.sum(top_terms, axis=0, keepdims=True)
    grad_low = grad_ffn_out.astype(BF)
    far_grad = swap(grad_low, "seq", SPLIT_BIT)
    near_grads = core_blocks(grad_low)
    near_back = ffn_backward(part_ref, near_grads, near[1], near[2], w_gate, w_up, w_down)
    far_grads = core_blocks(after(far_grad, near_back[0]))
    others = [m for m in masks(seq_count) if m != SPLIT_BIT]
    swapped, beyond = [others[1], others[0]] + others[2:], others[2:]

    def terms_of(left, right, *pieces):
        pieces = [(order + [SPLIT_BIT], size, quad) for order, size, quad in pieces]
        return weight_terms(own, seq_count, pieces, left, *right)

    tile, count = tiles(share)
    minor = max(1, count * 2 // 7) * tile
    outward_first = beyond[:1] + others[:2] + beyond[1:]

    down_terms = terms_of(
        near_grads + far_grads,
        (near[0], far[0]),
        (beyond, share - minor, True),
        (outward_first, minor, False),
    )
    down_b = Chain(*down_terms[1:], outward_first)
    down_quad = lax.all_to_all(
        down_terms[0], "seq", 0, 0, tiled=True, axis_index_groups=quads(seq_count)
    )
    far_grads[0] = after(far_grads[0], *down_terms)
    far_back = ffn_backward(part_ref, far_grads, far[1], far[2], w_gate, w_up, w_down)
    far_sum = core_sum(*far_back[2:]).astype(BF)
    got = swap(far_sum, "seq", SPLIT_BIT)
    keep = core_sum(*near_back[2:])

    gate_terms = terms_of(
        near_all + far_all, (near_back[0], after(far_back[0], far_sum)), (swapped, share, False)
    )
    up_terms = terms_of(
        near_all + far_all, (near_back[1], after(far_back[1], *gate_terms)), (others, share, False)
    )
    gate_c = Chain(*gate_terms, swapped)
    up_c = Chain(*up_terms, others)
    turns = Turns(up_terms[0])

    down_b.step(turns)
    down_first, down_rest = quad_sum(turns.wait(down_quad))
    turns.end(down_first)
    down_a = Chain(down_first, down_rest, beyond)

    (
        late, grad_middle, grad_branch_low, grad_query_low, grad_kv, grad_earlier, norm_terms,
        head_terms,
    ) = attention_back(
        hops, run, cores, core_ref, place_ref, lengths_ref, query_rot, kv_local, earlier, upstream_rows, w_out_full,
        norm_gains, head_gains, branch, middle, keep, turns.wait(got), query_proj, cosine, sine,
    )

    outward = grad_earlier
    if chunk % 16:
        outward = outward.reshape(hops, seq_count, chunk, 2 * HD).transpose(1, 0, 2, 3)
    outward = outward.reshape(seq_count, hops * chunk, 2 * HD)
    collected = lax.all_to_all(outward, "seq", 0, 0, tiled=True)

    turns.end(outward)
    every = swapped + [SPLIT_BIT]
    padded = width // seq_count
    if cores == 2:
        late = swap(late, "fsdp", 1)
        attention_terms = outer_pair(
            own_ref, core_ref, seq_count, every, padded, mixed_low, mixed_peer, grad_branch_low,
            grad_query_low, turns.wait(late), attn_in, attn_peer,
        )
    else:
        outer_keep, outer_send = outer_begin(
            core_ref, cores, mixed_low, grad_branch_low, turns.wait(grad_query_low), attn_in
        )
        outer_keep = core_sum(outer_keep, outer_send)
        outer_got = jnp.zeros(outer_keep.shape, BF)
        attention_terms = outer_end(own_ref, seq_count, every, outer_keep, outer_got, padded)
    turns.end(attention_terms[0])
    outer_c = Chain(*attention_terms, swapped)
    gate_c.step(turns)
    up_c.step(turns)
    down_b.step(turns)
    summed = pick_sum(
        hops,
        reader_table,
        reader_ok,
        turns.wait(collected).reshape(seq_count * hops, chunk, 2 * HD),
    )
    turns.end(summed)
    returned = lax.all_to_all(summed, "seq", 0, 0, tiled=True)
    while down_a.order:
        down_a.step(turns)
    gate_c.step(turns)
    up_c.step(turns)
    outer_c.step(turns)
    while down_b.order:
        down_b.step(turns)
    returned = turns.wait(returned)

    grad_inputs, kv_keep, kv_send, gain_terms = last(
        core_ref, query_peers, kv_peers, token_rows, attn_in, grad_middle, grad_query_low, grad_kv,
        returned.reshape(total, 2 * HD), key_proj, cosine, sine, norm_gains, head_gains, norm_terms,
        head_terms, top_terms,
    )
    kv_rows = HD // seq_count
    tail_order = beyond + [SPLIT_BIT]
    size = kv_keep.shape[1]
    starts = gain_starts(width, size)
    extra = len(starts) * GAIN_ROWS
    if cores == 2:
        kv_got, gains_got = swap(kv_send, "fsdp", 1), swap(gain_terms, "fsdp", 1)
    else:
        kv_keep = core_sum(kv_keep, kv_send)
        kv_got = jnp.zeros(kv_keep.shape, BF)
        for mask in masks(cores)[1:]:
            gain_terms = gain_terms + swap(gain_terms, "fsdp", mask)
        gains_got = swap(gain_terms, "fsdp", 1)
    if kv_rows % 16:
        gains = (gain_terms + gains_got).astype(BF)
        owners = jnp.stack([owner(own) for owner in places_of(tail_order, True)])
        tail = (kv_keep + kv_got.astype(F32)).astype(BF).reshape(2, seq_count, kv_rows, size)
        tail = jnp.take(tail, owners, axis=1, mode="clip").transpose(1, 0, 2, 3)
        tail = tail.reshape(QUAD, -1, size)
        gains = jnp.concatenate([gains[:, start : start + size] for start in starts], axis=0)
        gains = jnp.broadcast_to(gains, (QUAD,) + gains.shape)
        tail = jnp.concatenate([tail, gains], axis=1).reshape(-1, size)
    else:
        tail = tail_begin(own_ref, tail_order, seq_count, kv_keep, kv_got, gain_terms, gains_got)
    ended = lax.all_to_all(
        tail, "seq", 0, 0, tiled=True, axis_index_groups=quads(seq_count)
    )
    turns.end(tail)

    def exchanged(*chains):
        mine = jnp.concatenate([chain.total[1] for chain in chains], axis=1)
        sent = jnp.concatenate([chain.total[0].astype(BF) for chain in chains], axis=1)
        return mine, swap(sent, "seq", SPLIT_BIT)

    down_pair = exchanged(down_a, down_b)
    while gate_c.order:
        gate_c.step(turns)
    outer_c.step(turns)
    ended = turns.wait(ended).reshape(QUAD, -1, size)
    parts = [ended[q] for q in range(QUAD)]
    for mask in tail_order:
        sent, kept = tail_step(parts, extra, False)
        turns.end(sent)
        got = swap(sent, "seq", mask)
        if mask == tail_order[0]:
            while up_c.order:
                up_c.step(turns)
            gate_pair = exchanged(gate_c, up_c)
        if mask == tail_order[-1]:
            while outer_c.order:
                outer_c.step(turns)
            outer_mine, outer_got = exchanged(outer_c)
            pair_got = turns.wait(gate_pair[1])
            turns.end(pair_got)
        parts = [kept, turns.wait(got)]

    def own_columns(values):
        return lax.dynamic_slice_in_dim(values, core * narrow % 128, narrow, 1)

    if kv_rows % 16 or cores != 2:
        (ended,) = tail_step(parts, extra, True)
        key_grad = own_columns(ended[:kv_rows]).T
        value_grad = own_columns(ended[kv_rows : 2 * kv_rows]).T
        windows = ended[-extra:].reshape(len(starts), GAIN_ROWS, size)
        gains = jnp.concatenate(
            [windows[k][:, k * size - start :] for k, start in enumerate(starts)], axis=1
        )
        norm_total, head_total = gains[:4], gains[4:6, :HD]
    else:
        key_grad, value_grad, norm_total, head_total = tail_end(core_ref, width, kv_rows, parts)
        key_grad, value_grad = key_grad.T, value_grad.T

    mine, got = down_pair
    mine = jnp.concatenate([mine, gate_pair[0]], axis=1)
    got = jnp.concatenate([turns.wait(got), pair_got], axis=1).astype(F32)
    lower, upper = jnp.where(part == 0, mine, got), jnp.where(part == 0, got, mine)
    down_grad, gate_grad, up_grad = (
        jnp.concatenate(
            [
                lower[:, k * share : (k + 1) * share],
                upper[:, k * share + overlap : (k + 1) * share],
            ],
            axis=1,
        )
        for k in range(3)
    )
    down_grad = down_grad.T
    attention_grad = outer_mine + turns.wait(outer_got).astype(F32)
    query_rows = q_width // seq_count
    size = attention_grad.shape[1] // 2
    out_grad = own_columns(attention_grad[:query_rows, :size])
    query_grad = own_columns(attention_grad[:query_rows, size:]).T


    return (
        result.reshape(1, lanes, rows, width),
        grad_inputs.reshape(1, lanes, rows, width),
        query_grad,
        key_grad,
        value_grad,
        out_grad,
        gate_grad,
        up_grad,
        down_grad,
        norm_total,
        head_total,
    )


def solution(mesh):
    in_specs = (
        P("fsdp", None, "seq", None),
        P("fsdp", None, "seq", None),
        P("fsdp", None, None),
        P("fsdp", None),
        P("fsdp", None),
        P("fsdp", None),
        P("fsdp", None),
        P(None, "fsdp"),
        P(None, "fsdp"),
        P(None, "fsdp"),
        P("fsdp", None),
        P(),
        P(),
    )
    out_specs = (
        P("fsdp", None, "seq", None),
        P("fsdp", None, "seq", None),
        P("fsdp", "seq"),
        P("fsdp", "seq"),
        P("fsdp", "seq"),
        P("seq", "fsdp"),
        P("seq", "fsdp"),
        P("seq", "fsdp"),
        P("fsdp", "seq"),
        P(),
        P(),
    )
    return jax.shard_map(shards, mesh=mesh, in_specs=in_specs, out_specs=out_specs, check_vma=False)
```

```python
import functools
import math

import jax
import jax.numpy as jnp
from jax import lax
from jax.experimental import pallas as pl
from jax.experimental.pallas import tpu as pltpu
from jax.sharding import PartitionSpec as P

HQ = 4
HD = 256
W = 512
EPSILON = 1e-06
ROPE_BASE = 10000.0
SPLIT_BIT = 4

BF = jnp.bfloat16
F32 = jnp.float32


def swap(value, axis, mask):
    count = lax.axis_size(axis)
    return lax.ppermute(value, axis, [(i, i ^ mask) for i in range(count)])


def masks(count):
    return [1 << k for k in range(count.bit_length() - 1)]


def gather_cores(block):
    for mask in masks(lax.axis_size("fsdp")):
        block = jnp.concatenate([block, swap(block, "fsdp", mask)], axis=0)
    return block


def sum_cores(block):
    for mask in reversed(masks(lax.axis_size("fsdp"))):
        half = block.shape[0] // 2
        got = swap(block[half:].astype(BF), "fsdp", mask)
        block = block[:half].astype(F32) + got.astype(F32)
    return block


def flip(parts, index):
    count = parts.shape[0]
    for mask in masks(count):
        turned = jnp.stack([parts[j ^ mask] for j in range(count)])
        parts = jnp.where((index & mask) != 0, turned, parts)
    return parts


def rms_scale(values):
    return lax.rsqrt(jnp.mean(values * values, axis=-1, keepdims=True) + EPSILON)


def rms_forward(values, gain_vec):
    return values * rms_scale(values) * gain_vec


def rms_backward(values, gain_vec, grad_out):
    scale_rows = rms_scale(values)
    weighted = grad_out * gain_vec
    inner_mean = jnp.mean(weighted * values, axis=-1, keepdims=True)
    grad_in = scale_rows * weighted - values * (scale_rows * scale_rows * scale_rows) * inner_mean
    return (grad_in, grad_out * values * scale_rows)


def rope_tables(seq_pos, head_dim):
    half_dim = head_dim // 2
    frequency = jnp.exp(
        jnp.arange(half_dim, dtype=F32) * (-2.0 * math.log(ROPE_BASE) / head_dim)
    )
    angles = seq_pos.astype(F32)[..., None] * frequency
    return (jnp.cos(angles), jnp.sin(angles))


def rotate(values, cosine_table, sine_table):
    half_dim = values.shape[-1] // 2
    first_half = values[..., :half_dim]
    second_half = values[..., half_dim:]
    return jnp.concatenate(
        [
            first_half * cosine_table - second_half * sine_table,
            second_half * cosine_table + first_half * sine_table,
        ],
        axis=-1,
    )


def gelu_tanh(values):
    return jax.nn.gelu(values, approximate=True)


def sequence_info(lengths, stream_pos):
    seq_ends = jnp.cumsum(lengths, axis=-1)
    before = seq_ends[..., None, :] <= stream_pos[..., :, None]
    seq_ids = jnp.sum(before.astype(jnp.int32), axis=-1)
    starts = jnp.sum(jnp.where(before, lengths[..., None, :], 0), axis=-1)
    return (seq_ids, stream_pos - starts)


def dot(a, b):
    return jnp.dot(a, b, preferred_element_type=F32)


def dot_tn(a, b):
    return lax.dot_general(a, b, (((0,), (0,)), ((), ())), preferred_element_type=F32)


def dot_nt(a, b):
    return lax.dot_general(a, b, (((1,), (1,)), ((), ())), preferred_element_type=F32)


def pick(table, source):
    return jnp.take(source, table, axis=0, mode="clip")


def pick_sum(hops, table, valid, source):
    terms = jnp.take(source, table, axis=0, mode="clip").astype(F32) * valid.astype(F32)[:, None, None]
    count = table.shape[0] // hops
    return jnp.sum(terms.reshape((count, hops) + source.shape[1:]), axis=1).astype(source.dtype)


QUAD = 4


def quads(count):
    return [[base + q for q in range(QUAD)] for base in range(0, count, QUAD)]


def quad_arrangement(order):
    return [(q, j) for q in range(QUAD) for j in arrangement(order)]


def places_of(order, quad):
    if quad:
        return [lambda me, q=q, j=j: ((me & ~(QUAD - 1)) ^ j) + q for q, j in quad_arrangement(order)]
    return [lambda me, j=j: me ^ j for j in arrangement(order)]


def arrangement(order):
    if not order:
        return [0]
    rest = arrangement(order[1:])
    return [j | order[0] for j in rest] + rest


def after(value, *others):
    return lax.optimization_barrier((value,) + others)[0]


class Turns:
    def __init__(self, token):
        self.token = token

    def wait(self, value):
        return after(value, self.token)

    def end(self, token):
        self.token = token


def step_kernel(rest, got, *outs):
    count = rest.shape[0]
    for k in range(count):
        total = rest[k].astype(F32) + got[k].astype(F32)
        top, row = divmod(k, outs[0].shape[0])
        outs[top][row] = total.astype(outs[top].dtype)


def step_of(rest, got, final):
    count = rest.shape[0]
    parts, kind = (1, F32) if final else (2, BF)
    shape = jax.ShapeDtypeStruct((count // parts,) + rest.shape[1:], kind)
    return pl.pallas_call(
        step_kernel,
        out_shape=[shape] * parts,
        in_specs=[VMEM] * 2,
        out_specs=[VMEM] * parts,
        compiler_params=PARAMS,
        cost_estimate=COST,
    )(rest, got)


def quad_kernel(got, *outs):
    count = got.shape[0] // QUAD
    for k in range(count):
        total = sum(got[q * count + k].astype(F32) for q in range(QUAD))
        top, row = divmod(k, outs[0].shape[0])
        outs[top][row] = total.astype(BF)


def quad_sum(got):
    shape = jax.ShapeDtypeStruct((got.shape[0] // QUAD // 2,) + got.shape[1:], BF)
    return pl.pallas_call(
        quad_kernel,
        out_shape=[shape] * 2,
        in_specs=[VMEM],
        out_specs=[VMEM] * 2,
        compiler_params=PARAMS,
        cost_estimate=COST,
    )(got)


class Chain:
    def __init__(self, first, rest, order):
        self.rest, self.order = rest, list(order)
        self.got = swap(first, "seq", self.order[0])

    def step(self, turns):
        got = turns.wait(self.got)
        self.order.pop(0)
        if self.order:
            first, self.rest = step_of(self.rest, got, False)
            self.got = swap(first, "seq", self.order[0])
            turns.end(first)
        else:
            (self.total,) = step_of(self.rest, got, True)
            turns.end(self.total)


def tiles(size):
    tile = 256 if size % 256 == 0 else 128
    return tile, size // tile


def column_tiles(size):
    return [(start, min(256, size - start)) for start in range(0, size, 256)]


COST = pl.CostEstimate(flops=1024, bytes_accessed=1024, transcendentals=0)
VMEM = pl.BlockSpec(memory_space=pltpu.VMEM)
SMEM = pl.BlockSpec(memory_space=pltpu.SMEM)
PARAMS = pltpu.CompilerParams(vmem_limit_bytes=56 * 1024 * 1024)
ROOT = math.sqrt(2.0 / math.pi)
CUBE = 0.044715


def ffn_forward_kernel(n, overlap, *refs):
    part, x_refs, (wg, wu, wd) = refs[0], refs[1 : n + 1], refs[n + 1 : n + 4]
    hid_out, act_out, slope_out, keep, send = refs[n + 4 : n + 9]
    x_all, wg_all, wu_all, wd_all, gate, hid, act, slope, load, store = refs[n + 9 :]
    rows = x_refs[0].shape[0]
    share = hid.shape[1]
    tile, count = tiles(share)
    begin = pl.multiple_of(part[0] * (wg.shape[1] - share), 128)
    down_begin = pl.multiple_of(part[0] * (wd.shape[0] - share), 16)
    loads = [
        pltpu.make_async_copy(wg.at[:, pl.ds(begin, share)], wg_all, load.at[0]),
        pltpu.make_async_copy(wu.at[:, pl.ds(begin, share)], wu_all, load.at[1]),
        pltpu.make_async_copy(wd.at[pl.ds(down_begin, share), :], wd_all, load.at[2]),
    ]
    for copy in loads:
        copy.start()
    for j in range(n):
        x_all[j * rows : (j + 1) * rows, :] = x_refs[j][...]
    parts = [slice(i * tile, (i + 1) * tile) for i in range(count)]
    loads[0].wait()
    for cols in parts:
        gate[:, cols] = dot(x_all[...], wg_all[:, cols])
    loads[1].wait()
    for i, cols in enumerate(parts):
        g, u = gate[:, cols], dot(x_all[...], wu_all[:, cols])
        square = g * g
        t = jnp.tanh(g * (ROOT + ROOT * CUBE * square))
        half = 0.5 * (1.0 + t)
        a = g * half
        d = half + a * (1.0 - t) * (ROOT + 3.0 * ROOT * CUBE * square)
        if i * tile < overlap:
            index = i * tile + lax.broadcasted_iota(jnp.int32, a.shape, 1)
            counted = index >= part[0] * overlap
            a, u = jnp.where(counted, a, 0.0), jnp.where(counted, u, 0.0)
        hid[:, cols] = (a * u).astype(BF)
        act[:, cols] = a.astype(BF)
        slope[:, cols] = (u * d).astype(BF)
    stores = [
        pltpu.make_async_copy(hid, hid_out, store.at[0]),
        pltpu.make_async_copy(act, act_out, store.at[1]),
        pltpu.make_async_copy(slope, slope_out, store.at[2]),
    ]
    for copy in stores:
        copy.start()
    loads[2].wait()
    for start, size in column_tiles(wd.shape[1]):
        out = dot(hid[...], wd_all[:, start : start + size])
        half = out.shape[0] // 2
        keep[:, start : start + size] = out[:half]
        send[:, start : start + size] = out[half:].astype(BF)
    for copy in stores:
        copy.wait()


ANY = pl.BlockSpec(memory_space=pl.ANY)


def ffn_forward(part, blocks, wg, wu, wd, share, overlap):
    n, (rows, width) = len(blocks), blocks[0].shape
    total = n * rows
    return pl.pallas_call(
        functools.partial(ffn_forward_kernel, n, overlap),
        out_shape=[jax.ShapeDtypeStruct((total, share), BF)] * 3
        + [
            jax.ShapeDtypeStruct((total // 2, width), F32),
            jax.ShapeDtypeStruct((total // 2, width), BF),
        ],
        in_specs=[SMEM] + [VMEM] * n + [ANY] * 3,
        out_specs=[ANY] * 3 + [VMEM] * 2,
        scratch_shapes=[pltpu.VMEM((total, width), BF)]
        + [pltpu.VMEM((width, share), BF)] * 2
        + [pltpu.VMEM((share, width), BF)]
        + [pltpu.VMEM((total, share), F32)]
        + [pltpu.VMEM((total, share), BF)] * 3
        + [pltpu.SemaphoreType.DMA((3,))] * 2,
        compiler_params=PARAMS,
        cost_estimate=COST,
    )(part, *blocks, wg, wu, wd)


def ffn_backward_kernel(n, *refs):
    part, g_refs, (act, slope, wg, wu, wd) = refs[0], refs[1 : n + 1], refs[n + 1 : n + 6]
    gate_out, up_out, keep, send = refs[n + 6 : n + 10]
    g_all, act_all, slope_all, wg_all, wu_all, wd_all, d_gate, d_up, load, store = refs[n + 10 :]
    rows = g_refs[0].shape[0]
    share = d_gate.shape[1]
    tile, count = tiles(share)
    down_begin = pl.multiple_of(part[0] * (wd.shape[0] - share), 16)
    begin = pl.multiple_of(part[0] * (wg.shape[1] - share), 128)
    loads = [
        pltpu.make_async_copy(wd.at[pl.ds(down_begin, share), :], wd_all, load.at[0]),
        pltpu.make_async_copy(act, act_all, load.at[1]),
        pltpu.make_async_copy(slope, slope_all, load.at[2]),
        pltpu.make_async_copy(wg.at[:, pl.ds(begin, share)], wg_all, load.at[3]),
        pltpu.make_async_copy(wu.at[:, pl.ds(begin, share)], wu_all, load.at[4]),
    ]
    for copy in loads:
        copy.start()
    for j in range(n):
        g_all[j * rows : (j + 1) * rows, :] = g_refs[j][...]
    for copy in loads[:3]:
        copy.wait()
    for i in range(count):
        cols = slice(i * tile, (i + 1) * tile)
        d = dot_nt(g_all[...], wd_all[cols, :])
        d_gate[:, cols] = (d * slope_all[:, cols].astype(F32)).astype(BF)
        d_up[:, cols] = (d * act_all[:, cols].astype(F32)).astype(BF)
    stores = [
        pltpu.make_async_copy(d_gate, gate_out, store.at[0]),
        pltpu.make_async_copy(d_up, up_out, store.at[1]),
    ]
    for copy in stores:
        copy.start()
    for copy in loads[3:]:
        copy.wait()
    for start, size in column_tiles(wg.shape[0]):
        out = dot_nt(d_gate[...], wg_all[start : start + size, :])
        out = out + dot_nt(d_up[...], wu_all[start : start + size, :])
        half = out.shape[0] // 2
        keep[:, start : start + size] = out[:half]
        send[:, start : start + size] = out[half:].astype(BF)
    for copy in stores:
        copy.wait()


def ffn_backward(part, blocks, act, slope, wg, wu, wd):
    n, (rows, width), share = len(blocks), blocks[0].shape, act.shape[1]
    total = n * rows
    return pl.pallas_call(
        functools.partial(ffn_backward_kernel, n),
        out_shape=[jax.ShapeDtypeStruct((total, share), BF)] * 2
        + [
            jax.ShapeDtypeStruct((total // 2, width), F32),
            jax.ShapeDtypeStruct((total // 2, width), BF),
        ],
        in_specs=[SMEM] + [VMEM] * n + [ANY] * 5,
        out_specs=[ANY] * 2 + [VMEM] * 2,
        scratch_shapes=[pltpu.VMEM((total, width), BF)]
        + [pltpu.VMEM((total, share), BF)] * 2
        + [pltpu.VMEM((width, share), BF)] * 2
        + [pltpu.VMEM((share, width), BF)]
        + [pltpu.VMEM((total, share), BF)] * 2
        + [pltpu.SemaphoreType.DMA((5,)), pltpu.SemaphoreType.DMA((2,))],
        compiler_params=PARAMS,
        cost_estimate=COST,
    )(part, *blocks, act, slope, wg, wu, wd)


def weight_kernel(n, pieces, *refs):
    own, left = refs[0], refs[1 : n + 1]
    outs, (turned, out, right, load) = refs[n + 3 : -4], refs[-4:]
    rows = left[0].shape[0]
    tile, count = tiles(right.shape[1])
    half = right.shape[0] // 2

    def copies(i):
        cols = pl.ds(pl.multiple_of(i * tile, tile), tile)
        return [
            pltpu.make_async_copy(
                refs[n + 1 + k].at[:, cols], right.at[k * half : (k + 1) * half, cols], load.at[k, i]
            )
            for k in range(2)
        ]

    for i in range(count):
        for copy in copies(i):
            copy.start()
    for j in range(n):
        turned[:, j * rows : (j + 1) * rows] = left[j][...].T
    me = own[0]
    begin = 0
    for order, size, quad in pieces:
        halves, outs = (outs[:1], outs[1:]) if quad else (outs[:2], outs[2:])
        block = halves[0].shape[1]

        @pl.loop(0, size // tile)
        def _(i):
            cols = pl.ds(pl.multiple_of(begin + i * tile, tile), tile)
            into = pl.ds(pl.multiple_of(i * tile, tile), tile)
            for copy in copies(begin // tile + i):
                copy.wait()
            out[...] = dot(turned[...], right[:, cols])
            for k, owner in enumerate(places_of(order, quad)):
                source = pl.multiple_of(owner(me) * block, 8)
                top, k = divmod(k, halves[0].shape[0])
                halves[top][k, :, into] = out[pl.ds(source, block), :].astype(BF)

        begin = begin + size


def weight_terms(own, seq_count, pieces, left, near, far):
    width, share = left[0].shape[1], near.shape[1]
    block = width // seq_count
    half = seq_count // 2
    n = len(left)
    if block % 8:
        full = dot_tn(jnp.concatenate(left), jnp.concatenate([near, far])).astype(BF)
        full = full.reshape(seq_count, block, share)
        outs, begin = [], 0
        for order, size, quad in pieces:
            piece = full[:, :, begin : begin + size]
            owners = jnp.stack([owner(own) for owner in places_of(order, quad)])
            piece = jnp.take(piece, owners, axis=0, mode="clip")
            outs += [piece] if quad else [piece[:half], piece[half:]]
            begin += size
        return outs
    tile, _ = tiles(share)
    return pl.pallas_call(
        functools.partial(weight_kernel, n, pieces),
        out_shape=[
            jax.ShapeDtypeStruct((seq_count if quad else half, block, size), BF)
            for _, size, quad in pieces
            for _ in range(1 if quad else 2)
        ],
        in_specs=[SMEM] + [VMEM] * n + [ANY] * 2,
        out_specs=[VMEM] * sum(1 if quad else 2 for _, _, quad in pieces),
        scratch_shapes=[
            pltpu.VMEM((width, n * left[0].shape[0]), BF),
            pltpu.VMEM((width, tile), F32),
            pltpu.VMEM((n * left[0].shape[0], share), BF),
            pltpu.SemaphoreType.DMA((2, share // tile)),
        ],
        compiler_params=PARAMS,
        cost_estimate=COST,
    )(own.reshape(1), *left, near, far)


def window_size(width, cores):
    narrow = width // cores
    return max(-(-((c * narrow) % 128 + narrow) // 128) for c in range(cores)) * 128


def window_of(core, narrow, size):
    return pl.ds(pl.multiple_of(core * narrow // 128 * 128, 128), size)


def outer_kernel(cores, core, mixed, branch, query, attn_in, keep, send):
    size = keep.shape[1]
    split = mixed.shape[1]
    narrow = branch.shape[1] // cores
    for part, (left, right) in enumerate(((mixed, branch), (query, attn_in))):
        turned = left[...].T
        for j in range(cores):
            out = dot(turned, right[:, window_of(core[0] ^ j, narrow, size)])
            target, row = (keep, j) if j < cores // 2 else (send, j - cores // 2)
            row = (2 * row + part) * split
            target[row : row + split, :] = out.astype(target.dtype)


def outer_sum_kernel(order, own, keep, got, first, rest):
    me = own[0]
    half, padded, two = first.shape
    size = two // 2
    width = keep.shape[0] // 2
    block = width // (2 * half)
    for k, j in enumerate(arrangement(order)):
        target = first if k < half else rest
        for part in range(2):
            source = pl.ds(pl.multiple_of(part * width + (me ^ j) * block, 16), block)
            total = keep[source, :] + got[source, :].astype(F32)
            total = jnp.concatenate([total, jnp.zeros((padded - block, size), F32)], axis=0)
            target[k % half, :, part * size : (part + 1) * size] = total.astype(BF)


def outer_begin(core, cores, mixed, branch, query, attn_in):
    width = mixed.shape[1]
    size = window_size(branch.shape[1], cores)
    return pl.pallas_call(
        functools.partial(outer_kernel, cores),
        out_shape=[
            jax.ShapeDtypeStruct((cores * width, size), F32),
            jax.ShapeDtypeStruct((cores * width, size), BF),
        ],
        in_specs=[SMEM] + [VMEM] * 4,
        out_specs=[VMEM] * 2,
        compiler_params=PARAMS,
        cost_estimate=COST,
    )(core, mixed, branch, query, attn_in)


def outer_end(own, seq_count, order, keep, got, padded):
    total, size = keep.shape
    half = seq_count // 2
    return pl.pallas_call(
        functools.partial(outer_sum_kernel, order),
        out_shape=[jax.ShapeDtypeStruct((half, padded, 2 * size), BF)] * 2,
        in_specs=[SMEM, VMEM, VMEM],
        out_specs=[VMEM] * 2,
        compiler_params=PARAMS,
        cost_estimate=COST,
    )(own, keep, got)


def outer_pair_kernel(
    order, own, core, mixed, mixed_peer, branch, query, late, attn_in, attn_peer,
    first, rest, left, right, total,
):
    me = own[0]
    half, padded, two = first.shape
    size = two // 2
    rows, width = mixed.shape
    block = width // (2 * half)
    window = window_of(core[0], branch.shape[1] // 2, size)
    for part, (mine, peer, other, other_peer) in enumerate(
        (
            (mixed, mixed_peer, branch, late[:, width:]),
            (query, late.at[:, :width], attn_in, attn_peer[...]),
        )
    ):
        left[:rows, :] = mine[...]
        left[rows:, :] = peer[...]
        right[:rows, :] = other[:, window]
        right[rows:, :] = other_peer
        total[part] = dot_tn(left[...], right[...])
        for k, j in enumerate(arrangement(order)):
            target = first if k < half else rest
            value = total[part, pl.ds(pl.multiple_of((me ^ j) * block, 16), block), :]
            value = jnp.concatenate([value, jnp.zeros((padded - block, size), F32)], axis=0)
            target[k % half, :, part * size : (part + 1) * size] = value.astype(BF)


def outer_pair(own, core, seq_count, order, padded, mixed, *rest):
    rows, width = mixed.shape
    size = rest[-1].shape[1]
    half = seq_count // 2
    return pl.pallas_call(
        functools.partial(outer_pair_kernel, order),
        out_shape=[jax.ShapeDtypeStruct((half, padded, 2 * size), BF)] * 2,
        in_specs=[SMEM, SMEM] + [VMEM] * (1 + len(rest)),
        out_specs=[VMEM] * 2,
        scratch_shapes=[
            pltpu.VMEM((2 * rows, width), BF),
            pltpu.VMEM((2 * rows, size), BF),
            pltpu.VMEM((2, width, size), F32),
        ],
        compiler_params=PARAMS,
        cost_estimate=COST,
    )(own, core, mixed, *rest)


def whole_rows(core, peers, full):
    for j, peer in enumerate(peers):
        rows = peer.shape[0]
        full[pl.ds(pl.multiple_of((core[0] ^ j) * rows, 16), rows), :] = peer[...]


def angle_kernel(rows, own, deal, lengths, frequency, angles):
    place = deal[own[0]] * rows + lax.broadcasted_iota(jnp.int32, (rows, 1), 0)
    for lane in range(lengths.shape[0]):
        start, end = jnp.zeros_like(place), jnp.int32(0)
        for j in range(lengths.shape[1]):
            end = end + lengths[lane, j]
            start = start + jnp.where(end <= place, lengths[lane, j], 0)
        angles[lane * rows : (lane + 1) * rows, :] = (place - start).astype(F32) * frequency[...]


def angles_of(own, deal, lengths, rows):
    half = HD // 2
    frequency = jnp.exp(jnp.arange(half, dtype=F32) * (-2.0 * math.log(ROPE_BASE) / HD))
    return pl.pallas_call(
        functools.partial(angle_kernel, rows),
        out_shape=jax.ShapeDtypeStruct((lengths.shape[0] * rows, half), F32),
        in_specs=[SMEM] * 3 + [VMEM],
        out_specs=VMEM,
        compiler_params=PARAMS,
        cost_estimate=COST,
    )(own, deal, lengths, frequency.reshape(1, half))


def key_value_kernel(n, core, tokens, *refs):
    peers, (gains, head_gains, cosine, sine) = refs[:n], refs[n : n + 4]
    attn_in, key_proj, kv_local, full = refs[n + 4 :]
    whole_rows(core, peers, full)
    normed = rms_forward(tokens[...].astype(F32), gains[0:1, :]).astype(BF)
    attn_in[...] = normed
    both = dot(normed, full[...])
    keys = both[:, :HD]
    key_proj[...] = keys
    turned = rotate(rms_forward(keys, head_gains[1:2, :]), cosine[...], sine[...])
    kv_local[:, :HD] = turned.astype(BF)
    kv_local[:, HD:] = both[:, HD:].astype(BF)


def key_value(core, tokens, peers, gains, head_gains, cosine, sine):
    total, width = tokens.shape
    return pl.pallas_call(
        functools.partial(key_value_kernel, len(peers)),
        out_shape=[
            jax.ShapeDtypeStruct((total, width), BF),
            jax.ShapeDtypeStruct((total, HD), F32),
            jax.ShapeDtypeStruct((total, 2 * HD), BF),
        ],
        in_specs=[SMEM] + [VMEM] * (len(peers) + 5),
        out_specs=[VMEM] * 3,
        scratch_shapes=[pltpu.VMEM((width, 2 * HD), BF)],
        compiler_params=PARAMS,
        cost_estimate=COST,
    )(core, tokens, *peers, gains, head_gains, cosine, sine)


def query_kernel(n, core, attn_in, *refs):
    peers, (head_gains, cosine, sine, proj, query, full) = refs[:n], refs[n:]
    whole_rows(core, peers, full)
    for h in range(HQ):
        cols = slice(h * HD, (h + 1) * HD)
        out = dot(attn_in[...], full[:, cols])
        proj[:, cols] = out
        turned = rotate(rms_forward(out, head_gains[0:1, :]), cosine[...], sine[...])
        query[:, cols] = turned.astype(BF)


def queries_of(core, attn_in, peers, head_gains, cosine, sine):
    total, width = attn_in.shape
    return pl.pallas_call(
        functools.partial(query_kernel, len(peers)),
        out_shape=[
            jax.ShapeDtypeStruct((total, HQ * HD), F32),
            jax.ShapeDtypeStruct((total, HQ * HD), BF),
        ],
        in_specs=[SMEM] + [VMEM] * (len(peers) + 4),
        out_specs=[VMEM] * 2,
        scratch_shapes=[pltpu.VMEM((width, HQ * HD), BF)],
        compiler_params=PARAMS,
        cost_estimate=COST,
    )(core, attn_in, *peers, head_gains, cosine, sine)


GAIN_ROWS = 16


def gain_starts(width, size):
    return [min(start, width - size) for start in range(0, width, size)]


def last_kernel(n, core, *refs):
    q_peers, kv_peers = refs[:n], refs[n : 2 * n]
    (
        tokens, attn_in, grad_middle, grad_query, grad_kv, returned, key_proj, cosine, sine,
        gains, head_gains, norm_terms, head_terms, top_terms,
        grad_inputs, keep, send, gain_terms, q_full, kv_full,
    ) = refs[2 * n :]
    whole_rows(core, q_peers, q_full)
    whole_rows(core, kv_peers, kv_full)
    grads = grad_kv[...] + returned[...].astype(F32)
    normed = rotate(grads[:, :HD], cosine[...], -sine[...])
    d_key, key_terms = rms_backward(key_proj[...], head_gains[1:2, :], normed)
    low = jnp.concatenate([d_key.astype(BF), grads[:, HD:].astype(BF)], axis=1)
    size = keep.shape[1]
    narrow = attn_in.shape[1] // n
    turned = low.T
    for j in range(n):
        out = dot(turned, attn_in[:, window_of(core[0] ^ j, narrow, size)])
        target, row = (keep, j) if j < n // 2 else (send, j - n // 2)
        row = row * 2 * HD
        target[row : row + 2 * HD, :] = out.astype(target.dtype)
    d_in = dot_nt(grad_query[...], q_full[...]) + dot_nt(low, kv_full[...])
    d_tokens, in_terms = rms_backward(tokens[...].astype(F32), gains[0:1, :], d_in)
    grad_inputs[...] = grad_middle[...] + d_tokens
    gain_terms[...] = jnp.zeros_like(gain_terms)
    gain_terms[0:1, :] = jnp.sum(in_terms, axis=0, keepdims=True)
    gain_terms[1:3, :] = norm_terms[0:2, :]
    gain_terms[3:4, :] = top_terms[...]
    gain_terms[4:5, :HD] = head_terms[0:1, :]
    gain_terms[5:6, :HD] = jnp.sum(key_terms, axis=0, keepdims=True)


def last(core, q_peers, kv_peers, *rest):
    n = len(q_peers)
    total, width = rest[0].shape
    size = window_size(width, n)
    return pl.pallas_call(
        functools.partial(last_kernel, n),
        out_shape=[
            jax.ShapeDtypeStruct((total, width), F32),
            jax.ShapeDtypeStruct((n * HD, size), F32),
            jax.ShapeDtypeStruct((n * HD, size), BF),
            jax.ShapeDtypeStruct((GAIN_ROWS, width), F32),
        ],
        in_specs=[SMEM] + [VMEM] * (2 * n + len(rest)),
        out_specs=[VMEM] * 4,
        scratch_shapes=[pltpu.VMEM((width, HQ * HD), BF), pltpu.VMEM((width, 2 * HD), BF)],
        compiler_params=PARAMS,
        cost_estimate=COST,
    )(core, *q_peers, *kv_peers, *rest)


def tail_kernel(order, count, own, keep, got, gains, gains_got, out):
    me = own[0]
    size = keep.shape[1]
    block = keep.shape[0] // 2 // count
    places = places_of(order, True)
    part = len(places) // QUAD
    starts = gain_starts(gains.shape[1], size)
    rows = part * 2 * block + len(starts) * GAIN_ROWS
    summed = (gains[...] + gains_got[...]).astype(BF)
    for k, owner in enumerate(places):
        q, k = divmod(k, part)
        for half in range(2):
            source = pl.ds(pl.multiple_of((half * count + owner(me)) * block, 16), block)
            row = q * rows + (2 * k + half) * block
            out[row : row + block, :] = (keep[source, :] + got[source, :].astype(F32)).astype(BF)
    for q in range(QUAD):
        row = (q + 1) * rows - len(starts) * GAIN_ROWS
        for k, start in enumerate(starts):
            at = row + k * GAIN_ROWS
            out[at : at + GAIN_ROWS, :] = summed[:, start : start + size]


def tail_begin(own, order, count, keep, got, gains, gains_got):
    rows, size = keep.shape
    extra = len(gain_starts(gains.shape[1], size)) * GAIN_ROWS
    return pl.pallas_call(
        functools.partial(tail_kernel, order, count),
        out_shape=jax.ShapeDtypeStruct((rows + QUAD * extra, size), BF),
        in_specs=[SMEM] + [VMEM] * 4,
        out_specs=VMEM,
        compiler_params=PARAMS,
        cost_estimate=COST,
    )(own, keep, got, gains, gains_got)


def tail_step_kernel(ways, extra, final, *refs):
    parts, outs = refs[:ways], refs[ways:]
    total = sum(part[...].astype(F32) for part in parts)
    if final:
        outs[0][...] = total
        return
    low = total.astype(BF)
    body = low.shape[0] - extra
    half = body // 2
    send, keep = outs
    send[:half, :] = low[:half]
    keep[:half, :] = low[half:body]
    send[half:, :] = low[body:]
    keep[half:, :] = low[body:]


def tail_step(parts, extra, final):
    rows, size = parts[0].shape
    if final:
        shapes = [jax.ShapeDtypeStruct((rows, size), F32)]
    else:
        half = (rows - extra) // 2 + extra
        shapes = [jax.ShapeDtypeStruct((half, size), BF)] * 2
    return pl.pallas_call(
        functools.partial(tail_step_kernel, len(parts), extra, final),
        out_shape=shapes,
        in_specs=[VMEM] * len(parts),
        out_specs=[VMEM] * len(shapes),
        compiler_params=PARAMS,
        cost_estimate=COST,
    )(*parts)


def tail_end_kernel(core, kept, got, key_grad, value_grad, norm_total, head_total):
    total = kept[...].astype(F32) + got[...].astype(F32)
    rows, size = total.shape
    width = norm_total.shape[1]
    block, narrow = key_grad.shape
    starts = gain_starts(width, size)
    for k, target in enumerate((key_grad, value_grad)):
        rows_of = total[k * block : (k + 1) * block]
        start = narrow % 128
        target[...] = jnp.where(
            core[0] == 0, rows_of[:, :narrow], rows_of[:, start : start + narrow]
        )
    first = rows - len(starts) * GAIN_ROWS
    for k, begin in enumerate(starts):
        row = first + k * GAIN_ROWS
        norm_total[:, begin : begin + size] = total[row : row + 4]
    head_total[...] = total[first + 4 : first + 6, :HD]


def tail_end(core, width, block, parts):
    narrow, size = width // 2, parts[0].shape[1]
    return pl.pallas_call(
        tail_end_kernel,
        out_shape=[
            jax.ShapeDtypeStruct((block, narrow), F32),
            jax.ShapeDtypeStruct((block, narrow), F32),
            jax.ShapeDtypeStruct((4, width), F32),
            jax.ShapeDtypeStruct((2, HD), F32),
        ],
        in_specs=[SMEM, VMEM, VMEM],
        out_specs=[VMEM] * 4,
        compiler_params=PARAMS,
        cost_estimate=COST,
    )(core, *parts)


SCALE = HD ** (-0.5)


def pieces_of(lane, rows, hops, chunk, d):
    size = min(chunk, rows)
    for start in range(0, rows, size):
        row = lane * rows + start
        yield start, size, (row // chunk * hops + d - 1) * chunk + row % chunk


def keys_of(lane, rows, hops, chunk, earlier, kv_local, keys):
    for d in range(1, hops + 1):
        for start, size, source in pieces_of(lane, rows, hops, chunk, d):
            target = (hops - d) * rows + start
            keys[target : target + size, :] = earlier[source : source + size, :]
    keys[hops * rows :, :] = kv_local[lane * rows : (lane + 1) * rows, :]


def allowed_of(place, lengths, lane, rows, hops, window):
    first = place[0] * rows
    q_pos = first + lax.broadcasted_iota(jnp.int32, (rows, 1), 0)
    k_pos = first - hops * rows + lax.broadcasted_iota(jnp.int32, (1, (hops + 1) * rows), 1)
    q_id, k_id = jnp.zeros_like(q_pos), jnp.zeros_like(k_pos)
    end = jnp.int32(0)
    for j in range(lengths.shape[1]):
        end = end + lengths[lane, j]
        q_id = q_id + (end <= q_pos).astype(jnp.int32)
        k_id = k_id + (end <= k_pos).astype(jnp.int32)
    return (q_id == k_id) & (k_pos <= q_pos) & (q_pos - k_pos < window) & (k_pos >= 0)


def soft_of(query, keys, allowed):
    scores = jnp.where(allowed, dot_nt(query, keys) * SCALE, -1e30)
    grown = jnp.exp(scores - jnp.max(scores, axis=-1, keepdims=True))
    return grown * (1.0 / jnp.sum(grown, axis=-1, keepdims=True))


def attention_kernel(
    hops, chunk, place, lengths, query, kv_local, earlier, tokens, w_out, gains,
    mixed, branch, middle, ffn_in, keys,
):
    lanes = lengths.shape[0]
    rows = query.shape[0] // lanes
    for lane in range(lanes):
        span = slice(lane * rows, (lane + 1) * rows)
        keys_of(lane, rows, hops, chunk, earlier, kv_local, keys)
        allowed = allowed_of(place, lengths, lane, rows, hops, W)
        for h in range(HQ):
            cols = slice(h * HD, (h + 1) * HD)
            soft = soft_of(query[span, cols], keys[:, :HD], allowed)
            mixed[span, cols] = dot(soft.astype(BF), keys[:, HD:]).astype(BF)
        out = dot(mixed[span, :], w_out[...])
        branch[span, :] = out
        mid = tokens[span, :].astype(F32) + rms_forward(out, gains[1:2, :])
        middle[span, :] = mid
        ffn_in[span, :] = rms_forward(mid, gains[2:3, :]).astype(BF)


def attention(hops, chunk, place, lengths, query, kv_local, earlier, tokens, w_out, gains):
    total, width = tokens.shape
    lanes = lengths.shape[0]
    return pl.pallas_call(
        functools.partial(attention_kernel, hops, chunk),
        out_shape=[
            jax.ShapeDtypeStruct(query.shape, BF),
            jax.ShapeDtypeStruct((total, width), F32),
            jax.ShapeDtypeStruct((total, width), F32),
            jax.ShapeDtypeStruct((total, width), BF),
        ],
        in_specs=[SMEM, SMEM] + [VMEM] * 6,
        out_specs=[VMEM] * 4,
        scratch_shapes=[pltpu.VMEM(((hops + 1) * (total // lanes), 2 * HD), BF)],
        compiler_params=PARAMS,
        cost_estimate=COST,
    )(place, lengths, query, kv_local, earlier, tokens, w_out, gains)


def attention_back_kernel(
    hops, chunk, cores, core, place, lengths, query, kv_local, earlier, upstream, w_out, gains,
    head_gains, branch, middle, keep, got, query_proj, cosine, sine, late, grad_middle, grad_branch, grad_query, grad_kv, grad_earlier, norm_terms, head_terms,
    keys, d_mixed, raws, softs, queries, mixes,
):
    lanes = lengths.shape[0]
    rows = query.shape[0] // lanes
    width = upstream.shape[1]
    norm_terms[...] = jnp.zeros_like(norm_terms)
    head_terms[...] = jnp.zeros_like(head_terms)
    for lane in range(lanes):
        span = slice(lane * rows, (lane + 1) * rows)
        d_ffn_in = keep[span, :] + got[span, :].astype(F32)
        d_mid, ffn_terms = rms_backward(middle[span, :], gains[2:3, :], d_ffn_in)
        d_mid = d_mid + upstream[span, :].astype(F32)
        grad_middle[span, :] = d_mid
        d_branch, mid_terms = rms_backward(branch[span, :], gains[1:2, :], d_mid)
        norm_terms[0:1, :] += jnp.sum(mid_terms, axis=0, keepdims=True)
        norm_terms[1:2, :] += jnp.sum(ffn_terms, axis=0, keepdims=True)
        low = d_branch.astype(BF)
        grad_branch[span, :] = low
        if cores == 2:
            size = late.shape[1] - HQ * HD
            window = window_of(core[0] ^ 1, width // 2, size)
            late[span, HQ * HD :] = grad_branch[span, window]
        d_mixed[...] = dot_nt(low, w_out[...]).astype(BF)
        keys_of(lane, rows, hops, chunk, earlier, kv_local, keys)
        allowed = allowed_of(place, lengths, lane, rows, hops, W)
        cos, sin = cosine[span, :], sine[span, :]
        for h in range(HQ):
            cols = slice(h * HD, (h + 1) * HD)
            stack = slice(h * rows, (h + 1) * rows)
            soft = soft_of(query[span, cols], keys[:, :HD], allowed)
            d_soft = dot_nt(d_mixed[:, cols], keys[:, HD:])
            inner = jnp.sum(soft * d_soft, axis=-1, keepdims=True)
            raw = (soft * (d_soft - inner) * SCALE).astype(BF)
            raws[stack, :] = raw
            softs[stack, :] = soft.astype(BF)
            queries[stack, :] = query[span, cols]
            mixes[stack, :] = d_mixed[:, cols]
            normed = rotate(dot(raw, keys[:, :HD]), cos, -sin)
            d_query, terms = rms_backward(query_proj[span, cols], head_gains[0:1, :], normed)
            grad_query[span, cols] = d_query.astype(BF)
            if cores == 2:
                late[span, cols] = d_query.astype(BF)
            head_terms[0:1, :] += jnp.sum(terms, axis=0, keepdims=True)
        for part, (left, right) in enumerate(((raws, queries), (softs, mixes))):
            cols = slice(part * HD, (part + 1) * HD)
            out = dot_tn(left[...], right[...])
            for d in range(1, hops + 1):
                for start, size, target in pieces_of(lane, rows, hops, chunk, d):
                    source = (hops - d) * rows + start
                    grad_earlier[target : target + size, cols] = out[
                        source : source + size
                    ].astype(BF)
            grad_kv[span, cols] = out[hops * rows :]


def attention_back(
    hops, chunk, cores, core, place, lengths, query, kv_local, earlier, upstream, w_out, gains, head_gains,
    branch, middle, keep, got, query_proj, cosine, sine,
):
    total, width = upstream.shape
    lanes = lengths.shape[0]
    rows = total // lanes
    span = (hops + 1) * rows
    return pl.pallas_call(
        functools.partial(attention_back_kernel, hops, chunk, cores),
        out_shape=[
            jax.ShapeDtypeStruct((total, HQ * HD + window_size(width, cores)), BF),
            jax.ShapeDtypeStruct((total, width), F32),
            jax.ShapeDtypeStruct((total, width), BF),
            jax.ShapeDtypeStruct(query.shape, BF),
            jax.ShapeDtypeStruct(kv_local.shape, F32),
            jax.ShapeDtypeStruct(earlier.shape, BF),
            jax.ShapeDtypeStruct((8, width), F32),
            jax.ShapeDtypeStruct((8, HD), F32),
        ],
        in_specs=[SMEM] * 3 + [VMEM] * 14,
        out_specs=[VMEM] * 8,
        scratch_shapes=[
            pltpu.VMEM((span, 2 * HD), BF),
            pltpu.VMEM((rows, HQ * HD), BF),
            pltpu.VMEM((HQ * rows, span), BF),
            pltpu.VMEM((HQ * rows, span), BF),
            pltpu.VMEM((HQ * rows, HD), BF),
            pltpu.VMEM((HQ * rows, HD), BF),
        ],
        compiler_params=PARAMS,
        cost_estimate=COST,
    )(
        core, place, lengths, query, kv_local, earlier, upstream, w_out, gains, head_gains,
        branch, middle, keep, got, query_proj, cosine, sine,
    )


def shards(
    tokens,
    cotangent,
    lengths,
    deal_order,
    w_query,
    w_key,
    w_value,
    w_out,
    w_gate,
    w_up,
    w_down,
    norm_gains,
    head_gains,
):
    lanes, rows, width = tokens.shape[1:]
    total = lanes * rows
    seq_count = lax.axis_size("seq")
    cores = lax.axis_size("fsdp")
    own = lax.axis_index("seq")
    core = lax.axis_index("fsdp")
    window = W
    hops = (window - 1 + rows - 1) // rows
    chunk = total // seq_count

    deal = deal_order[0]
    places = jnp.arange(seq_count, dtype=jnp.int32)
    back = jnp.sum(jnp.where(deal[None, :] == places[:, None], places[None, :], 0), axis=1)
    place = deal[own]
    steps = jnp.arange(1, hops + 1, dtype=jnp.int32)
    wanted = deal[:, None] - steps[None, :]
    fetch_table = back[jnp.maximum(wanted, 0)].reshape(-1)
    readers = deal[:, None] + steps[None, :]
    reader_ok = (readers < seq_count).astype(jnp.int32).reshape(-1)
    reader_table = (
        back[jnp.minimum(readers, seq_count - 1)] * hops + (steps[None, :] - 1)
    ).reshape(-1)

    token_rows = tokens.reshape(total, width)
    upstream_rows = cotangent.reshape(total, width)
    q_width = HQ * HD
    narrow = width // cores
    core_ref, own_ref = core.reshape(1), own.reshape(1)

    def core_blocks(block):
        blocks = [block]
        for mask in masks(cores):
            together = jnp.concatenate(blocks, axis=0) if len(blocks) > 1 else blocks[0]
            got = swap(together, "fsdp", mask)
            size = block.shape[0]
            blocks = blocks + [got[j * size : (j + 1) * size] for j in range(len(blocks))]
        return blocks

    def core_sum(keep, send):
        steps = masks(cores)[::-1]
        for mask in steps:
            out = keep + swap(send, "fsdp", mask).astype(F32)
            half = out.shape[0] // 2
            keep, send = out[:half], out[half:].astype(BF)
        return out

    kv_peers = core_blocks(jnp.concatenate([w_key, w_value], axis=1))
    angles = angles_of(own_ref, deal, lengths[0], rows)
    cosine, sine = jnp.cos(angles), jnp.sin(angles)
    attn_in, key_proj, kv_local = key_value(
        core_ref, token_rows, kv_peers, norm_gains, head_gains, cosine, sine
    )

    spread = lax.all_to_all(
        kv_local.reshape(seq_count, chunk, 2 * HD), "seq", 0, 0, tiled=True
    )
    picked = pick(fetch_table, spread).reshape(seq_count, hops * chunk, 2 * HD)
    arrived = lax.all_to_all(picked, "seq", 0, 0, tiled=True)
    run = chunk
    if chunk % 16:
        run = total
        arrived = arrived.reshape(seq_count, hops, chunk, 2 * HD).transpose(1, 0, 2, 3)
    earlier = arrived.reshape(hops * total, 2 * HD)

    w_query, w_out = lax.optimization_barrier((w_query, w_out, kv_local))[:2]
    query_peers = core_blocks(w_query)
    size = -(-narrow // 128) * 128
    peers_out = gather_cores(jnp.pad(w_out, ((0, 0), (0, size - narrow))))
    peers_out = flip(peers_out.reshape(cores, q_width, size), core)
    w_out_full = jnp.concatenate([peers_out[j, :, :narrow] for j in range(cores)], axis=1)
    query_proj, query_rot = queries_of(
        core_ref, attn_in, query_peers, head_gains, cosine, sine
    )

    size = window_size(width, cores)

    def peer_window(values):
        start = (core ^ 1) * narrow // 128 * 128
        return lax.dynamic_slice_in_dim(values, start, size, 1)

    hidden_cols = w_gate.shape[1]
    share = -(-hidden_cols // 256) * 128
    overlap = 2 * share - hidden_cols
    part = ((own & SPLIT_BIT) != 0).astype(jnp.int32)
    part_ref = part.reshape(1)
    if (hidden_cols - share) % 128:
        begin = part * (hidden_cols - share)
        w_gate = lax.dynamic_slice_in_dim(w_gate, begin, share, 1)
        w_up = lax.dynamic_slice_in_dim(w_up, begin, share, 1)
        w_down = lax.dynamic_slice_in_dim(w_down, begin, share, 0)

    earlier = after(earlier, query_rot, w_out_full)
    place_ref, lengths_ref = place.reshape(1), lengths[0]
    mixed_low, branch, middle, ffn_in = attention(
        hops, run, place_ref, lengths_ref, query_rot, kv_local, earlier, token_rows, w_out_full, norm_gains
    )

    if cores == 2:
        mixed_peer = swap(mixed_low, "fsdp", 1)
        attn_peer = swap(peer_window(attn_in), "fsdp", 1)
        early = (mixed_peer, attn_peer)
    else:
        early = ()

    def sum_group(near_part, far_part):
        got = swap(core_sum(*far_part).astype(BF), "seq", SPLIT_BIT)
        return core_sum(*near_part), got

    far_in = swap(ffn_in, "seq", SPLIT_BIT)
    near_all = core_blocks(ffn_in)
    near = ffn_forward(part_ref, near_all, w_gate, w_up, w_down, share, overlap)
    far_all = core_blocks(after(far_in, near[0], *early))
    far = ffn_forward(part_ref, far_all, w_gate, w_up, w_down, share, overlap)
    keep, got = sum_group(near[3:], far[3:])
    ffn_out = keep + got.astype(F32)
    result = middle + rms_forward(ffn_out, norm_gains[3])

    grad_ffn_out, top_terms = rms_backward(ffn_out, norm_gains[3], upstream_rows.astype(F32))
    top_terms = jnp.sum(top_terms, axis=0, keepdims=True)
    grad_low = grad_ffn_out.astype(BF)
    far_grad = swap(grad_low, "seq", SPLIT_BIT)
    near_grads = core_blocks(grad_low)
    near_back = ffn_backward(part_ref, near_grads, near[1], near[2], w_gate, w_up, w_down)
    far_grads = core_blocks(after(far_grad, near_back[0]))
    others = [m for m in masks(seq_count) if m != SPLIT_BIT]
    swapped, beyond = [others[1], others[0]] + others[2:], others[2:]

    def terms_of(left, right, *pieces):
        pieces = [(order + [SPLIT_BIT], size, quad) for order, size, quad in pieces]
        return weight_terms(own, seq_count, pieces, left, *right)

    tile, count = tiles(share)
    minor = max(1, count * 2 // 7) * tile
    outward_first = beyond[:1] + others[:2] + beyond[1:]

    down_terms = terms_of(
        near_grads + far_grads,
        (near[0], far[0]),
        (beyond, share - minor, True),
        (outward_first, minor, False),
    )
    down_b = Chain(*down_terms[1:], outward_first)
    down_quad = lax.all_to_all(
        down_terms[0], "seq", 0, 0, tiled=True, axis_index_groups=quads(seq_count)
    )
    far_grads[0] = after(far_grads[0], *down_terms)
    far_back = ffn_backward(part_ref, far_grads, far[1], far[2], w_gate, w_up, w_down)
    far_sum = core_sum(*far_back[2:]).astype(BF)
    got = swap(far_sum, "seq", SPLIT_BIT)
    keep = core_sum(*near_back[2:])

    gate_terms = terms_of(
        near_all + far_all, (near_back[0], after(far_back[0], far_sum)), (swapped, share, False)
    )
    up_terms = terms_of(
        near_all + far_all, (near_back[1], after(far_back[1], *gate_terms)), (others, share, False)
    )
    gate_c = Chain(*gate_terms, swapped)
    up_c = Chain(*up_terms, others)
    turns = Turns(up_terms[0])

    down_b.step(turns)
    (
        late, grad_middle, grad_branch_low, grad_query_low, grad_kv, grad_earlier, norm_terms,
        head_terms,
    ) = attention_back(
        hops, run, cores, core_ref, place_ref, lengths_ref, query_rot, kv_local, earlier, upstream_rows, w_out_full,
        norm_gains, head_gains, branch, middle, keep, turns.wait(got), query_proj, cosine, sine,
    )

    outward = grad_earlier
    if chunk % 16:
        outward = outward.reshape(hops, seq_count, chunk, 2 * HD).transpose(1, 0, 2, 3)
    outward = outward.reshape(seq_count, hops * chunk, 2 * HD)
    collected = lax.all_to_all(outward, "seq", 0, 0, tiled=True)

    turns.end(outward)
    down_first, down_rest = quad_sum(turns.wait(down_quad))
    turns.end(down_first)
    down_a = Chain(down_first, down_rest, beyond)
    every = swapped + [SPLIT_BIT]
    padded = width // seq_count
    if cores == 2:
        late = swap(late, "fsdp", 1)
        attention_terms = outer_pair(
            own_ref, core_ref, seq_count, every, padded, mixed_low, mixed_peer, grad_branch_low,
            grad_query_low, turns.wait(late), attn_in, attn_peer,
        )
    else:
        outer_keep, outer_send = outer_begin(
            core_ref, cores, mixed_low, grad_branch_low, turns.wait(grad_query_low), attn_in
        )
        outer_keep = core_sum(outer_keep, outer_send)
        outer_got = jnp.zeros(outer_keep.shape, BF)
        attention_terms = outer_end(own_ref, seq_count, every, outer_keep, outer_got, padded)
    turns.end(attention_terms[0])
    outer_c = Chain(*attention_terms, swapped)
    gate_c.step(turns)
    up_c.step(turns)
    down_b.step(turns)
    summed = pick_sum(
        hops,
        reader_table,
        reader_ok,
        turns.wait(collected).reshape(seq_count * hops, chunk, 2 * HD),
    )
    turns.end(summed)
    returned = lax.all_to_all(summed, "seq", 0, 0, tiled=True)
    while down_a.order:
        down_a.step(turns)
    gate_c.step(turns)
    up_c.step(turns)
    outer_c.step(turns)
    while down_b.order:
        down_b.step(turns)
    returned = turns.wait(returned)

    grad_inputs, kv_keep, kv_send, gain_terms = last(
        core_ref, query_peers, kv_peers, token_rows, attn_in, grad_middle, grad_query_low, grad_kv,
        returned.reshape(total, 2 * HD), key_proj, cosine, sine, norm_gains, head_gains, norm_terms,
        head_terms, top_terms,
    )
    kv_rows = HD // seq_count
    tail_order = beyond + [SPLIT_BIT]
    size = kv_keep.shape[1]
    starts = gain_starts(width, size)
    extra = len(starts) * GAIN_ROWS
    if cores == 2:
        kv_got, gains_got = swap(kv_send, "fsdp", 1), swap(gain_terms, "fsdp", 1)
    else:
        kv_keep = core_sum(kv_keep, kv_send)
        kv_got = jnp.zeros(kv_keep.shape, BF)
        for mask in masks(cores)[1:]:
            gain_terms = gain_terms + swap(gain_terms, "fsdp", mask)
        gains_got = swap(gain_terms, "fsdp", 1)
    if kv_rows % 16:
        gains = (gain_terms + gains_got).astype(BF)
        owners = jnp.stack([owner(own) for owner in places_of(tail_order, True)])
        tail = (kv_keep + kv_got.astype(F32)).astype(BF).reshape(2, seq_count, kv_rows, size)
        tail = jnp.take(tail, owners, axis=1, mode="clip").transpose(1, 0, 2, 3)
        tail = tail.reshape(QUAD, -1, size)
        gains = jnp.concatenate([gains[:, start : start + size] for start in starts], axis=0)
        gains = jnp.broadcast_to(gains, (QUAD,) + gains.shape)
        tail = jnp.concatenate([tail, gains], axis=1).reshape(-1, size)
    else:
        tail = tail_begin(own_ref, tail_order, seq_count, kv_keep, kv_got, gain_terms, gains_got)
    ended = lax.all_to_all(
        tail, "seq", 0, 0, tiled=True, axis_index_groups=quads(seq_count)
    )
    turns.end(tail)

    def exchanged(*chains):
        mine = jnp.concatenate([chain.total[1] for chain in chains], axis=1)
        sent = jnp.concatenate([chain.total[0].astype(BF) for chain in chains], axis=1)
        return mine, swap(sent, "seq", SPLIT_BIT)

    down_pair = exchanged(down_a, down_b)
    while gate_c.order:
        gate_c.step(turns)
    outer_c.step(turns)
    ended = turns.wait(ended).reshape(QUAD, -1, size)
    parts = [ended[q] for q in range(QUAD)]
    for mask in tail_order:
        sent, kept = tail_step(parts, extra, False)
        turns.end(sent)
        got = swap(sent, "seq", mask)
        if mask == tail_order[0]:
            while up_c.order:
                up_c.step(turns)
            gate_pair = exchanged(gate_c, up_c)
        if mask == tail_order[-1]:
            while outer_c.order:
                outer_c.step(turns)
            outer_mine, outer_got = exchanged(outer_c)
            pair_got = turns.wait(gate_pair[1])
            turns.end(pair_got)
        parts = [kept, turns.wait(got)]

    def own_columns(values):
        return lax.dynamic_slice_in_dim(values, core * narrow % 128, narrow, 1)

    if kv_rows % 16 or cores != 2:
        (ended,) = tail_step(parts, extra, True)
        key_grad = own_columns(ended[:kv_rows]).T
        value_grad = own_columns(ended[kv_rows : 2 * kv_rows]).T
        windows = ended[-extra:].reshape(len(starts), GAIN_ROWS, size)
        gains = jnp.concatenate(
            [windows[k][:, k * size - start :] for k, start in enumerate(starts)], axis=1
        )
        norm_total, head_total = gains[:4], gains[4:6, :HD]
    else:
        key_grad, value_grad, norm_total, head_total = tail_end(core_ref, width, kv_rows, parts)
        key_grad, value_grad = key_grad.T, value_grad.T

    mine, got = down_pair
    mine = jnp.concatenate([mine, gate_pair[0]], axis=1)
    got = jnp.concatenate([turns.wait(got), pair_got], axis=1).astype(F32)
    lower, upper = jnp.where(part == 0, mine, got), jnp.where(part == 0, got, mine)
    down_grad, gate_grad, up_grad = (
        jnp.concatenate(
            [
                lower[:, k * share : (k + 1) * share],
                upper[:, k * share + overlap : (k + 1) * share],
            ],
            axis=1,
        )
        for k in range(3)
    )
    down_grad = down_grad.T
    attention_grad = outer_mine + turns.wait(outer_got).astype(F32)
    query_rows = q_width // seq_count
    size = attention_grad.shape[1] // 2
    out_grad = own_columns(attention_grad[:query_rows, :size])
    query_grad = own_columns(attention_grad[:query_rows, size:]).T


    return (
        result.reshape(1, lanes, rows, width),
        grad_inputs.reshape(1, lanes, rows, width),
        query_grad,
        key_grad,
        value_grad,
        out_grad,
        gate_grad,
        up_grad,
        down_grad,
        norm_total,
        head_total,
    )


def solution(mesh):
    in_specs = (
        P("fsdp", None, "seq", None),
        P("fsdp", None, "seq", None),
        P("fsdp", None, None),
        P("fsdp", None),
        P("fsdp", None),
        P("fsdp", None),
        P("fsdp", None),
        P(None, "fsdp"),
        P(None, "fsdp"),
        P(None, "fsdp"),
        P("fsdp", None),
        P(),
        P(),
    )
    out_specs = (
        P("fsdp", None, "seq", None),
        P("fsdp", None, "seq", None),
        P("fsdp", "seq"),
        P("fsdp", "seq"),
        P("fsdp", "seq"),
        P("seq", "fsdp"),
        P("seq", "fsdp"),
        P("seq", "fsdp"),
        P("fsdp", "seq"),
        P(),
        P(),
    )
    return jax.shard_map(shards, mesh=mesh, in_specs=in_specs, out_specs=out_specs, check_vma=False)
```
